32 devices in a mesh: dp: 4 (over y, x), mp: 8 (over z, core).
Axes of the slice: x: 2, y: 2, z: 4, core: 2. Of those that a mesh axis runs over, the one named last changes fastest.
Arguments:
- inputs: bfloat16 [2048, 4096], P('dp'), may hold values from -6 to 6
- out_grads: bfloat16 [2048, 4096], P('dp'), may hold values from -0.3984375 to 0.3984375
- w_gate: bfloat16 [4096, 11008], P(None, 'mp'), may hold values from -0.09375 to 0.09375
- w_up: bfloat16 [4096, 11008], P(None, 'mp'), may hold values from -0.09375 to 0.09375
- w_down: bfloat16 [11008, 4096], P('mp'), may hold values from -0.0546875 to 0.0546875
- err_down: bfloat16 [4, 11008, 4096], P('dp', 'mp'), may hold values from -3 to 3
- mom_down: float32 [11008, 4096], P('mp', 'dp'), may hold values from -0.3 to 0.3
- q_down: float32 [4096, 8], replicated, may hold values from -5 to 5
Outputs:
- in_grads: bfloat16 [2048, 4096], P('dp', 'mp')
- new_down: bfloat16 [11008, 4096], P('mp')
- next_err_down: bfloat16 [4, 11008, 4096], P('dp', 'mp')
- next_mom_down: float32 [11008, 4096], P('mp', 'dp')
The draws below stay inside these ranges and needn't reach their ends.
All inputs are finite; a program needn't handle non-finite values.
Results may differ from the reference program's by a relative error of at most 0.005.
Values may be sent and summed in bfloat16 or wider, within the bound.
No kernel may reach another device: no remote copies, remote signals or barrier semaphores. Data moves between devices by JAX's collectives and lax.ppermute only.
A program may use at most 192 MiB of HBM per device.

```python
import jax
import jax.numpy as jnp
from jax import lax

D = 4096
FF = 11008
TOK = 512
R = 8
TOKENS = 2048
N_DP = 4


def shard_levels(own_key, extent, pieces, low, high):
    def one(axis_at, blocks):
        draws = jax.random.uniform(jax.random.fold_in(jax.random.fold_in(own_key, 6), axis_at), (blocks,), jnp.float32, low / len(pieces), high / len(pieces))
        return jnp.repeat(jnp.exp(draws), extent[axis_at] // blocks).reshape((-1,) + (1,) * (len(extent) - axis_at - 1))

    factor_of = one(*pieces[0])
    for cut in pieces[1:]:
        factor_of = factor_of * one(*cut)
    return factor_of


def gaussian(stream_key, dims, spread, most, pieces=(), dtype=jnp.bfloat16):
    array = jax.random.normal(stream_key, dims, jnp.float32) * spread
    if len(pieces) > 0:
        array = shard_levels(stream_key, dims, pieces, -0.22, 0.18) * array
    return jnp.clip(array, min=-most, max=most).astype(dtype)


def setup_inputs(seed: int = 0) -> dict:
    splits = jax.random.split(jax.random.key(seed), 9)
    return {
        "inputs": gaussian(splits[0], (TOKENS, D), 1.0, 6.0, ((0, 4),)),
        "out_grads": gaussian(splits[1], (TOKENS, D), 0.0625, 0.3984375, ((0, 4),)),
        "w_gate": gaussian(splits[2], (D, FF), D ** -0.5, 0.09375, ((1, 8),)),
        "w_up": gaussian(splits[3], (D, FF), D ** -0.5, 0.09375, ((1, 8),)),
        "w_down": gaussian(splits[4], (FF, D), FF ** -0.5, 0.0546875, ((0, 8),)),
        "err_down": gaussian(splits[5], (N_DP, FF, D), 0.5, 3.0, ((0, 4), (1, 8))),
        "mom_down": gaussian(splits[6], (FF, D), 0.05, 0.3, ((0, 8), (1, 4)), jnp.float32),
        "q_down": gaussian(splits[7], (D, R), 1.0, 5.0, (), jnp.float32),
    }


HIGH = lax.Precision.HIGHEST

def orthonormal(panel):
    finished = []
    for col in range(R):
        vector = panel[:, col]
        if col > 0:
            basis = jnp.stack(finished, 1)
            coeffs = jnp.dot(basis.T, vector, precision=HIGH)
            vector = vector - jnp.dot(basis, coeffs, precision=HIGH)
        vector = vector * lax.rsqrt(jnp.sum(vector * vector) + 1e-06)
        finished.append(vector)
    return jnp.stack(finished, 1)

def compress(corrected, right):
    left = sum((jnp.dot(m, right, precision=HIGH) for m in corrected)) / N_DP
    left = orthonormal(left)
    right_new = sum((jnp.dot(m.T, left, precision=HIGH) for m in corrected)) / N_DP
    return jnp.dot(left, right_new.T, precision=HIGH)

def reference(inputs, out_grads, w_gate, w_up, w_down, err_down, mom_down, q_down):
    in_rows = []
    m_down = []
    for rep in range(N_DP):
        x_rows = inputs[rep * TOK:(rep + 1) * TOK]
        dy_rows = out_grads[rep * TOK:(rep + 1) * TOK]
        gate = jnp.dot(x_rows, w_gate, preferred_element_type=jnp.float32)
        up_val = jnp.dot(x_rows, w_up, preferred_element_type=jnp.float32)
        sig = jax.nn.sigmoid(gate)
        hidden = (gate * sig * up_val).astype(jnp.bfloat16)
        d_hidden = jnp.dot(dy_rows, w_down.T, preferred_element_type=jnp.float32)
        d_gate = (d_hidden * up_val * sig * (1.0 + gate * (1.0 - sig))).astype(jnp.bfloat16)
        d_up = (d_hidden * gate * sig).astype(jnp.bfloat16)
        part = jnp.dot(d_gate, w_gate.T, preferred_element_type=jnp.float32) + jnp.dot(d_up, w_up.T, preferred_element_type=jnp.float32)
        in_rows.append(part.astype(jnp.bfloat16))
        m_down.append(jnp.dot(hidden.T, dy_rows, preferred_element_type=jnp.float32) + err_down[rep].astype(jnp.float32))
    approx = compress(m_down, q_down)
    errors = jnp.stack([(m - approx).astype(jnp.bfloat16) for m in m_down], 0)
    mom_next = 0.9 * mom_down + approx
    weight_next = (w_down.astype(jnp.float32) - 0.1 * mom_next).astype(jnp.bfloat16)
    return (jnp.concatenate(in_rows, 0), weight_next, errors, mom_next)
```

```python
import functools

import jax
import jax.numpy as jnp
from jax import lax
from jax.experimental import pallas as pl
from jax.experimental.pallas import tpu as pltpu
from jax.sharding import PartitionSpec as P

R = 8
SPLIT = 4 * R
EPS = 1e-06
F32 = jnp.float32
BF16 = jnp.bfloat16
HIGH = lax.Precision.HIGHEST
VMEM = 48 * 2**20
ONCE = pl.Buffered(1)


def params():
    return pltpu.CompilerParams(vmem_limit_bytes=VMEM)


def cost(flops, nbytes):
    return pl.CostEstimate(flops=int(flops), bytes_accessed=int(nbytes), transcendentals=0)


def dot(left, right):
    return jnp.dot(left, right, preferred_element_type=F32)


def dot_nt(left, right):
    return lax.dot_general(left, right, (((1,), (1,)), ((), ())), preferred_element_type=F32)


def terms(rows):
    hi = rows.astype(BF16).astype(F32)
    rest = rows - hi
    mid = rest.astype(BF16).astype(F32)
    return hi, mid, rest - mid


def spread(rows):
    hi, mid, low = terms(rows)
    return jnp.concatenate([hi, mid, low, jnp.zeros_like(hi)], axis=0).astype(BF16)


def gather_terms(rows):
    return rows[:R] + rows[R : 2 * R] + rows[2 * R : 3 * R]


def whole(shape):
    return pl.BlockSpec(shape, lambda *_: (0,) * len(shape), pipeline_mode=ONCE)


def hidden_kernel(x_ref, dy_ref, wg_ref, wu_ref, wd_ref, hid_ref, dg_ref, du_ref):
    gate = dot_nt(x_ref[...], wg_ref[...])
    up = dot_nt(x_ref[...], wu_ref[...])
    dh = dot_nt(dy_ref[...], wd_ref[...])
    sig = jax.nn.sigmoid(gate)
    silu = gate * sig
    hid_ref[...] = (silu * up).T.astype(BF16)
    dg_ref[...] = (dh * up * sig * (1.0 + gate * (1.0 - sig))).astype(BF16)
    du_ref[...] = (dh * silu).astype(BF16)


def hidden_call(x, dy, wg, wu, wd):
    tok, depth = x.shape
    units = wg.shape[0]
    tile = min(256, units)
    return pl.pallas_call(
        hidden_kernel,
        grid=(pl.cdiv(units, tile),),
        in_specs=[
            whole((tok, depth)),
            whole((tok, depth)),
            pl.BlockSpec((tile, depth), lambda f: (f, 0)),
            pl.BlockSpec((tile, depth), lambda f: (f, 0)),
            pl.BlockSpec((tile, depth), lambda f: (f, 0)),
        ],
        out_specs=[
            pl.BlockSpec((tile, tok), lambda f: (f, 0)),
            pl.BlockSpec((tok, tile), lambda f: (0, f)),
            pl.BlockSpec((tok, tile), lambda f: (0, f)),
        ],
        out_shape=[
            jax.ShapeDtypeStruct((units, tok), BF16),
            jax.ShapeDtypeStruct((tok, units), BF16),
            jax.ShapeDtypeStruct((tok, units), BF16),
        ],
        compiler_params=params(),
        cost_estimate=cost(6 * tok * depth * units, 6 * depth * units + 4 * tok * depth),
        name="hidden",
    )(x, dy, wg, wu, wd)


def left_kernel(q_ref, err_ref, dy_ref, hid_ref, out_ref, err_acc, dy_acc):
    step = pl.program_id(0)

    @pl.when(step == 0)
    def _():
        err_acc[...] = jnp.zeros_like(err_acc)
        dy_acc[...] = jnp.zeros_like(dy_acc)

    q = spread(q_ref[...])
    err_acc[...] += dot_nt(q, err_ref[0])
    dy_acc[...] += dot_nt(q, dy_ref[...])

    @pl.when(step == pl.num_programs(0) - 1)
    def _():
        mixed = spread(gather_terms(dy_acc[...]))
        out_ref[...] = gather_terms(err_acc[...]) + gather_terms(dot_nt(mixed, hid_ref[...]))


def left_call(q_t, err, dy, hid):
    units, tok = hid.shape
    depth = dy.shape[1]
    tile = min(512, depth)
    return pl.pallas_call(
        left_kernel,
        grid=(depth // tile,),
        in_specs=[
            pl.BlockSpec((R, tile), lambda d: (0, d)),
            pl.BlockSpec((1, units, tile), lambda d: (0, 0, d)),
            pl.BlockSpec((tok, tile), lambda d: (0, d)),
            whole((units, tok)),
        ],
        out_specs=whole((R, units)),
        out_shape=jax.ShapeDtypeStruct((R, units), F32),
        scratch_shapes=[pltpu.VMEM((SPLIT, units), F32), pltpu.VMEM((SPLIT, tok), F32)],
        compiler_params=params(),
        cost_estimate=cost(2 * 256 * units * depth, 2 * units * depth + 2 * tok * depth),
        name="left",
    )(q_t, err, dy, hid)


def right_kernel(left_ref, hid_ref, err_ref, dy_ref, out_ref, left_terms, mixed_terms):
    step = pl.program_id(0)
    depth = dy_ref.shape[1]

    @pl.when(step == 0)
    def _():
        left = left_ref[...]
        left_terms[...] = spread(left)
        mixed_terms[...] = spread(gather_terms(dot(left_terms[...], hid_ref[...])))
        gram = lax.dot_general(
            left, left, (((1,), (1,)), ((), ())), precision=HIGH, preferred_element_type=F32
        )
        out_ref[:, out_ref.shape[1] - 128 :] = jnp.concatenate(
            [gram, jnp.zeros((R, 128 - R), F32)], axis=1
        )

    part = dot(left_terms[...], err_ref[0]) + dot(mixed_terms[...], dy_ref[...])
    out_ref[:, pl.ds(pl.multiple_of(step * depth, depth), depth)] = gather_terms(part)


def right_call(left, hid, err, dy):
    units, tok = hid.shape
    depth = dy.shape[1]
    tile = min(512, depth)
    return pl.pallas_call(
        right_kernel,
        grid=(depth // tile,),
        in_specs=[
            whole((R, units)),
            whole((units, tok)),
            pl.BlockSpec((1, units, tile), lambda d: (0, 0, d)),
            pl.BlockSpec((tok, tile), lambda d: (0, d)),
        ],
        out_specs=whole((R, depth + 128)),
        out_shape=jax.ShapeDtypeStruct((R, depth + 128), F32),
        scratch_shapes=[pltpu.VMEM((SPLIT, units), BF16), pltpu.VMEM((SPLIT, tok), BF16)],
        compiler_params=params(),
        cost_estimate=cost(2 * 256 * units * depth, 2 * units * depth + 2 * tok * depth),
        name="right",
    )(left, hid, err, dy)


def factors_kernel(replicas, sum_ref, left_ref, l_ref, r_ref):
    depth = r_ref.shape[1]
    gram = sum_ref[:, depth : depth + R] / replicas
    row = lax.broadcasted_iota(jnp.int32, (R, R), 0)
    col = lax.broadcasted_iota(jnp.int32, (R, R), 1)
    eye = (row == col).astype(F32)
    basis = jnp.zeros((R, R), F32)
    for k in range(R):
        unit = eye[k : k + 1]
        coeffs = jnp.sum(basis * gram[k : k + 1], axis=1, keepdims=True)
        rest = unit - jnp.sum(coeffs * basis, axis=0, keepdims=True)
        rest_col = jnp.sum(eye * rest, axis=1, keepdims=True)
        image = jnp.sum(rest_col * gram, axis=0, keepdims=True)
        square = jnp.sum(image * rest, axis=1, keepdims=True)
        basis = jnp.where(row == k, rest * lax.rsqrt(jnp.maximum(square, 0.0) + EPS), basis)
    left = jnp.dot(basis, left_ref[...], precision=HIGH, preferred_element_type=F32)
    right = jnp.dot(basis, sum_ref[:, :depth], precision=HIGH, preferred_element_type=F32)
    hi, mid, _ = terms(left)
    zero = jnp.zeros_like(hi)
    l_ref[...] = jnp.concatenate([hi, hi, mid, zero], axis=0).T.astype(BF16)
    hi, mid, _ = terms(right / replicas)
    zero = jnp.zeros_like(hi)
    r_ref[...] = jnp.concatenate([hi, mid, hi, zero], axis=0).astype(BF16)


def factors_call(total, left, replicas):
    units = left.shape[1]
    depth = total.shape[1] - 128
    return pl.pallas_call(
        functools.partial(factors_kernel, replicas),
        out_shape=[
            jax.ShapeDtypeStruct((units, SPLIT), BF16),
            jax.ShapeDtypeStruct((SPLIT, depth), BF16),
        ],
        compiler_params=params(),
        cost_estimate=cost(2 * 256 * 6 * R * (units + depth), 4 * R * (units + depth)),
        name="factors",
    )(total, left)


def blocks_kernel(add, where_ref, dg_ref, du_ref, wg_ref, wu_ref, *refs):
    step = pl.program_id(0)
    if add:
        added, outs = refs[: len(refs) // 2], refs[len(refs) // 2 :]
    else:
        added, outs = (None,) * len(refs), refs
    part = dot(dg_ref[...], wg_ref[...]) + dot(du_ref[...], wu_ref[...])
    for slot, (more, out) in enumerate(zip(added, outs)):

        @pl.when(step == slot)
        def _(more=more, out=out):
            out[...] = (part if more is None else part + more[...].astype(F32)).astype(BF16)


def blocks_call(pos, parity, dg, du, wg, wu, count, added=()):
    tok, units = dg.shape
    depth = wg.shape[1]
    width = depth // (2 * count)
    where = jnp.stack([pos // 2, parity]).astype(jnp.int32)
    block = pl.BlockSpec((units, width), lambda s, at: (0, 2 * (s ^ at[0]) + at[1]))
    return pl.pallas_call(
        functools.partial(blocks_kernel, bool(added)),
        grid_spec=pltpu.PrefetchScalarGridSpec(
            num_scalar_prefetch=1,
            grid=(count,),
            in_specs=[whole((tok, units)), whole((tok, units)), block, block]
            + [whole((tok, width))] * len(added),
            out_specs=[whole((tok, width))] * count,
        ),
        out_shape=[jax.ShapeDtypeStruct((tok, width), BF16)] * count,
        compiler_params=params(),
        cost_estimate=cost(2 * tok * units * depth, 2 * units * depth + tok * depth),
        name="blocks",
    )(where, dg, du, wg, wu, *added)


def error_kernel(hid_ref, dy_ref, err_ref, l_ref, r_ref, out_ref):
    grown = dot(hid_ref[...], dy_ref[...]) + err_ref[0].astype(F32)
    out_ref[0] = (grown - dot(l_ref[...], r_ref[...])).astype(BF16)


def error_call(hid, dy, err, l, r):
    units, tok = hid.shape
    depth = dy.shape[1]
    tile = min(512, depth)
    return pl.pallas_call(
        error_kernel,
        grid=(depth // tile,),
        in_specs=[
            whole((units, tok)),
            pl.BlockSpec((tok, tile), lambda d: (0, d)),
            pl.BlockSpec((1, units, tile), lambda d: (0, 0, d)),
            whole((units, SPLIT)),
            pl.BlockSpec((SPLIT, tile), lambda d: (0, d)),
        ],
        out_specs=pl.BlockSpec((1, units, tile), lambda d: (0, 0, d)),
        out_shape=jax.ShapeDtypeStruct(err.shape, BF16),
        compiler_params=params(),
        cost_estimate=cost(2 * tok * units * depth, 4 * units * depth + 2 * tok * depth),
        name="error",
    )(hid, dy, err, l, r)


def row_tile(units):
    return units // 2 if units % 32 == 0 and units > 512 else units


def updated(w, mom, approx):
    return (w.astype(F32) - 0.1 * (0.9 * mom.astype(F32) + approx)).astype(BF16)


def own_kernel(at_ref, mom_ref, w_ref, l_ref, r_ref, mom_out, w_out):
    approx = dot(l_ref[...], r_ref[...])
    mom = mom_ref[...]
    mom_out[...] = 0.9 * mom + approx
    w_out[...] = updated(w_ref[...], mom.astype(BF16), approx)


def own_call(at, mom, w, l, r, half):
    units, cols = mom.shape
    tile = row_tile(units)
    halves = cols // half
    place = pl.BlockSpec((tile, half), lambda c, f, at: (f, at[0] * halves + c))
    mine = pl.BlockSpec((tile, half), lambda c, f, at: (f, c))
    return pl.pallas_call(
        own_kernel,
        grid_spec=pltpu.PrefetchScalarGridSpec(
            num_scalar_prefetch=1,
            grid=(halves, units // tile),
            in_specs=[
                mine,
                place,
                pl.BlockSpec((tile, SPLIT), lambda c, f, at: (f, 0)),
                pl.BlockSpec((SPLIT, half), lambda c, f, at: (0, at[0] * halves + c)),
            ],
            out_specs=[mine, place],
        ),
        out_shape=[jax.ShapeDtypeStruct(mom.shape, F32), jax.ShapeDtypeStruct(w.shape, BF16)],
        compiler_params=params(),
        cost_estimate=cost(512 * units * cols, 12 * units * cols),
        name="own",
    )(at, mom, w, l, r)


def others_kernel(count, at_ref, *refs):
    pieces = refs[:count]
    w_ref, l_ref, r_ref, _, w_out = refs[count:]
    for slot, piece in enumerate(pieces):

        @pl.when(pl.program_id(0) == slot)
        def _(piece=piece):
            w_out[...] = updated(w_ref[...], piece[...], dot(l_ref[...], r_ref[...]))


def others_call(at, pieces, w, l, r, new):
    units, half = pieces[0].shape
    tile = row_tile(units)
    steps = units // tile
    count = len(pieces)

    def piece_spec(slot):
        def index(c, f, at):
            return (jnp.where(c == slot, f, jnp.where(c < slot, 0, steps - 1)), 0)

        return pl.BlockSpec((tile, half), index)

    place = pl.BlockSpec((tile, half), lambda c, f, at: (f, at[c]))
    return pl.pallas_call(
        functools.partial(others_kernel, count),
        grid_spec=pltpu.PrefetchScalarGridSpec(
            num_scalar_prefetch=1,
            grid=(count, steps),
            in_specs=[piece_spec(slot) for slot in range(count)]
            + [
                place,
                pl.BlockSpec((tile, SPLIT), lambda c, f, at: (f, 0)),
                pl.BlockSpec((SPLIT, half), lambda c, f, at: (0, at[c])),
                pl.BlockSpec(memory_space=pl.ANY),
            ],
            out_specs=place,
        ),
        out_shape=jax.ShapeDtypeStruct(w.shape, BF16),
        input_output_aliases={count + 4: 0},
        compiler_params=params(),
        cost_estimate=cost(512 * units * half * count, 6 * units * half * count),
        name="others",
    )(at, *pieces, w, l, r, new)


def exchange(value, axis, mask):
    size = lax.axis_size(axis)
    return lax.ppermute(value, axis, [(i, i ^ mask) for i in range(size)])


def after(value, *earlier):
    return lax.optimization_barrier((value, *earlier))[0]


def masks(size):
    return [1 << bit for bit in range(size.bit_length() - 1)]


def body(inputs, out_grads, w_gate, w_up, w_down, err_down, mom_down, q_down):
    replicas = lax.axis_size("dp")
    shards = lax.axis_size("mp")
    rank_dp = lax.axis_index("dp")
    rank_mp = lax.axis_index("mp")
    cols = mom_down.shape[1]
    half = cols // 2
    w_gate, w_up = w_gate.T, w_up.T

    mom_low = [mom_down[:, :half].astype(BF16), mom_down[:, half:].astype(BF16)]
    far = replicas == 4
    got = {}
    got[2, 0] = exchange(mom_low[0], "dp", 2)
    got[1, 1] = exchange(mom_low[1], "dp", 1)

    hid, d_gate, d_up = hidden_call(inputs, out_grads, w_gate, w_up, w_down)
    late = after(mom_low[0], hid), after(mom_low[1], hid)
    got[1, 0] = exchange(late[0], "dp", 1)
    got[2, 1] = exchange(late[1], "dp", 2)
    for mask in range(3, replicas):
        if not far:
            got[mask, 0] = exchange(late[0], "dp", mask)
            got[mask, 1] = exchange(late[1], "dp", mask)

    left = left_call(q_down.T, err_down, out_grads, hid)
    left = left / replicas
    if far:
        parts = [exchange(left, "dp", mask) for mask in (1, 2, 3)]
    count = shards // 2
    other = blocks_call(rank_mp, 1 - rank_mp % 2, d_gate, d_up, w_gate, w_up, count)
    if far:
        left = (left + parts[0]) + (parts[1] + parts[2])
    else:
        for mask in masks(replicas):
            left = left + exchange(left, "dp", mask)
    left = after(left, other[0])
    other = [exchange(block, "mp", 1) for block in other]
    total = right_call(left, hid, err_down, out_grads)

    if far:
        got[3, 0] = exchange(after(got[2, 0], total), "dp", 1)
        got[3, 1] = exchange(after(got[1, 1], total), "dp", 2)

    mine = blocks_call(rank_mp, rank_mp % 2, d_gate, d_up, w_gate, w_up, count, tuple(other))
    for mask in masks(shards):
        total = total + exchange(total, "mp", mask)
    for mask in masks(replicas):
        total = total + exchange(total, "dp", mask)
    landed = [exchange(mine[slot], "mp", 2 * slot) for slot in range(1, count)]

    l, r = factors_call(total, left, replicas)
    next_err = error_call(hid, out_grads, err_down, l, r)
    at = jnp.reshape(rank_dp, (1,)).astype(jnp.int32)
    next_mom, new = own_call(at, mom_down, w_down, l, r, half)

    in_grads = mine[0].astype(F32)
    for block in landed:
        in_grads = in_grads + block.astype(F32)
    in_grads = in_grads.astype(BF16)

    def place(keys):
        return jnp.stack([2 * (rank_dp ^ mask) + side for mask, side in keys]).astype(jnp.int32)

    first = [(2, 0), (1, 1)]
    second = [key for key in sorted(got) if key not in first]
    for keys in (first, second):
        new = others_call(place(keys), [got[key] for key in keys], w_down, l, r, new)
    return (in_grads, new, next_err, next_mom)


def solution(mesh):
    in_specs = (
        P("dp", None),
        P("dp", None),
        P(None, "mp"),
        P(None, "mp"),
        P("mp", None),
        P("dp", "mp", None),
        P("mp", "dp"),
        P(),
    )
    out_specs = (P("dp", "mp"), P("mp", None), P("dp", "mp", None), P("mp", "dp"))
    return jax.shard_map(body, mesh=mesh, in_specs=in_specs, out_specs=out_specs, check_vma=False)
```

```python
import functools

import jax
import jax.numpy as jnp
from jax import lax
from jax.experimental import pallas as pl
from jax.experimental.pallas import tpu as pltpu
from jax.sharding import PartitionSpec as P

R = 8
SPLIT = 4 * R
EPS = 1e-06
F32 = jnp.float32
BF16 = jnp.bfloat16
HIGH = lax.Precision.HIGHEST
VMEM = 48 * 2**20
ONCE = pl.Buffered(1)
HELD = pl.BlockSpec(memory_space=pl.ANY)


def launch(kernel, name, grid, args, in_specs, out_specs, out_shape, *, places=(), held=(),
           through=(), scratch=(), aliases=None):
    n_in, n_out = len(args), len(out_shape)
    n_held, n_through, n_place = len(held), len(through), len(places)
    first = n_place + n_in

    def inner(*refs):
        outs = first + n_held + n_through
        kernel(*refs[:first], *refs[outs : outs + n_out], *refs[outs + n_out + n_through :])

    links = {first + n_held + i: n_out + i for i in range(n_through)}
    return pl.pallas_call(
        inner,
        grid_spec=pltpu.PrefetchScalarGridSpec(
            num_scalar_prefetch=n_place,
            grid=grid,
            in_specs=list(in_specs) + [HELD] * (n_held + n_through),
            out_specs=list(out_specs) + [HELD] * n_through,
            scratch_shapes=list(scratch),
        ),
        out_shape=list(out_shape)
        + [jax.ShapeDtypeStruct(array.shape, array.dtype) for array in through],
        input_output_aliases={**links, **(aliases or {})},
        compiler_params=pltpu.CompilerParams(vmem_limit_bytes=VMEM),
        cost_estimate=pl.CostEstimate(flops=1, bytes_accessed=1, transcendentals=0),
        name=name,
    )(*places, *args, *held, *through)


def shaped(shape, dtype):
    return jax.ShapeDtypeStruct(shape, dtype)


def dot(left, right):
    return jnp.dot(left, right, preferred_element_type=F32)


def dot_nt(left, right):
    return lax.dot_general(left, right, (((1,), (1,)), ((), ())), preferred_element_type=F32)


def terms(rows):
    hi = rows.astype(BF16).astype(F32)
    rest = rows - hi
    mid = rest.astype(BF16).astype(F32)
    return hi, mid, rest - mid


def spread(rows):
    hi, mid, low = terms(rows)
    return jnp.concatenate([hi, mid, low, jnp.zeros_like(hi)], axis=0).astype(BF16)


def gather_terms(rows):
    return rows[:R] + rows[R : 2 * R] + rows[2 * R : 3 * R]


def tree(parts):
    while len(parts) > 1:
        odd = parts[len(parts) // 2 * 2 :]
        parts = [left + right for left, right in zip(parts[::2], parts[1::2])] + odd
    return parts[0]


def whole(shape):
    return pl.BlockSpec(shape, lambda *_: (0,) * len(shape), pipeline_mode=ONCE)


def row_tile(units):
    return units // 2 if units % 32 == 0 and units > 512 else units


def cast_kernel(mom_ref, *halves):
    half = halves[0].shape[1]
    low, high = mom_ref[:, :half].astype(BF16), mom_ref[:, half:].astype(BF16)
    halves[0][...] = low
    halves[1][...] = high
    halves[2][...] = low
    halves[3][...] = high


def cast_call(mom):
    units, cols = mom.shape
    tile = row_tile(units)
    part = pl.BlockSpec((tile, cols // 2), lambda f: (f, 0))
    return launch(
        cast_kernel,
        "cast",
        (units // tile,),
        [mom],
        [pl.BlockSpec((tile, cols), lambda f: (f, 0))],
        [part] * 4,
        [shaped((units, cols // 2), BF16)] * 4,
    )


def hidden_kernel(x_ref, wg_ref, wu_ref, hid_ref, fac_ref, silu_ref):
    gate = dot_nt(x_ref[...], wg_ref[...])
    up = dot_nt(x_ref[...], wu_ref[...])
    sig = jax.nn.sigmoid(gate)
    silu = gate * sig
    hid_ref[...] = (silu * up).T.astype(BF16)
    fac_ref[...] = up * sig * (1.0 + gate * (1.0 - sig))
    silu_ref[...] = silu


def hidden_call(x, wg, wu, **links):
    tok, depth = x.shape
    units = wg.shape[0]
    tile = min(256, units)
    rows = pl.BlockSpec((tile, depth), lambda f: (f, 0))
    part = pl.BlockSpec((tok, tile), lambda f: (0, f))
    return launch(
        hidden_kernel,
        "hidden",
        (pl.cdiv(units, tile),),
        [x, wg, wu],
        [whole((tok, depth)), rows, rows],
        [pl.BlockSpec((tile, tok), lambda f: (f, 0)), part, part],
        [shaped((units, tok), BF16), shaped((tok, units), F32), shaped((tok, units), F32)],
        **links,
    )


def slopes_kernel(dy_ref, wd_ref, fac_ref, silu_ref, dg_ref, du_ref):
    dh = dot_nt(dy_ref[...], wd_ref[...])
    dg_ref[...] = (dh * fac_ref[...]).astype(BF16)
    du_ref[...] = (dh * silu_ref[...]).astype(BF16)


def slopes_call(dy, wd, fac, silu, **links):
    tok, depth = dy.shape
    units = wd.shape[0]
    tile = min(256, units)
    part = pl.BlockSpec((tok, tile), lambda f: (0, f))
    return launch(
        slopes_kernel,
        "slopes",
        (pl.cdiv(units, tile),),
        [dy, wd, fac, silu],
        [whole((tok, depth)), pl.BlockSpec((tile, depth), lambda f: (f, 0)), part, part],
        [part, part],
        [shaped((tok, units), BF16)] * 2,
        **links,
    )


def left_kernel(replicas, q_ref, err_ref, dy_ref, hid_ref, out_ref, err_acc, dy_acc):
    step = pl.program_id(0)

    @pl.when(step == 0)
    def _():
        err_acc[...] = jnp.zeros_like(err_acc)
        dy_acc[...] = jnp.zeros_like(dy_acc)

    q = spread(q_ref[...])
    err_acc[...] += dot_nt(err_ref[0], q)
    dy_acc[...] += dot_nt(dy_ref[...], q)

    @pl.when(step == pl.num_programs(0) - 1)
    def _():
        mixed = spread(gather_terms(dy_acc[...].T))
        both = gather_terms((err_acc[...] + dot_nt(hid_ref[...], mixed)).T)
        out_ref[...] = both / replicas


def left_call(q_t, err, dy, hid, replicas, **links):
    units, tok = hid.shape
    depth = dy.shape[1]
    tile = min(512, depth)
    return launch(
        functools.partial(left_kernel, replicas),
        "left",
        (depth // tile,),
        [q_t, err, dy, hid],
        [
            pl.BlockSpec((R, tile), lambda d: (0, d)),
            pl.BlockSpec((1, units, tile), lambda d: (0, 0, d)),
            pl.BlockSpec((tok, tile), lambda d: (0, d)),
            whole((units, tok)),
        ],
        [whole((R, units))],
        [shaped((R, units), F32)],
        scratch=[pltpu.VMEM((units, SPLIT), F32), pltpu.VMEM((tok, SPLIT), F32)],
        **links,
    )


def right_kernel(parts, *refs):
    lefts, (hid_ref, err_ref, dy_ref, out_ref, left_ref, left_terms, mixed_terms) = (
        refs[:parts],
        refs[parts:],
    )
    step = pl.program_id(0)
    depth = dy_ref.shape[1]

    @pl.when(step == 0)
    def _():
        left = tree([ref[...] for ref in lefts])
        left_ref[...] = left
        left_terms[...] = spread(left)
        mixed_terms[...] = spread(gather_terms(dot(left_terms[...], hid_ref[...])))
        gram = lax.dot_general(
            left, left, (((1,), (1,)), ((), ())), precision=HIGH, preferred_element_type=F32
        )
        out_ref[:, out_ref.shape[1] - 128 :] = jnp.concatenate(
            [gram, jnp.zeros((R, 128 - R), F32)], axis=1
        )

    part = dot(left_terms[...], err_ref[0]) + dot(mixed_terms[...], dy_ref[...])
    out_ref[:, pl.ds(pl.multiple_of(step * depth, depth), depth)] = gather_terms(part)


def right_call(lefts, hid, err, dy, **links):
    units, tok = hid.shape
    depth = dy.shape[1]
    tile = min(512, depth)
    return launch(
        functools.partial(right_kernel, len(lefts)),
        "right",
        (depth // tile,),
        [*lefts, hid, err, dy],
        [whole((R, units))] * len(lefts)
        + [
            whole((units, tok)),
            pl.BlockSpec((1, units, tile), lambda d: (0, 0, d)),
            pl.BlockSpec((tok, tile), lambda d: (0, d)),
        ],
        [whole((R, depth + 128)), whole((R, units))],
        [shaped((R, depth + 128), F32), shaped((R, units), F32)],
        scratch=[pltpu.VMEM((SPLIT, units), BF16), pltpu.VMEM((SPLIT, tok), BF16)],
        **links,
    )


def sum_kernel(one_ref, two_ref, out_ref):
    out_ref[...] = one_ref[...] + two_ref[...]


def sum_call(one, two, **links):
    return launch(
        sum_kernel,
        "sum",
        (1,),
        [one, two],
        [whole(one.shape)] * 2,
        [whole(one.shape)],
        [shaped(one.shape, one.dtype)],
        **links,
    )


def join_kernel(*refs):
    refs[-1][...] = tree([ref[...].astype(F32) for ref in refs[:-1]]).astype(BF16)


def join_call(parts, **links):
    shape = parts[0].shape
    return launch(
        join_kernel,
        "join",
        (1,),
        parts,
        [whole(shape)] * len(parts),
        [whole(shape)],
        [shaped(shape, BF16)],
        **links,
    )


def factors_kernel(replicas, sum_ref, left_ref, l_ref, r_ref):
    depth = r_ref.shape[1]
    gram = sum_ref[:, depth : depth + R] / replicas
    row = lax.broadcasted_iota(jnp.int32, (R, R), 0)
    col = lax.broadcasted_iota(jnp.int32, (R, R), 1)
    eye = (row == col).astype(F32)
    basis = jnp.zeros((R, R), F32)
    for k in range(R):
        unit = eye[k : k + 1]
        coeffs = jnp.sum(basis * gram[k : k + 1], axis=1, keepdims=True)
        rest = unit - jnp.sum(coeffs * basis, axis=0, keepdims=True)
        rest_col = jnp.sum(eye * rest, axis=1, keepdims=True)
        image = jnp.sum(rest_col * gram, axis=0, keepdims=True)
        square = jnp.sum(image * rest, axis=1, keepdims=True)
        basis = jnp.where(row == k, rest * lax.rsqrt(jnp.maximum(square, 0.0) + EPS), basis)
    left = jnp.dot(basis, left_ref[...], precision=HIGH, preferred_element_type=F32)
    right = jnp.dot(basis, sum_ref[:, :depth], precision=HIGH, preferred_element_type=F32)
    hi, mid, _ = terms(left)
    zero = jnp.zeros_like(hi)
    l_ref[...] = jnp.concatenate([hi, hi, mid, zero], axis=0).T.astype(BF16)
    hi, mid, _ = terms(right / replicas)
    zero = jnp.zeros_like(hi)
    r_ref[...] = jnp.concatenate([hi, mid, hi, zero], axis=0).astype(BF16)


def factors_call(total, left, replicas, **links):
    units = left.shape[1]
    depth = total.shape[1] - 128
    return launch(
        functools.partial(factors_kernel, replicas),
        "factors",
        (1,),
        [total, left],
        [whole(total.shape), whole(left.shape)],
        [whole((units, SPLIT)), whole((SPLIT, depth))],
        [shaped((units, SPLIT), BF16), shaped((SPLIT, depth), BF16)],
        **links,
    )


def other_kernel(where_ref, dg_ref, du_ref, wg_ref, wu_ref, out_ref):
    out_ref[0] = (dot(dg_ref[...], wg_ref[...]) + dot(du_ref[...], wu_ref[...])).astype(BF16)


def mine_kernel(where_ref, dg_ref, du_ref, wg_ref, wu_ref, add_ref, *outs):
    part = dot(dg_ref[...], wg_ref[...]) + dot(du_ref[...], wu_ref[...])
    part = (part + add_ref[0].astype(F32)).astype(BF16)
    for slot, out in enumerate(outs):

        @pl.when(pl.program_id(0) == slot)
        def _(out=out):
            out[...] = part


def blocks_call(pos, parity, slots, count, dg, du, wg, wu, add=None, **links):
    tok, units = dg.shape
    depth = wg.shape[1]
    width = depth // (2 * count)
    where = jnp.stack([pos // 2, parity]).astype(jnp.int32)
    first, steps = slots
    block = pl.BlockSpec((units, width), lambda s, at: (0, 2 * ((s + first) ^ at[0]) + at[1]))
    slot = pl.BlockSpec((1, tok, width), lambda s, at: (s, 0, 0))
    in_specs = [whole((tok, units)), whole((tok, units)), block, block]
    args = [dg, du, wg, wu]
    if add is None:
        kernel = other_kernel
        out_specs = [slot]
        out_shape = [shaped((steps, tok, width), BF16)]
    else:
        kernel = mine_kernel
        in_specs.append(slot)
        args.append(add)
        out_specs = [whole((tok, width))] * steps
        out_shape = [shaped((tok, width), BF16)] * steps
    return launch(
        kernel, "blocks", (steps,), args, in_specs, out_specs, out_shape, places=[where], **links
    )


def updated(w, mom, approx):
    return (w.astype(F32) - 0.1 * (0.9 * mom.astype(F32) + approx)).astype(BF16)


def final_kernel(early, own, at_ref, hid_ref, dy_ref, err_ref, l_ref, r_ref, w_ref, mom_ref, *refs):
    pieces, (err_out, w_out, mom_out) = refs[:-3], refs[-3:]
    step = pl.program_id(0)
    approx = dot(l_ref[...], r_ref[...])
    grown = dot(hid_ref[...], dy_ref[...]) + err_ref[0].astype(F32)
    err_out[0] = (grown - approx).astype(BF16)

    @pl.when((step >= early) & (step < early + own))
    def _():
        mom = mom_ref[...]
        mom_out[...] = 0.9 * mom + approx
        w_out[...] = updated(w_ref[...], mom.astype(BF16), approx)

    for slot, piece in enumerate(pieces):

        @pl.when(step == early + own + slot)
        def _(piece=piece):
            w_out[...] = updated(w_ref[...], piece[...], approx)


def final_call(at, early, hid, dy, err, l, r, w, mom, pieces, **links):
    units, tok = hid.shape
    cols = mom.shape[1]
    half = pieces[0].shape[1]
    own = cols // half
    tile = row_tile(units)
    tiles = units // tile
    count = dy.shape[1] // half

    def held_to(low, high, column):
        def index(c, f, at):
            row = jnp.where(c < low, 0, jnp.where(c > high, tiles - 1, f))
            return row, column(jnp.clip(c, low, high), at)

        return pl.BlockSpec((tile, half), index)

    weights = held_to(early, count - 1, lambda c, at: at[c])
    momenta = held_to(early, early + own - 1, lambda c, at: c - early)
    arrived = [held_to(early + own + s, early + own + s, lambda c, at: 0) for s in range(len(pieces))]
    error = pl.BlockSpec((1, tile, half), lambda c, f, at: (0, f, at[c]))
    return launch(
        functools.partial(final_kernel, early, own),
        "final",
        (count, tiles),
        [hid, dy, err, l, r, w, mom, *pieces],
        [
            pl.BlockSpec((tile, tok), lambda c, f, at: (f, 0)),
            pl.BlockSpec((tok, half), lambda c, f, at: (0, at[c])),
            error,
            pl.BlockSpec((tile, SPLIT), lambda c, f, at: (f, 0)),
            pl.BlockSpec((SPLIT, half), lambda c, f, at: (0, at[c])),
            weights,
            momenta,
            *arrived,
        ],
        [error, weights, momenta],
        [shaped(err.shape, BF16), shaped(w.shape, BF16), shaped(mom.shape, F32)],
        places=[at],
        **links,
    )


def last_kernel(at_ref, low_ref, high_ref, w_ref, l_ref, r_ref, _, w_out):
    half = low_ref.shape[1]
    approx = dot(l_ref[...], r_ref[...])
    w_out[:, :half] = updated(w_ref[:, :half], low_ref[...], approx[:, :half])
    w_out[:, half:] = updated(w_ref[:, half:], high_ref[...], approx[:, half:])


def last_call(at, low, high, w, l, r, new):
    units, half = low.shape
    tile = min(256, units)
    part = pl.BlockSpec((tile, half), lambda f, at: (f, 0))
    place = pl.BlockSpec((tile, 2 * half), lambda f, at: (f, at[0]))
    return launch(
        last_kernel,
        "last",
        (pl.cdiv(units, tile),),
        [low, high, w, l, r, new],
        [
            part,
            part,
            place,
            pl.BlockSpec((tile, SPLIT), lambda f, at: (f, 0)),
            pl.BlockSpec((SPLIT, 2 * half), lambda f, at: (0, at[0])),
            HELD,
        ],
        [place],
        [shaped(w.shape, BF16)],
        places=[at],
        aliases={6: 0},
    )


def exchange(value, axis, mask):
    size = lax.axis_size(axis)
    return lax.ppermute(value, axis, [(i, i ^ mask) for i in range(size)])


def masks(size):
    return [1 << bit for bit in range(size.bit_length() - 1)]


def body(inputs, out_grads, w_gate, w_up, w_down, err_down, mom_down, q_down):
    replicas = lax.axis_size("dp")
    shards = lax.axis_size("mp")
    rank_dp = lax.axis_index("dp")
    rank_mp = lax.axis_index("mp")
    w_gate, w_up = w_gate.T, w_up.T
    count = shards // 2
    split = max(1, count // 2)
    got = {}

    low, high, later_low, later_high = cast_call(mom_down)
    got[2, 0] = exchange(low, "dp", 2)
    got[1, 1] = exchange(high, "dp", 1)

    hid, fac, silu = hidden_call(inputs, w_gate, w_up, held=[low])
    (left,) = left_call(q_down.T, err_down, out_grads, hid, replicas)
    lefts = [left] + [exchange(left, "dp", mask) for mask in range(1, replicas)]
    d_gate, d_up = slopes_call(out_grads, w_down, fac, silu, held=[left])

    def blocks(parity, slots, add=None, **links):
        return blocks_call(
            rank_mp, parity, slots, count, d_gate, d_up, w_gate, w_up, add, **links
        )

    here, there = rank_mp % 2, 1 - rank_mp % 2
    early, late = (0, split), (split, count - split)
    other, later_low, later_high = blocks(
        there,
        early,
        held=[got[2, 0], got[1, 1], *lefts[1:]],
        through=[later_low, later_high],
    )
    got[1, 0] = exchange(later_low, "dp", 1)
    got[2, 1] = exchange(later_high, "dp", 2)

    total, left, other = right_call(lefts, hid, err_down, out_grads, through=[other])

    others = [exchange(other, "mp", 1)]
    mine = []
    for index, mask in enumerate(masks(shards)):
        more = exchange(total, "mp", mask)
        held = []
        if index == 0 and late[1]:
            (other,) = blocks(there, late, held=[total])
            others.append(exchange(other, "mp", 1))
            held = [other]
        elif index == 1 or (index == 0 and not late[1]):
            mine = list(blocks(here, early, others[0], held=[total]))
            held = [mine[0]]
        elif index == 2 and late[1]:
            mine = list(blocks(here, late, others[1], held=[total], through=mine))
            mine = mine[late[1] :] + mine[: late[1]]
            held = [mine[-1]]
        if index == len(masks(shards)) - 1:
            held += [got[1, 0], got[2, 1]]
        (total,) = sum_call(total, more, held=held)
    for mask in masks(replicas):
        (total,) = sum_call(total, exchange(total, "dp", mask))

    l, r, low, high = factors_call(total, left, replicas, through=[got[2, 0], got[1, 1]])
    got[3, 0] = exchange(low, "dp", 1)
    got[3, 1] = exchange(high, "dp", 2)
    got[2, 0], got[1, 1] = low, high
    landed = [exchange(mine[slot], "mp", 2 * slot) for slot in range(1, count)]

    keys = [(1, 1), (2, 0), (1, 0), (2, 1)]
    order = [(3, 0), (3, 1), (0, 0), (0, 1)] + keys
    at = jnp.stack([2 * (rank_dp ^ mask) + side for mask, side in order]).astype(jnp.int32)
    next_err, new, next_mom = final_call(
        at, 2, hid, out_grads, err_down, l, r, w_down, mom_down, [got[key] for key in keys]
    )

    (in_grads,) = join_call([mine[0]] + landed, held=[next_err])

    last = jnp.reshape(rank_dp ^ 3, (1,)).astype(jnp.int32)
    (new,) = last_call(last, got[3, 0], got[3, 1], w_down, l, r, new)
    return (in_grads, new, next_err, next_mom)


def solution(mesh):
    in_specs = (
        P("dp", None),
        P("dp", None),
        P(None, "mp"),
        P(None, "mp"),
        P("mp", None),
        P("dp", "mp", None),
        P("mp", "dp"),
        P(),
    )
    out_specs = (P("dp", "mp"), P("mp", None), P("dp", "mp", None), P("mp", "dp"))
    return jax.shard_map(body, mesh=mesh, in_specs=in_specs, out_specs=out_specs, check_vma=False)
```

```python
import functools

import jax
import jax.numpy as jnp
from jax import lax
from jax.experimental import pallas as pl
from jax.experimental.pallas import tpu as pltpu
from jax.sharding import PartitionSpec as P

R = 8
SPLIT = 4 * R
EPS = 1e-06
F32 = jnp.float32
BF16 = jnp.bfloat16
HIGH = lax.Precision.HIGHEST
VMEM = 62 * 2**20
ONCE = pl.Buffered(1)
HELD = pl.BlockSpec(memory_space=pl.ANY)


def launch(kernel, name, grid, args, in_specs, out_specs, out_shape, *, places=(), held=(),
           through=(), scratch=(), aliases=None):
    n_in, n_out = len(args), len(out_shape)
    n_held, n_through, n_place = len(held), len(through), len(places)
    first = n_place + n_in

    def inner(*refs):
        outs = first + n_held + n_through
        kernel(*refs[:first], *refs[outs : outs + n_out], *refs[outs + n_out + n_through :])

    links = {first + n_held + i: n_out + i for i in range(n_through)}
    return pl.pallas_call(
        inner,
        grid_spec=pltpu.PrefetchScalarGridSpec(
            num_scalar_prefetch=n_place,
            grid=grid,
            in_specs=list(in_specs) + [HELD] * (n_held + n_through),
            out_specs=list(out_specs) + [HELD] * n_through,
            scratch_shapes=list(scratch),
        ),
        out_shape=list(out_shape)
        + [jax.ShapeDtypeStruct(array.shape, array.dtype) for array in through],
        input_output_aliases={**links, **(aliases or {})},
        compiler_params=pltpu.CompilerParams(vmem_limit_bytes=VMEM),
        cost_estimate=pl.CostEstimate(flops=1, bytes_accessed=1, transcendentals=0),
        name=name,
    )(*places, *args, *held, *through)


def shaped(shape, dtype):
    return jax.ShapeDtypeStruct(shape, dtype)


def dot(left, right):
    return jnp.dot(left, right, preferred_element_type=F32)


def dot_nt(left, right):
    return lax.dot_general(left, right, (((1,), (1,)), ((), ())), preferred_element_type=F32)


def terms(rows):
    hi = rows.astype(BF16).astype(F32)
    rest = rows - hi
    mid = rest.astype(BF16).astype(F32)
    return hi, mid, rest - mid


def spread(rows):
    hi, mid, low = terms(rows)
    return jnp.concatenate([hi, mid, low, jnp.zeros_like(hi)], axis=0).astype(BF16)


def gather_terms(rows):
    return rows[:R] + rows[R : 2 * R] + rows[2 * R : 3 * R]


def tree(parts):
    while len(parts) > 1:
        odd = parts[len(parts) // 2 * 2 :]
        parts = [left + right for left, right in zip(parts[::2], parts[1::2])] + odd
    return parts[0]


def whole(shape):
    return pl.BlockSpec(shape, lambda *_: (0,) * len(shape), pipeline_mode=ONCE)


def unit_tile(units):
    return 256 if units > 512 and units % 16 == 0 else units


def cast_kernel(mom_ref, out_ref):
    out_ref[...] = mom_ref[...].astype(BF16)


def cast_call(mom):
    units, cols = mom.shape
    tile = unit_tile(units)
    part = pl.BlockSpec((tile, cols), lambda f: (f, 0))
    return launch(
        cast_kernel, "cast", (pl.cdiv(units, tile),), [mom], [part], [part], [shaped(mom.shape, BF16)]
    )


def hidden_kernel(
    x_ref, wg_ref, wu_ref, wd_ref, q_ref, dy_any, hid_ref, dg_ref, du_ref, dyq_ref, dy_ref, sem
):
    fetch = pltpu.make_async_copy(dy_any, dy_ref, sem)

    @pl.when(pl.program_id(0) == 0)
    def _():
        fetch.start()

    gate = dot_nt(x_ref[...], wg_ref[...])
    up = dot_nt(x_ref[...], wu_ref[...])

    @pl.when(pl.program_id(0) == 0)
    def _():
        fetch.wait()
        dyq_ref[...] = gather_terms(dot_nt(spread(q_ref[...]), dy_ref[...]))

    dh = dot_nt(dy_ref[...], wd_ref[...])
    sig = jax.nn.sigmoid(gate)
    silu = gate * sig
    hid_ref[...] = (silu * up).T.astype(BF16)
    dg_ref[0] = (dh * up * sig * (1.0 + gate * (1.0 - sig))).astype(BF16)
    du_ref[0] = (dh * silu).astype(BF16)


def hidden_call(x, dy, wg, wu, wd, q_t, **links):
    tok, depth = x.shape
    units = wg.shape[0]
    tile = unit_tile(units)
    tiles = pl.cdiv(units, tile)
    rows = pl.BlockSpec((tile, depth), lambda f: (f, 0))
    part = pl.BlockSpec((1, tok, tile), lambda f: (f, 0, 0))
    return launch(
        hidden_kernel,
        "hidden",
        (tiles,),
        [x, wg, wu, wd, q_t, dy],
        [whole((tok, depth)), rows, rows, rows, whole(q_t.shape), HELD],
        [pl.BlockSpec((tile, tok), lambda f: (f, 0)), part, part, whole((R, tok))],
        [
            shaped((units, tok), BF16),
            shaped((tiles, tok, tile), BF16),
            shaped((tiles, tok, tile), BF16),
            shaped((R, tok), F32),
        ],
        scratch=[pltpu.VMEM((tok, depth), BF16), pltpu.SemaphoreType.DMA(())],
        **links,
    )


def left_kernel(replicas, q_ref, dyq_ref, err_ref, hid_ref, out_ref, q_terms, dyq_terms):
    @pl.when(pl.program_id(0) == 0)
    def _():
        q_terms[...] = spread(q_ref[...])
        dyq_terms[...] = spread(dyq_ref[...])

    both = dot_nt(err_ref[0], q_terms[...]) + dot_nt(hid_ref[...], dyq_terms[...])
    out_ref[...] = gather_terms(both.T) / replicas


def left_call(q_t, dyq, err, hid, replicas, **links):
    units, tok = hid.shape
    depth = q_t.shape[1]
    tile = unit_tile(units)
    return launch(
        functools.partial(left_kernel, replicas),
        "left",
        (pl.cdiv(units, tile),),
        [q_t, dyq, err, hid],
        [
            whole(q_t.shape),
            whole(dyq.shape),
            pl.BlockSpec((1, tile, depth), lambda f: (0, f, 0)),
            pl.BlockSpec((tile, tok), lambda f: (f, 0)),
        ],
        [pl.BlockSpec((R, tile), lambda f: (0, f))],
        [shaped((R, units), F32)],
        scratch=[pltpu.VMEM((SPLIT, depth), BF16), pltpu.VMEM((SPLIT, tok), BF16)],
        **links,
    )


def columns(ref, step, tile):
    if ref.shape[1] == tile:
        return ref[...]
    return ref[:, pl.ds(pl.multiple_of(step * tile, tile), tile)]


def right_kernel(parts, dy_steps, *refs):
    lefts = refs[:parts]
    hid_ref, err_ref, dy_ref, out_ref, left_ref, left_terms, mixed_terms, total = refs[parts:]
    step = pl.program_id(0)
    units = left_ref.shape[1]
    tile, depth = err_ref.shape[1:]
    dy_tile = dy_ref.shape[0]
    tail = units % tile
    last = pl.num_programs(0) - 1

    @pl.when(step == 0)
    def _():
        left = tree([ref[...] for ref in lefts])
        left_ref[...] = left
        left_terms[:, :units] = spread(left)
        mixed_terms[...] = spread(gather_terms(dot(left_terms[:, :units], hid_ref[...])))
        gram = lax.dot_general(
            left, left, (((1,), (1,)), ((), ())), precision=HIGH, preferred_element_type=F32
        )
        out_ref[:, depth:] = jnp.concatenate([gram, jnp.zeros((R, 128 - R), F32)], axis=1)
        total[...] = jnp.zeros_like(total)

    @pl.when(step < dy_steps)
    def _():
        total[...] += dot(columns(mixed_terms, step, dy_tile), dy_ref[...])

    if tail:

        @pl.when(step < last)
        def _():
            total[...] += dot(columns(left_terms, step, tile), err_ref[0])

        @pl.when(step == last)
        def _():
            total[...] += dot(left_terms[:, units - tail : units], err_ref[0, :tail])

    else:
        total[...] += dot(columns(left_terms, step, tile), err_ref[0])

    @pl.when(step == last)
    def _():
        out_ref[:, :depth] = gather_terms(total[...])


def right_call(lefts, hid, err, dy, **links):
    units, tok = hid.shape
    depth = dy.shape[1]
    tile = unit_tile(units)
    tiles = pl.cdiv(units, tile)
    dy_steps = 2 if tiles > 1 else 1
    return launch(
        functools.partial(right_kernel, len(lefts), dy_steps),
        "right",
        (tiles,),
        [*lefts, hid, err, dy],
        [whole((R, units))] * len(lefts)
        + [
            whole((units, tok)),
            pl.BlockSpec((1, tile, depth), lambda f: (0, f, 0)),
            pl.BlockSpec((tok // dy_steps, depth), lambda f: (jnp.minimum(f, dy_steps - 1), 0)),
        ],
        [whole((R, depth + 128)), whole((R, units))],
        [shaped((R, depth + 128), F32), shaped((R, units), F32)],
        scratch=[
            pltpu.VMEM((SPLIT, tiles * tile), BF16),
            pltpu.VMEM((SPLIT, tok), BF16),
            pltpu.VMEM((SPLIT, depth), F32),
        ],
        **links,
    )


def sum_kernel(one_ref, two_ref, out_ref):
    out_ref[...] = one_ref[...] + two_ref[...]


def sum_call(one, two, **links):
    return launch(
        sum_kernel,
        "sum",
        (1,),
        [one, two],
        [whole(one.shape)] * 2,
        [whole(one.shape)],
        [shaped(one.shape, one.dtype)],
        **links,
    )


def join_kernel(*refs):
    refs[-1][...] = tree([ref[...].astype(F32) for ref in refs[:-1]]).astype(BF16)


def join_call(parts, **links):
    shape = parts[0].shape
    return launch(
        join_kernel,
        "join",
        (1,),
        parts,
        [whole(shape)] * len(parts),
        [whole(shape)],
        [shaped(shape, BF16)],
        **links,
    )


def factors_kernel(replicas, sum_ref, left_ref, l_ref, r_ref):
    depth = r_ref.shape[1]
    gram = sum_ref[:, depth : depth + R] / replicas
    row = lax.broadcasted_iota(jnp.int32, (R, R), 0)
    col = lax.broadcasted_iota(jnp.int32, (R, R), 1)
    eye = (row == col).astype(F32)
    basis = jnp.zeros((R, R), F32)
    for k in range(R):
        unit = eye[k : k + 1]
        coeffs = jnp.sum(basis * gram[k : k + 1], axis=1, keepdims=True)
        rest = unit - jnp.sum(coeffs * basis, axis=0, keepdims=True)
        rest_col = jnp.sum(eye * rest, axis=1, keepdims=True)
        image = jnp.sum(rest_col * gram, axis=0, keepdims=True)
        square = jnp.sum(image * rest, axis=1, keepdims=True)
        basis = jnp.where(row == k, rest * lax.rsqrt(jnp.maximum(square, 0.0) + EPS), basis)
    left = jnp.dot(basis, left_ref[...], precision=HIGH, preferred_element_type=F32)
    right = jnp.dot(basis, sum_ref[:, :depth], precision=HIGH, preferred_element_type=F32)
    hi, mid, _ = terms(left)
    zero = jnp.zeros_like(hi)
    l_ref[...] = jnp.concatenate([hi, hi, mid, zero], axis=0).T.astype(BF16)
    hi, mid, _ = terms(right / replicas)
    zero = jnp.zeros_like(hi)
    r_ref[...] = jnp.concatenate([hi, mid, hi, zero], axis=0).astype(BF16)


def factors_call(total, left, replicas, **links):
    units = left.shape[1]
    depth = total.shape[1] - 128
    return launch(
        functools.partial(factors_kernel, replicas),
        "factors",
        (1,),
        [total, left],
        [whole(total.shape), whole(left.shape)],
        [whole((units, SPLIT)), whole((SPLIT, depth))],
        [shaped((units, SPLIT), BF16), shaped((SPLIT, depth), BF16)],
        **links,
    )


def blocks_kernel(width, tail, where_ref, dg_ref, du_ref, wg_ref, wu_ref, other_ref, mine_ref, acc):
    step = pl.program_id(0)
    last = pl.num_programs(0) - 1
    pairs = acc.shape[1] // width

    def add(units, first):
        for block in range(pairs):
            cols = slice(block * width, (block + 1) * width)
            part = dot(dg_ref[0, :, :units], wg_ref[:units, cols])
            part += dot(du_ref[0, :, :units], wu_ref[:units, cols])
            acc[:, cols] = part if first else acc[:, cols] + part

    full = dg_ref.shape[2]

    @pl.when(step == 0)
    def _():
        add(full, True)

    @pl.when((step > 0) & ((step < last) | (tail == full)))
    def _():
        add(full, False)

    if tail != full:

        @pl.when((step > 0) & (step == last))
        def _():
            add(tail, False)

    @pl.when(step == last)
    def _():
        for block in range(pairs):
            cols = slice(block * width, (block + 1) * width)
            slot = (block // 2) ^ lax.rem(where_ref[0], pairs // 2)

            @pl.when(where_ref[1] == block % 2)
            def _(cols=cols, slot=slot):
                mine_ref[slot] = acc[:, cols]

            @pl.when(where_ref[1] != block % 2)
            def _(cols=cols, slot=slot):
                other_ref[slot] = acc[:, cols].astype(BF16)


def blocks_call(pos, side, count, dg, du, wg, wu, **links):
    tiles, tok, tile = dg.shape
    units, depth = wg.shape
    width = depth // (2 * count)
    split = count // 2
    tail = units - (tiles - 1) * tile
    where = jnp.stack([pos // 2, pos % 2]).astype(jnp.int32)
    part = pl.BlockSpec((1, tok, tile), lambda f, at: (f, 0, 0))
    rows = pl.BlockSpec((tile, depth // 2), lambda f, at: (f, (at[0] // split) ^ side))
    return launch(
        functools.partial(blocks_kernel, width, tail),
        "blocks",
        (tiles,),
        [dg, du, wg, wu],
        [part, part, rows, rows],
        [whole((split, tok, width))] * 2,
        [shaped((split, tok, width), BF16), shaped((split, tok, width), F32)],
        places=[where],
        scratch=[pltpu.VMEM((tok, depth // 2), F32)],
        **links,
    )


def add_kernel(one_ref, two_ref, *outs):
    for slot, out in enumerate(outs):

        @pl.when(pl.program_id(0) == slot)
        def _(out=out):
            out[...] = (one_ref[0] + two_ref[0].astype(F32)).astype(BF16)


def add_call(one, two, **links):
    slots, tok, width = one.shape
    slot = pl.BlockSpec((1, tok, width), lambda s: (s, 0, 0))
    return launch(
        add_kernel,
        "add",
        (slots,),
        [one, two],
        [slot, slot],
        [whole((tok, width))] * slots,
        [shaped((tok, width), BF16)] * slots,
        **links,
    )


def error_kernel(hid_ref, dy_ref, err_ref, l_ref, r_ref, out_ref):
    grown = dot(hid_ref[...], dy_ref[...]) + err_ref[0].astype(F32)
    out_ref[0] = (grown - dot(l_ref[...], r_ref[...])).astype(BF16)


def error_call(hid, dy, err, l, r, **links):
    units, tok = hid.shape
    depth = dy.shape[1]
    tile = 352 if units > 512 else units
    rows = pl.BlockSpec((1, tile, depth), lambda f: (0, f, 0))
    return launch(
        error_kernel,
        "error",
        (pl.cdiv(units, tile),),
        [hid, dy, err, l, r],
        [
            pl.BlockSpec((tile, tok), lambda f: (f, 0)),
            whole(dy.shape),
            rows,
            pl.BlockSpec((tile, SPLIT), lambda f: (f, 0)),
            whole(r.shape),
        ],
        [rows],
        [shaped(err.shape, BF16)],
        **links,
    )


def update_kernel(at_ref, mom_ref, all_ref, w_ref, l_ref, r_ref, mine_ref, mom_out, w_out):
    cols = mom_ref.shape[1]
    mom_out[...] = 0.9 * mom_ref[...] + dot(l_ref[...], mine_ref[...])
    for part in range(all_ref.shape[0]):
        at = slice(part * cols, (part + 1) * cols)
        mom = 0.9 * all_ref[part].astype(F32) + dot(l_ref[...], r_ref[:, at])
        w_out[:, at] = (w_ref[:, at].astype(F32) - 0.1 * mom).astype(BF16)


def update_call(at, mom, everyone, w, l, r, **links):
    units, cols = mom.shape
    depth = w.shape[1]
    tile = 176 if units > 512 else units
    rows = pl.BlockSpec((tile, depth), lambda f, at: (f, 0))
    mine = pl.BlockSpec((tile, cols), lambda f, at: (f, 0))
    return launch(
        update_kernel,
        "update",
        (pl.cdiv(units, tile),),
        [mom, everyone, w, l, r, r],
        [
            mine,
            pl.BlockSpec((everyone.shape[0], tile, cols), lambda f, at: (0, f, 0)),
            rows,
            pl.BlockSpec((tile, SPLIT), lambda f, at: (f, 0)),
            whole(r.shape),
            pl.BlockSpec((SPLIT, cols), lambda f, at: (0, at[0])),
        ],
        [mine, rows],
        [shaped(mom.shape, F32), shaped(w.shape, BF16)],
        places=[at],
        **links,
    )


def exchange(value, axis, mask):
    size = lax.axis_size(axis)
    return lax.ppermute(value, axis, [(i, i ^ mask) for i in range(size)])


def masks(size):
    return [1 << bit for bit in range(size.bit_length() - 1)]


def body(inputs, out_grads, w_gate, w_up, w_down, err_down, mom_down, q_down):
    replicas = lax.axis_size("dp")
    shards = lax.axis_size("mp")
    rank_dp = lax.axis_index("dp")
    rank_mp = lax.axis_index("mp")
    w_gate, w_up, q_t = w_gate.T, w_up.T, q_down.T
    count = shards // 2

    (low,) = cast_call(mom_down)
    everyone = lax.all_gather(low, "dp")

    hid, d_gate, d_up, dyq = hidden_call(
        inputs, out_grads, w_gate, w_up, w_down, q_t, held=[low]
    )
    (left,) = left_call(q_t, dyq, err_down, hid, replicas)
    lefts = [left] + [exchange(left, "dp", mask) for mask in range(1, replicas)]

    def blocks(side, **links):
        return blocks_call(rank_mp, side, count, d_gate, d_up, w_gate, w_up, **links)

    other, first = blocks(0, held=[left])
    total, left, other = right_call(lefts, hid, err_down, out_grads, through=[other])

    others = [exchange(other, "mp", 1)]
    steps = masks(shards)
    for index, mask in enumerate(steps):
        more = exchange(total, "mp", mask)
        held, through = [], []
        if index == 0:
            other, second = blocks(1, held=[total])
            others.append(exchange(other, "mp", 1))
            held = [other]
        elif index == 1:
            mine = list(add_call(first, others[0], held=[total]))
            held = [mine[0]]
        elif index == 2:
            mine += list(add_call(second, others[1], held=[total]))
            held = [mine[-1]]
        if index == len(steps) - 1:
            through = mine
        total, *mine_now = sum_call(total, more, held=held, through=through)
        if through:
            mine = mine_now
    landed = [exchange(mine[slot], "mp", 2 * slot) for slot in range(1, count)]
    for mask in masks(replicas):
        (total,) = sum_call(total, exchange(total, "dp", mask))

    l, r = factors_call(total, left, replicas)
    (next_err,) = error_call(hid, out_grads, err_down, l, r)
    (in_grads,) = join_call([mine[0]] + landed, held=[next_err])
    at = jnp.reshape(rank_dp, (1,)).astype(jnp.int32)
    next_mom, new = update_call(at, mom_down, everyone, w_down, l, r, held=[in_grads])
    return (in_grads, new, next_err, next_mom)


def solution(mesh):
    in_specs = (
        P("dp", None),
        P("dp", None),
        P(None, "mp"),
        P(None, "mp"),
        P("mp", None),
        P("dp", "mp", None),
        P("mp", "dp"),
        P(),
    )
    out_specs = (P("dp", "mp"), P("mp", None), P("dp", "mp", None), P("mp", "dp"))
    return jax.shard_map(body, mesh=mesh, in_specs=in_specs, out_specs=out_specs, check_vma=False)
```

```python
import functools

import jax
import jax.numpy as jnp
from jax import lax
from jax.experimental import pallas as pl
from jax.experimental.pallas import tpu as pltpu
from jax.sharding import PartitionSpec as P

R = 8
SPLIT = 4 * R
EPS = 1e-06
F32 = jnp.float32
BF16 = jnp.bfloat16
HIGH = lax.Precision.HIGHEST
VMEM = 48 * 2**20
SMALL = 12 * 2**20
LARGE = 62 * 2**20
ONCE = pl.Buffered(1)
STREAMS = 4
HELD = pl.BlockSpec(memory_space=pl.ANY)


def launch(kernel, name, grid, args, in_specs, out_specs, out_shape, *, places=(), held=(),
           through=(), scratch=(), vmem=VMEM):
    n_in, n_out = len(args), len(out_shape)
    n_held, n_through, n_place = len(held), len(through), len(places)
    first = n_place + n_in

    def inner(*refs):
        outs = first + n_held + n_through
        kernel(*refs[:first], *refs[outs : outs + n_out], *refs[outs + n_out + n_through :])

    links = {first + n_held + i: n_out + i for i in range(n_through)}
    return pl.pallas_call(
        inner,
        grid_spec=pltpu.PrefetchScalarGridSpec(
            num_scalar_prefetch=n_place,
            grid=grid,
            in_specs=list(in_specs) + [HELD] * (n_held + n_through),
            out_specs=list(out_specs) + [HELD] * n_through,
            scratch_shapes=list(scratch),
        ),
        out_shape=list(out_shape)
        + [jax.ShapeDtypeStruct(array.shape, array.dtype) for array in through],
        input_output_aliases=links,
        compiler_params=pltpu.CompilerParams(vmem_limit_bytes=vmem),
        cost_estimate=pl.CostEstimate(flops=1, bytes_accessed=1, transcendentals=0),
        name=name,
    )(*places, *args, *held, *through)


def shaped(shape, dtype):
    return jax.ShapeDtypeStruct(shape, dtype)


def dot(left, right):
    return jnp.dot(left, right, preferred_element_type=F32)


def dot_nt(left, right):
    return lax.dot_general(left, right, (((1,), (1,)), ((), ())), preferred_element_type=F32)


def terms(rows):
    hi = rows.astype(BF16).astype(F32)
    rest = rows - hi
    mid = rest.astype(BF16).astype(F32)
    return hi, mid, rest - mid


def spread(rows):
    hi, mid, low = terms(rows)
    return jnp.concatenate([hi, mid, low, jnp.zeros_like(hi)], axis=0).astype(BF16)


def gather_terms(rows):
    return rows[:R] + rows[R : 2 * R] + rows[2 * R : 3 * R]


def tree(parts):
    while len(parts) > 1:
        odd = parts[len(parts) // 2 * 2 :]
        parts = [left + right for left, right in zip(parts[::2], parts[1::2])] + odd
    return parts[0]


def whole(shape):
    return pl.BlockSpec(shape, lambda *_: (0,) * len(shape), pipeline_mode=ONCE)


def unit_tile(units):
    return 256 if units > 512 and units % 16 == 0 else units


def cast_kernel(mom_ref, out_ref):
    out_ref[...] = mom_ref[...].astype(BF16)


def cast_call(mom):
    units, cols = mom.shape
    tile = 352 if units > 512 else units
    part = pl.BlockSpec((tile, cols), lambda f: (f, 0))
    return launch(
        cast_kernel,
        "cast",
        (pl.cdiv(units, tile),),
        [mom],
        [part],
        [part],
        [shaped(mom.shape, BF16)],
    )


def dot_parts(left_ref, parts):
    width = parts[0].shape[-1]
    total = None
    for at, part in enumerate(parts):
        more = dot_nt(left_ref[:, at * width : (at + 1) * width], part[...])
        total = more if total is None else total + more
    return total


def hidden_kernel(
    x_ref, q_ref, dy_any, *refs
):
    weights, (hid_ref, dg_ref, du_ref, dyq_ref, dy_ref, sem) = refs[:-6], refs[-6:]
    ways = len(weights) // 3
    fetch = pltpu.make_async_copy(dy_any, dy_ref, sem)

    @pl.when(pl.program_id(0) == 0)
    def _():
        fetch.start()

    gate = dot_parts(x_ref, weights[:ways])
    up = dot_parts(x_ref, weights[ways : 2 * ways])

    @pl.when(pl.program_id(0) == 0)
    def _():
        fetch.wait()
        dyq_ref[...] = gather_terms(dot_nt(spread(q_ref[...]), dy_ref[...]))

    dh = dot_parts(dy_ref, weights[2 * ways :])
    sig = jax.nn.sigmoid(gate)
    silu = gate * sig
    hid_ref[...] = (silu * up).T.astype(BF16)
    dg_ref[0] = (dh * up * sig * (1.0 + gate * (1.0 - sig))).astype(BF16)
    du_ref[0] = (dh * silu).astype(BF16)


def hidden_call(x, dy, wg, wu, wd, q_t, **links):
    tok, depth = x.shape
    units = wg.shape[0]
    tile = unit_tile(units)
    tiles = pl.cdiv(units, tile)
    ways = 2
    rows = [pl.BlockSpec((tile, depth // ways), lambda f, c=c: (f, c)) for c in range(ways)]
    part = pl.BlockSpec((1, tok, tile), lambda f: (f, 0, 0))
    return launch(
        hidden_kernel,
        "hidden",
        (tiles,),
        [x, q_t, dy] + [wg] * ways + [wu] * ways + [wd] * ways,
        [whole((tok, depth)), whole(q_t.shape), HELD] + rows * 3,
        [pl.BlockSpec((tile, tok), lambda f: (f, 0)), part, part, whole((R, tok))],
        [
            shaped((units, tok), BF16),
            shaped((tiles, tok, tile), BF16),
            shaped((tiles, tok, tile), BF16),
            shaped((R, tok), F32),
        ],
        scratch=[pltpu.VMEM((tok, depth), BF16), pltpu.SemaphoreType.DMA(())],
        **links,
    )


def left_kernel(replicas, q_ref, dyq_ref, hid_ref, *refs):
    errs, (out_ref, q_terms, dyq_terms) = refs[:-3], refs[-3:]
    width = errs[0].shape[2]

    @pl.when(pl.program_id(0) == 0)
    def _():
        q_terms[...] = spread(q_ref[...])
        dyq_terms[...] = spread(dyq_ref[...])

    both = dot_nt(hid_ref[...], dyq_terms[...])
    for at, err_ref in enumerate(errs):
        both += dot_nt(err_ref[0], q_terms[:, at * width : (at + 1) * width])
    out_ref[...] = gather_terms(both.T) / replicas


def error_streams(tile, depth):
    shape = (1, tile, depth // STREAMS)
    return [pl.BlockSpec(shape, lambda f, c=c: (0, f, c)) for c in range(STREAMS)]


def left_call(q_t, dyq, err, hid, replicas, **links):
    units, tok = hid.shape
    depth = q_t.shape[1]
    tile = unit_tile(units)
    return launch(
        functools.partial(left_kernel, replicas),
        "left",
        (pl.cdiv(units, tile),),
        [q_t, dyq, hid] + [err] * STREAMS,
        [whole(q_t.shape), whole(dyq.shape), pl.BlockSpec((tile, tok), lambda f: (f, 0))]
        + error_streams(tile, depth),
        [pl.BlockSpec((R, tile), lambda f: (0, f))],
        [shaped((R, units), F32)],
        scratch=[pltpu.VMEM((SPLIT, depth), BF16), pltpu.VMEM((SPLIT, tok), BF16)],
        **links,
    )


def columns(ref, step, tile):
    if ref.shape[1] == tile:
        return ref[...]
    return ref[:, pl.ds(pl.multiple_of(step * tile, tile), tile)]


def right_kernel(parts, dy_steps, *refs):
    lefts = refs[:parts]
    errs, (hid_ref, dy_ref, out_ref, left_ref, left_terms, mixed_terms, total) = (
        refs[parts:-7],
        refs[-7:],
    )
    step = pl.program_id(0)
    units = left_ref.shape[1]
    tile, width = errs[0].shape[1:]
    depth = width * len(errs)
    dy_tile = dy_ref.shape[0]
    tail = units % tile
    last = pl.num_programs(0) - 1

    @pl.when(step == 0)
    def _():
        left = tree([ref[...] for ref in lefts])
        left_ref[...] = left
        left_terms[:, :units] = spread(left)
        mixed_terms[...] = spread(gather_terms(dot(left_terms[:, :units], hid_ref[...])))
        gram = lax.dot_general(
            left, left, (((1,), (1,)), ((), ())), precision=HIGH, preferred_element_type=F32
        )
        out_ref[:, depth:] = jnp.concatenate([gram, jnp.zeros((R, 128 - R), F32)], axis=1)
        total[...] = jnp.zeros_like(total)

    @pl.when(step < dy_steps)
    def _():
        total[...] += dot(columns(mixed_terms, step, dy_tile), dy_ref[...])

    if tail:

        @pl.when(step < last)
        def _():
            left = columns(left_terms, step, tile)
            for at, err_ref in enumerate(errs):
                total[:, at * width : (at + 1) * width] += dot(left, err_ref[0])

        @pl.when(step == last)
        def _():
            left = left_terms[:, units - tail : units]
            for at, err_ref in enumerate(errs):
                total[:, at * width : (at + 1) * width] += dot(left, err_ref[0, :tail])

    else:
        left = columns(left_terms, step, tile)
        for at, err_ref in enumerate(errs):
            total[:, at * width : (at + 1) * width] += dot(left, err_ref[0])

    @pl.when(step == last)
    def _():
        out_ref[:, :depth] = gather_terms(total[...])


def right_call(lefts, hid, err, dy, **links):
    units, tok = hid.shape
    depth = dy.shape[1]
    tile = unit_tile(units)
    tiles = pl.cdiv(units, tile)
    dy_steps = 2 if tiles > 1 else 1
    return launch(
        functools.partial(right_kernel, len(lefts), dy_steps),
        "right",
        (tiles,),
        [*lefts] + [err] * STREAMS + [hid, dy],
        [whole((R, units))] * len(lefts)
        + error_streams(tile, depth)
        + [
            whole((units, tok)),
            pl.BlockSpec((tok // dy_steps, depth), lambda f: (jnp.minimum(f, dy_steps - 1), 0)),
        ],
        [whole((R, depth + 128)), whole((R, units))],
        [shaped((R, depth + 128), F32), shaped((R, units), F32)],
        scratch=[
            pltpu.VMEM((SPLIT, tiles * tile), BF16),
            pltpu.VMEM((SPLIT, tok), BF16),
            pltpu.VMEM((SPLIT, depth), F32),
        ],
        **links,
    )


def sum_kernel(one_ref, two_ref, out_ref):
    out_ref[...] = one_ref[...] + two_ref[...]


def sum_call(one, two, **links):
    return launch(
        sum_kernel,
        "sum",
        (1,),
        [one, two],
        [whole(one.shape)] * 2,
        [whole(one.shape)],
        [shaped(one.shape, one.dtype)],
        vmem=SMALL,
        **links,
    )


def join_kernel(*refs):
    refs[-1][...] = tree([ref[...].astype(F32) for ref in refs[:-1]]).astype(BF16)


def join_call(parts, **links):
    shape = parts[0].shape
    return launch(
        join_kernel,
        "join",
        (1,),
        parts,
        [whole(shape)] * len(parts),
        [whole(shape)],
        [shaped(shape, BF16)],
        vmem=SMALL,
        **links,
    )


def factors_kernel(replicas, sum_ref, left_ref, l_ref, r_ref):
    depth = r_ref.shape[1]
    gram = sum_ref[:, depth : depth + R] / replicas
    row = lax.broadcasted_iota(jnp.int32, (R, R), 0)
    col = lax.broadcasted_iota(jnp.int32, (R, R), 1)
    eye = (row == col).astype(F32)
    basis = jnp.zeros((R, R), F32)
    for k in range(R):
        unit = eye[k : k + 1]
        coeffs = jnp.sum(basis * gram[k : k + 1], axis=1, keepdims=True)
        rest = unit - jnp.sum(coeffs * basis, axis=0, keepdims=True)
        rest_col = jnp.sum(eye * rest, axis=1, keepdims=True)
        image = jnp.sum(rest_col * gram, axis=0, keepdims=True)
        square = jnp.sum(image * rest, axis=1, keepdims=True)
        basis = jnp.where(row == k, rest * lax.rsqrt(jnp.maximum(square, 0.0) + EPS), basis)
    left = jnp.dot(basis, left_ref[...], precision=HIGH, preferred_element_type=F32)
    right = jnp.dot(basis, sum_ref[:, :depth], precision=HIGH, preferred_element_type=F32)
    hi, mid, _ = terms(left)
    zero = jnp.zeros_like(hi)
    l_ref[...] = jnp.concatenate([hi, hi, mid, zero], axis=0).T.astype(BF16)
    hi, mid, _ = terms(right / replicas)
    zero = jnp.zeros_like(hi)
    r_ref[...] = jnp.concatenate([hi, mid, hi, zero], axis=0).astype(BF16)


def factors_call(total, left, replicas, **links):
    units = left.shape[1]
    depth = total.shape[1] - 128
    return launch(
        functools.partial(factors_kernel, replicas),
        "factors",
        (1,),
        [total, left],
        [whole(total.shape), whole(left.shape)],
        [whole((units, SPLIT)), whole((SPLIT, depth))],
        [shaped((units, SPLIT), BF16), shaped((SPLIT, depth), BF16)],
        vmem=SMALL,
        **links,
    )


def blocks_kernel(width, tail, where_ref, dg_ref, du_ref, wg_ref, wu_ref, other_ref, mine_ref, acc):
    step = pl.program_id(0)
    last = pl.num_programs(0) - 1
    pairs = acc.shape[1] // width

    def add(units, first):
        for block in range(pairs):
            cols = slice(block * width, (block + 1) * width)
            part = dot(dg_ref[0, :, :units], wg_ref[:units, cols])
            part += dot(du_ref[0, :, :units], wu_ref[:units, cols])
            acc[:, cols] = part if first else acc[:, cols] + part

    full = dg_ref.shape[2]

    @pl.when(step == 0)
    def _():
        add(full, True)

    @pl.when((step > 0) & ((step < last) | (tail == full)))
    def _():
        add(full, False)

    if tail != full:

        @pl.when((step > 0) & (step == last))
        def _():
            add(tail, False)

    @pl.when(step == last)
    def _():
        for block in range(pairs):
            cols = slice(block * width, (block + 1) * width)
            slot = (block // 2) ^ lax.rem(where_ref[0], pairs // 2)

            @pl.when(where_ref[1] == block % 2)
            def _(cols=cols, slot=slot):
                mine_ref[slot] = acc[:, cols]

            @pl.when(where_ref[1] != block % 2)
            def _(cols=cols, slot=slot):
                other_ref[slot] = acc[:, cols].astype(BF16)


def blocks_call(pos, side, count, dg, du, wg, wu, **links):
    tiles, tok, tile = dg.shape
    units, depth = wg.shape
    width = depth // (2 * count)
    split = count // 2
    tail = units - (tiles - 1) * tile
    where = jnp.stack([pos // 2, pos % 2]).astype(jnp.int32)
    part = pl.BlockSpec((1, tok, tile), lambda f, at: (f, 0, 0))
    half = depth // 2
    rows = pl.BlockSpec((tile, half), lambda f, at: (f, (at[0] // split) ^ side))
    return launch(
        functools.partial(blocks_kernel, width, tail),
        "blocks",
        (tiles,),
        [dg, du, wg, wu],
        [part, part, rows, rows],
        [whole((split, tok, width))] * 2,
        [shaped((split, tok, width), BF16), shaped((split, tok, width), F32)],
        places=[where],
        scratch=[pltpu.VMEM((tok, half), F32)],
        **links,
    )


def add_kernel(one_ref, two_ref, *outs):
    for slot, out in enumerate(outs):

        @pl.when(pl.program_id(0) == slot)
        def _(out=out):
            out[...] = (one_ref[0] + two_ref[0].astype(F32)).astype(BF16)


def add_call(one, two, **links):
    slots, tok, width = one.shape
    slot = pl.BlockSpec((1, tok, width), lambda s: (s, 0, 0))
    return launch(
        add_kernel,
        "add",
        (slots,),
        [one, two],
        [slot, slot],
        [whole((tok, width))] * slots,
        [shaped((tok, width), BF16)] * slots,
        vmem=SMALL,
        **links,
    )


def error_kernel(hid_ref, dy_ref, l_ref, r_ref, *refs):
    errs, out_ref = refs[:-1], refs[-1]
    width = errs[0].shape[2]
    for part, err_ref in enumerate(errs):
        at = slice(part * width, (part + 1) * width)
        grown = dot(hid_ref[...], dy_ref[:, at]) + err_ref[0].astype(F32)
        out_ref[0, :, at] = (grown - dot(l_ref[...], r_ref[:, at])).astype(BF16)


def error_call(hid, dy, err, l, r, **links):
    units, tok = hid.shape
    depth = dy.shape[1]
    tile = 352 if units > 512 else units
    return launch(
        error_kernel,
        "error",
        (pl.cdiv(units, tile),),
        [hid, dy, l, r] + [err] * STREAMS,
        [
            pl.BlockSpec((tile, tok), lambda f: (f, 0)),
            whole(dy.shape),
            pl.BlockSpec((tile, SPLIT), lambda f: (f, 0)),
            whole(r.shape),
            *error_streams(tile, depth),
        ],
        [pl.BlockSpec((1, tile, depth), lambda f: (0, f, 0))],
        [shaped(err.shape, BF16)],
        **links,
    )


def update_kernel(at_ref, mom_ref, all_ref, w_ref, l_ref, r_ref, mine_ref, mom_out, w_out):
    cols = mom_ref.shape[1]
    mom_out[...] = 0.9 * mom_ref[...] + dot(l_ref[...], mine_ref[...])
    for part in range(all_ref.shape[0]):
        at = slice(part * cols, (part + 1) * cols)
        mom = 0.9 * all_ref[part].astype(F32) + dot(l_ref[...], r_ref[:, at])
        w_out[:, at] = (w_ref[:, at].astype(F32) - 0.1 * mom).astype(BF16)


def update_call(at, mom, everyone, w, l, r, **links):
    units, cols = mom.shape
    depth = w.shape[1]
    tile = 176 if units > 512 else units
    rows = pl.BlockSpec((tile, depth), lambda f, at: (f, 0))
    mine = pl.BlockSpec((tile, cols), lambda f, at: (f, 0))
    parts = everyone.shape[0]
    return launch(
        update_kernel,
        "update",
        (pl.cdiv(units, tile),),
        [mom, everyone, w, l, r, r],
        [
            mine,
            pl.BlockSpec((parts, tile, cols), lambda f, at: (0, f, 0)),
            rows,
            pl.BlockSpec((tile, SPLIT), lambda f, at: (f, 0)),
            whole(r.shape),
            pl.BlockSpec((SPLIT, cols), lambda f, at: (0, at[0])),
        ],
        [mine, rows],
        [shaped(mom.shape, F32), shaped(w.shape, BF16)],
        places=[at],
        vmem=LARGE,
        **links,
    )


def exchange(value, axis, mask):
    size = lax.axis_size(axis)
    return lax.ppermute(value, axis, [(i, i ^ mask) for i in range(size)])


def masks(size):
    return [1 << bit for bit in range(size.bit_length() - 1)]


def body(inputs, out_grads, w_gate, w_up, w_down, err_down, mom_down, q_down):
    replicas = lax.axis_size("dp")
    shards = lax.axis_size("mp")
    rank_dp = lax.axis_index("dp")
    rank_mp = lax.axis_index("mp")
    w_gate, w_up, q_t = w_gate.T, w_up.T, q_down.T
    count = shards // 2

    (low,) = cast_call(mom_down)
    everyone = lax.all_gather(low, "dp")

    hid, d_gate, d_up, dyq = hidden_call(
        inputs, out_grads, w_gate, w_up, w_down, q_t, held=[low]
    )
    (left,) = left_call(q_t, dyq, err_down, hid, replicas)
    lefts = [left] + [exchange(left, "dp", mask) for mask in range(1, replicas)]

    def blocks(side, **links):
        return blocks_call(rank_mp, side, count, d_gate, d_up, w_gate, w_up, **links)

    other, first = blocks(0, held=[left])
    total, left, other = right_call(lefts, hid, err_down, out_grads, through=[other])

    others = [exchange(other, "mp", 1)]
    steps = masks(shards)
    for index, mask in enumerate(steps):
        more = exchange(total, "mp", mask)
        held, through = [], []
        if index == 0:
            other, second = blocks(1, held=[total])
            others.append(exchange(other, "mp", 1))
            held = [other]
        elif index == 1:
            mine = list(add_call(first, others[0], held=[total]))
            held = [mine[0]]
        elif index == 2:
            mine += list(add_call(second, others[1], held=[total]))
            held = [mine[-1]]
        if index == len(steps) - 1:
            through = mine
        total, *mine_now = sum_call(total, more, held=held, through=through)
        if through:
            mine = mine_now
    landed = [exchange(mine[slot], "mp", 2 * slot) for slot in range(1, count)]
    for mask in masks(replicas):
        (total,) = sum_call(total, exchange(total, "dp", mask))

    l, r = factors_call(total, left, replicas)
    (next_err,) = error_call(hid, out_grads, err_down, l, r)
    at = jnp.reshape(rank_dp, (1,)).astype(jnp.int32)
    next_mom, new = update_call(at, mom_down, everyone, w_down, l, r, held=[next_err])
    (in_grads,) = join_call([mine[0]] + landed, held=[next_mom])
    return (in_grads, new, next_err, next_mom)


def solution(mesh):
    in_specs = (
        P("dp", None),
        P("dp", None),
        P(None, "mp"),
        P(None, "mp"),
        P("mp", None),
        P("dp", "mp", None),
        P("mp", "dp"),
        P(),
    )
    out_specs = (P("dp", "mp"), P("mp", None), P("dp", "mp", None), P("mp", "dp"))
    return jax.shard_map(body, mesh=mesh, in_specs=in_specs, out_specs=out_specs, check_vma=False)
```

```python
import functools

import jax
import jax.numpy as jnp
from jax import lax
from jax.experimental import pallas as pl
from jax.experimental.pallas import tpu as pltpu
from jax.sharding import PartitionSpec as P

R = 8
SPLIT = 4 * R
EPS = 1e-06
F32 = jnp.float32
BF16 = jnp.bfloat16
HIGH = lax.Precision.HIGHEST
VMEM = 48 * 2**20
SMALL = 12 * 2**20
LARGE = 62 * 2**20
ONCE = pl.Buffered(1)
STREAMS = 4
HELD = pl.BlockSpec(memory_space=pl.ANY)


def launch(kernel, name, grid, args, in_specs, out_specs, out_shape, *, places=(), held=(),
           through=(), scratch=(), vmem=VMEM, aliases=None):
    n_in, n_out = len(args), len(out_shape)
    n_held, n_through, n_place = len(held), len(through), len(places)
    first = n_place + n_in

    def inner(*refs):
        outs = first + n_held + n_through
        kernel(*refs[:first], *refs[outs : outs + n_out], *refs[outs + n_out + n_through :])

    links = {first + n_held + i: n_out + i for i in range(n_through)}
    return pl.pallas_call(
        inner,
        grid_spec=pltpu.PrefetchScalarGridSpec(
            num_scalar_prefetch=n_place,
            grid=grid,
            in_specs=list(in_specs) + [HELD] * (n_held + n_through),
            out_specs=list(out_specs) + [HELD] * n_through,
            scratch_shapes=list(scratch),
        ),
        out_shape=list(out_shape)
        + [jax.ShapeDtypeStruct(array.shape, array.dtype) for array in through],
        input_output_aliases={**links, **(aliases or {})},
        compiler_params=pltpu.CompilerParams(vmem_limit_bytes=vmem),
        cost_estimate=pl.CostEstimate(flops=1, bytes_accessed=1, transcendentals=0),
        name=name,
    )(*places, *args, *held, *through)


def shaped(shape, dtype):
    return jax.ShapeDtypeStruct(shape, dtype)


def dot(left, right):
    return jnp.dot(left, right, preferred_element_type=F32)


def dot_nt(left, right):
    return lax.dot_general(left, right, (((1,), (1,)), ((), ())), preferred_element_type=F32)


def terms(rows):
    hi = rows.astype(BF16).astype(F32)
    rest = rows - hi
    mid = rest.astype(BF16).astype(F32)
    return hi, mid, rest - mid


def spread(rows):
    hi, mid, low = terms(rows)
    return jnp.concatenate([hi, mid, low, jnp.zeros_like(hi)], axis=0).astype(BF16)


def gather_terms(rows):
    return rows[:R] + rows[R : 2 * R] + rows[2 * R : 3 * R]


def tree(parts):
    while len(parts) > 1:
        odd = parts[len(parts) // 2 * 2 :]
        parts = [left + right for left, right in zip(parts[::2], parts[1::2])] + odd
    return parts[0]


def whole(shape):
    return pl.BlockSpec(shape, lambda *_: (0,) * len(shape), pipeline_mode=ONCE)


def unit_tile(units):
    return 256 if units > 512 and units % 16 == 0 else units


def cast_kernel(mom_ref, *outs):
    half = mom_ref.shape[1] // 2
    low, high = mom_ref[:, :half].astype(BF16), mom_ref[:, half:].astype(BF16)
    for out, part in zip(outs, (low, high, low, high)):
        out[...] = part


def cast_call(mom, **links):
    units, cols = mom.shape
    tile = units // 2 if units % 32 == 0 and units > 512 else units
    part = pl.BlockSpec((tile, cols // 2), lambda f: (f, 0))
    return launch(
        cast_kernel,
        "cast",
        (units // tile,),
        [mom],
        [pl.BlockSpec((tile, cols), lambda f: (f, 0))],
        [part] * 4,
        [shaped((units, cols // 2), BF16)] * 4,
        **links,
    )


def hidden_kernel(
    x_ref, wg_ref, wu_ref, wd_ref, q_ref, dy_any, hid_ref, dg_ref, du_ref, dyq_ref, dy_ref, sem
):
    fetch = pltpu.make_async_copy(dy_any, dy_ref, sem)

    @pl.when(pl.program_id(0) == 0)
    def _():
        fetch.start()

    gate = dot_nt(x_ref[...], wg_ref[...])
    up = dot_nt(x_ref[...], wu_ref[...])

    @pl.when(pl.program_id(0) == 0)
    def _():
        fetch.wait()
        dyq_ref[...] = gather_terms(dot_nt(dy_ref[...], spread(q_ref[...])).T)

    dh = dot_nt(dy_ref[...], wd_ref[...])
    sig = jax.nn.sigmoid(gate)
    silu = gate * sig
    hid_ref[...] = (silu * up).T.astype(BF16)
    dg_ref[...] = (dh * up * sig * (1.0 + gate * (1.0 - sig))).astype(BF16)
    du_ref[...] = (dh * silu).astype(BF16)


def hidden_call(x, dy, wg, wu, wd, q_t, **links):
    tok, depth = x.shape
    units = wg.shape[0]
    tile = unit_tile(units)
    rows = pl.BlockSpec((tile, depth), lambda f: (f, 0))
    part = pl.BlockSpec((tok, tile), lambda f: (0, f))
    return launch(
        hidden_kernel,
        "hidden",
        (pl.cdiv(units, tile),),
        [x, wg, wu, wd, q_t, dy],
        [whole((tok, depth)), rows, rows, rows, whole(q_t.shape), HELD],
        [pl.BlockSpec((tile, tok), lambda f: (f, 0)), part, part, whole((R, tok))],
        [
            shaped((units, tok), BF16),
            shaped((tok, units), BF16),
            shaped((tok, units), BF16),
            shaped((R, tok), F32),
        ],
        scratch=[pltpu.VMEM((tok, depth), BF16), pltpu.SemaphoreType.DMA(())],
        **links,
    )


def left_kernel(replicas, q_ref, dyq_ref, hid_ref, *refs):
    errs, (out_ref, q_terms, dyq_terms) = refs[:-3], refs[-3:]
    width = errs[0].shape[2]

    @pl.when(pl.program_id(0) == 0)
    def _():
        q_terms[...] = spread(q_ref[...])
        dyq_terms[...] = spread(dyq_ref[...])

    both = dot_nt(hid_ref[...], dyq_terms[...])
    for at, err_ref in enumerate(errs):
        both += dot_nt(err_ref[0], q_terms[:, at * width : (at + 1) * width])
    out_ref[...] = gather_terms(both.T) / replicas


def error_streams(tile, depth):
    shape = (1, tile, depth // STREAMS)
    return [pl.BlockSpec(shape, lambda f, c=c: (0, f, c)) for c in range(STREAMS)]


def left_call(q_t, dyq, err, hid, replicas, **links):
    units, tok = hid.shape
    depth = q_t.shape[1]
    tile = unit_tile(units)
    return launch(
        functools.partial(left_kernel, replicas),
        "left",
        (pl.cdiv(units, tile),),
        [q_t, dyq, hid] + [err] * STREAMS,
        [whole(q_t.shape), whole(dyq.shape), pl.BlockSpec((tile, tok), lambda f: (f, 0))]
        + error_streams(tile, depth),
        [pl.BlockSpec((R, tile), lambda f: (0, f))],
        [shaped((R, units), F32)],
        scratch=[pltpu.VMEM((SPLIT, depth), BF16), pltpu.VMEM((SPLIT, tok), BF16)],
        **links,
    )


def columns(ref, step, tile):
    if ref.shape[1] == tile:
        return ref[...]
    return ref[:, pl.ds(pl.multiple_of(step * tile, tile), tile)]


def right_kernel(parts, dy_steps, *refs):
    lefts = refs[:parts]
    errs, (hid_ref, dy_ref, out_ref, left_ref, left_terms, mixed_terms, total) = (
        refs[parts:-7],
        refs[-7:],
    )
    step = pl.program_id(0)
    units = left_ref.shape[1]
    tile, width = errs[0].shape[1:]
    depth = width * len(errs)
    dy_tile = dy_ref.shape[0]
    tail = units % tile
    last = pl.num_programs(0) - 1

    @pl.when(step == 0)
    def _():
        left = tree([ref[...] for ref in lefts])
        left_ref[...] = left
        left_terms[:, :units] = spread(left)
        mixed_terms[...] = spread(gather_terms(dot(left_terms[:, :units], hid_ref[...])))
        gram = lax.dot_general(
            left, left, (((1,), (1,)), ((), ())), precision=HIGH, preferred_element_type=F32
        )
        out_ref[:, depth:] = jnp.concatenate([gram, jnp.zeros((R, 128 - R), F32)], axis=1)
        total[...] = jnp.zeros_like(total)

    @pl.when(step < dy_steps)
    def _():
        total[...] += dot(columns(mixed_terms, step, dy_tile), dy_ref[...])

    if tail:

        @pl.when(step < last)
        def _():
            left = columns(left_terms, step, tile)
            for at, err_ref in enumerate(errs):
                total[:, at * width : (at + 1) * width] += dot(left, err_ref[0])

        @pl.when(step == last)
        def _():
            left = left_terms[:, units - tail : units]
            for at, err_ref in enumerate(errs):
                total[:, at * width : (at + 1) * width] += dot(left, err_ref[0, :tail])

    else:
        left = columns(left_terms, step, tile)
        for at, err_ref in enumerate(errs):
            total[:, at * width : (at + 1) * width] += dot(left, err_ref[0])

    @pl.when(step == last)
    def _():
        out_ref[:, :depth] = gather_terms(total[...])


def right_call(lefts, hid, err, dy, **links):
    units, tok = hid.shape
    depth = dy.shape[1]
    tile = unit_tile(units)
    tiles = pl.cdiv(units, tile)
    dy_steps = 2 if tiles > 1 else 1
    return launch(
        functools.partial(right_kernel, len(lefts), dy_steps),
        "right",
        (tiles,),
        [*lefts] + [err] * STREAMS + [hid, dy],
        [whole((R, units))] * len(lefts)
        + error_streams(tile, depth)
        + [
            whole((units, tok)),
            pl.BlockSpec((tok // dy_steps, depth), lambda f: (jnp.minimum(f, dy_steps - 1), 0)),
        ],
        [whole((R, depth + 128)), whole((R, units))],
        [shaped((R, depth + 128), F32), shaped((R, units), F32)],
        scratch=[
            pltpu.VMEM((SPLIT, tiles * tile), BF16),
            pltpu.VMEM((SPLIT, tok), BF16),
            pltpu.VMEM((SPLIT, depth), F32),
        ],
        **links,
    )


def sum_kernel(one_ref, two_ref, out_ref):
    out_ref[...] = one_ref[...] + two_ref[...]


def sum_call(one, two, **links):
    return launch(
        sum_kernel,
        "sum",
        (1,),
        [one, two],
        [whole(one.shape)] * 2,
        [whole(one.shape)],
        [shaped(one.shape, one.dtype)],
        vmem=SMALL,
        **links,
    )


def join_kernel(*refs):
    refs[-1][...] = tree([ref[...].astype(F32) for ref in refs[:-1]]).astype(BF16)


def join_call(parts, **links):
    shape = parts[0].shape
    return launch(
        join_kernel,
        "join",
        (1,),
        parts,
        [whole(shape)] * len(parts),
        [whole(shape)],
        [shaped(shape, BF16)],
        vmem=SMALL,
        **links,
    )


def factors_kernel(replicas, sum_ref, left_ref, l_ref, r_ref):
    depth = r_ref.shape[1]
    gram = sum_ref[:, depth : depth + R] / replicas
    row = lax.broadcasted_iota(jnp.int32, (R, R), 0)
    col = lax.broadcasted_iota(jnp.int32, (R, R), 1)
    eye = (row == col).astype(F32)
    basis = jnp.zeros((R, R), F32)
    for k in range(R):
        unit = eye[k : k + 1]
        coeffs = jnp.sum(basis * gram[k : k + 1], axis=1, keepdims=True)
        rest = unit - jnp.sum(coeffs * basis, axis=0, keepdims=True)
        rest_col = jnp.sum(eye * rest, axis=1, keepdims=True)
        image = jnp.sum(rest_col * gram, axis=0, keepdims=True)
        square = jnp.sum(image * rest, axis=1, keepdims=True)
        basis = jnp.where(row == k, rest * lax.rsqrt(jnp.maximum(square, 0.0) + EPS), basis)
    left = jnp.dot(basis, left_ref[...], precision=HIGH, preferred_element_type=F32)
    right = jnp.dot(basis, sum_ref[:, :depth], precision=HIGH, preferred_element_type=F32)
    hi, mid, _ = terms(left)
    zero = jnp.zeros_like(hi)
    l_ref[...] = jnp.concatenate([hi, hi, mid, zero], axis=0).T.astype(BF16)
    hi, mid, _ = terms(right / replicas)
    zero = jnp.zeros_like(hi)
    r_ref[...] = jnp.concatenate([hi, mid, hi, zero], axis=0).astype(BF16)


def factors_call(total, left, replicas, **links):
    units = left.shape[1]
    depth = total.shape[1] - 128
    return launch(
        functools.partial(factors_kernel, replicas),
        "factors",
        (1,),
        [total, left],
        [whole(total.shape), whole(left.shape)],
        [whole((units, SPLIT)), whole((SPLIT, depth))],
        [shaped((units, SPLIT), BF16), shaped((SPLIT, depth), BF16)],
        vmem=LARGE,
        **links,
    )


def other_kernel(where_ref, dg_ref, du_ref, wg_ref, wu_ref, out_ref):
    out_ref[0] = (dot(dg_ref[...], wg_ref[...]) + dot(du_ref[...], wu_ref[...])).astype(BF16)


def mine_kernel(where_ref, dg_ref, du_ref, wg_ref, wu_ref, add_ref, *outs):
    part = dot(dg_ref[...], wg_ref[...]) + dot(du_ref[...], wu_ref[...])
    part = (part + add_ref[0].astype(F32)).astype(BF16)
    for slot, out in enumerate(outs):

        @pl.when(pl.program_id(0) == slot)
        def _(out=out):
            out[...] = part


def blocks_call(pos, parity, slots, count, dg, du, wg, wu, add=None, **links):
    tok, units = dg.shape
    depth = wg.shape[1]
    width = depth // (2 * count)
    where = jnp.stack([pos // 2, parity]).astype(jnp.int32)
    first, steps = slots
    block = pl.BlockSpec((units, width), lambda s, at: (0, 2 * ((s + first) ^ at[0]) + at[1]))
    slot = pl.BlockSpec((1, tok, width), lambda s, at: (s, 0, 0))
    in_specs = [whole((tok, units)), whole((tok, units)), block, block]
    args = [dg, du, wg, wu]
    if add is None:
        kernel = other_kernel
        out_specs = [slot]
        out_shape = [shaped((steps, tok, width), BF16)]
    else:
        kernel = mine_kernel
        in_specs.append(slot)
        args.append(add)
        out_specs = [whole((tok, width))] * steps
        out_shape = [shaped((tok, width), BF16)] * steps
    return launch(
        kernel, "blocks", (steps,), args, in_specs, out_specs, out_shape, places=[where], **links
    )


def error_kernel(hid_ref, dy_ref, l_ref, r_ref, *refs):
    errs, out_ref = refs[:-1], refs[-1]
    width = errs[0].shape[2]
    for part, err_ref in enumerate(errs):
        at = slice(part * width, (part + 1) * width)
        grown = dot(hid_ref[...], dy_ref[:, at]) + err_ref[0].astype(F32)
        out_ref[0, :, at] = (grown - dot(l_ref[...], r_ref[:, at])).astype(BF16)


def error_call(hid, dy, err, l, r, **links):
    units, tok = hid.shape
    depth = dy.shape[1]
    tile = 352 if units > 512 else units
    return launch(
        error_kernel,
        "error",
        (pl.cdiv(units, tile),),
        [hid, dy, l, r] + [err] * STREAMS,
        [
            pl.BlockSpec((tile, tok), lambda f: (f, 0)),
            whole(dy.shape),
            pl.BlockSpec((tile, SPLIT), lambda f: (f, 0)),
            whole(r.shape),
            *error_streams(tile, depth),
        ],
        [pl.BlockSpec((1, tile, depth), lambda f: (0, f, 0))],
        [shaped(err.shape, BF16)],
        **links,
    )


def updated(w, mom, approx):
    return (w.astype(F32) - 0.1 * (0.9 * mom.astype(F32) + approx)).astype(BF16)


def update_kernel(own, at_ref, mom_ref, l_ref, r_ref, w_ref, *refs):
    pieces, (mom_out, w_out) = refs[:-2], refs[-2:]
    step = pl.program_id(0)

    @pl.when(step < own)
    def _():
        approx = dot(l_ref[...], r_ref[...])
        mom = mom_ref[...]
        mom_out[...] = 0.9 * mom + approx
        w_out[...] = updated(w_ref[...], mom.astype(BF16), approx)

    for slot, piece in enumerate(pieces):

        @pl.when(step == own + slot)
        def _(piece=piece):
            w_out[...] = updated(w_ref[...], piece[...], dot(l_ref[...], r_ref[...]))


def update_call(at, mom, pieces, w, l, r, **links):
    units, cols = mom.shape
    half = pieces[0].shape[1]
    own = cols // half
    tile = units // 2 if units % 32 == 0 and units > 512 else units
    tiles = units // tile

    def during(low, high, column):
        def index(c, f, at):
            row = jnp.where(c < low, 0, jnp.where(c > high, tiles - 1, f))
            return row, column(jnp.clip(c, low, high))

        return pl.BlockSpec((tile, half), index)

    momenta = during(0, own - 1, lambda c: c)
    weights = pl.BlockSpec((tile, half), lambda c, f, at: (f, at[c]))
    return launch(
        functools.partial(update_kernel, own),
        "update",
        (own + len(pieces), tiles),
        [mom, l, r, w, *pieces],
        [
            momenta,
            pl.BlockSpec((tile, SPLIT), lambda c, f, at: (f, 0)),
            pl.BlockSpec((SPLIT, half), lambda c, f, at: (0, at[c])),
            weights,
            *[during(own + s, own + s, lambda c: 0) for s in range(len(pieces))],
        ],
        [momenta, weights],
        [shaped(mom.shape, F32), shaped(w.shape, BF16)],
        places=[at],
        **links,
    )


def last_kernel(at_ref, low_ref, high_ref, w_ref, l_ref, r_ref, _, w_out):
    half = low_ref.shape[1]
    approx = dot(l_ref[...], r_ref[...])
    w_out[:, :half] = updated(w_ref[:, :half], low_ref[...], approx[:, :half])
    w_out[:, half:] = updated(w_ref[:, half:], high_ref[...], approx[:, half:])


def last_call(at, low, high, w, l, r, new, **links):
    units, half = low.shape
    tile = 352 if units > 512 else units
    part = pl.BlockSpec((tile, half), lambda f, at: (f, 0))
    place = pl.BlockSpec((tile, 2 * half), lambda f, at: (f, at[0]))
    return launch(
        last_kernel,
        "last",
        (pl.cdiv(units, tile),),
        [low, high, w, l, r, new],
        [
            part,
            part,
            place,
            pl.BlockSpec((tile, SPLIT), lambda f, at: (f, 0)),
            pl.BlockSpec((SPLIT, 2 * half), lambda f, at: (0, at[0])),
            HELD,
        ],
        [place],
        [shaped(w.shape, BF16)],
        places=[at],
        aliases={6: 0},
        **links,
    )


def exchange(value, axis, mask):
    size = lax.axis_size(axis)
    return lax.ppermute(value, axis, [(i, i ^ mask) for i in range(size)])


def arrived(one, two):
    return one[:16, :128] + two[:16, :128]


def masks(size):
    return [1 << bit for bit in range(size.bit_length() - 1)]


def body(inputs, out_grads, w_gate, w_up, w_down, err_down, mom_down, q_down):
    replicas = lax.axis_size("dp")
    shards = lax.axis_size("mp")
    rank_dp = lax.axis_index("dp")
    rank_mp = lax.axis_index("mp")
    w_gate, w_up, q_t = w_gate.T, w_up.T, q_down.T
    count = shards // 2
    split = max(1, count // 2)
    early, late = (0, split), (split, count - split)

    low, high, later_low, later_high = cast_call(mom_down)
    got = {(2, 0): exchange(low, "dp", 2), (1, 1): exchange(high, "dp", 1)}

    hid, d_gate, d_up, dyq = hidden_call(
        inputs, out_grads, w_gate, w_up, w_down, q_t, held=[low]
    )
    (left,) = left_call(q_t, dyq, err_down, hid, replicas)
    lefts = [left] + [exchange(left, "dp", mask) for mask in range(1, replicas)]

    here, there = rank_mp % 2, 1 - rank_mp % 2
    others, mine = [], []

    def blocks(turn, order, held=()):
        parity, slots = (there, here)[turn // 2], (early, late)[turn % 2]
        if slots[1] == 0:
            return order
        add = others[turn % 2] if turn > 1 else None
        *outs, order = blocks_call(
            rank_mp, parity, slots, count, d_gate, d_up, w_gate, w_up, add, held=held, through=[order]
        )
        (mine if turn > 1 else others).extend(outs)
        return order

    def send_other(through):
        if through:
            others[-1] = exchange(through[0], "mp", 1)

    order = blocks(0, dyq, [left, arrived(got[2, 0], got[1, 1])])
    total, left, order, later_low, later_high, *fresh = right_call(
        lefts,
        hid,
        err_down,
        out_grads,
        through=[order, later_low, later_high, others[0]],
    )
    send_other(fresh)
    got[1, 0] = exchange(later_low, "dp", 1)
    got[2, 1] = exchange(later_high, "dp", 2)

    rounds = [("mp", mask) for mask in masks(shards)] + [("dp", mask) for mask in masks(replicas)]
    for index, (axis, mask) in enumerate(rounds):
        more = exchange(total, axis, mask)
        if index < 3:
            order = blocks(index + 1, order, [total])
        through = others[1:] if index == 0 else []
        held = [arrived(got[1, 0], got[2, 1])] if index == 2 else []
        total, order, *fresh = sum_call(total, more, held=held, through=[order, *through])
        send_other(fresh)
    l, r, got[2, 0], got[1, 1] = factors_call(
        total, left, replicas, through=[got[2, 0], got[1, 1]]
    )
    got[3, 0] = exchange(got[2, 0], "dp", 1)
    got[3, 1] = exchange(got[1, 1], "dp", 2)
    landed = [exchange(mine[slot], "mp", 2 * slot) for slot in range(1, count)]

    (next_err,) = error_call(hid, out_grads, err_down, l, r)
    keys = [(1, 0), (1, 1), (2, 0), (2, 1)]
    at = jnp.stack([2 * (rank_dp ^ mask) + side for mask, side in [(0, 0), (0, 1)] + keys])
    next_mom, new, order = update_call(
        at.astype(jnp.int32),
        mom_down,
        [got[key] for key in keys],
        w_down,
        l,
        r,
        held=[next_err],
        through=[order],
    )
    far = jnp.reshape(rank_dp ^ 3, (1,)).astype(jnp.int32)
    new, order = last_call(far, got[3, 0], got[3, 1], w_down, l, r, new, through=[order])
    (in_grads,) = join_call([mine[0]] + landed, held=[order])
    return (in_grads, new, next_err, next_mom)


def solution(mesh):
    in_specs = (
        P("dp", None),
        P("dp", None),
        P(None, "mp"),
        P(None, "mp"),
        P("mp", None),
        P("dp", "mp", None),
        P("mp", "dp"),
        P(),
    )
    out_specs = (P("dp", "mp"), P("mp", None), P("dp", "mp", None), P("mp", "dp"))
    return jax.shard_map(body, mesh=mesh, in_specs=in_specs, out_specs=out_specs, check_vma=False)
```

```python
import functools

import jax
import jax.numpy as jnp
from jax import lax
from jax.experimental import pallas as pl
from jax.experimental.pallas import tpu as pltpu
from jax.sharding import PartitionSpec as P

R = 8
SPLIT = 4 * R
EPS = 1e-06
F32 = jnp.float32
BF16 = jnp.bfloat16
HIGH = lax.Precision.HIGHEST
VMEM = 48 * 2**20
SMALL = 12 * 2**20
LARGE = 62 * 2**20
ONCE = pl.Buffered(1)
STREAMS = 4
MEDIUM = 48 * 2**20
HELD = pl.BlockSpec(memory_space=pl.ANY)


def launch(kernel, name, grid, args, in_specs, out_specs, out_shape, *, places=(), held=(),
           through=(), scratch=(), vmem=VMEM, aliases=None):
    n_in, n_out = len(args), len(out_shape)
    n_held, n_through, n_place = len(held), len(through), len(places)
    first = n_place + n_in

    def inner(*refs):
        outs = first + n_held + n_through
        kernel(*refs[:first], *refs[outs : outs + n_out], *refs[outs + n_out + n_through :])

    links = {first + n_held + i: n_out + i for i in range(n_through)}
    return pl.pallas_call(
        inner,
        grid_spec=pltpu.PrefetchScalarGridSpec(
            num_scalar_prefetch=n_place,
            grid=grid,
            in_specs=list(in_specs) + [HELD] * (n_held + n_through),
            out_specs=list(out_specs) + [HELD] * n_through,
            scratch_shapes=list(scratch),
        ),
        out_shape=list(out_shape)
        + [jax.ShapeDtypeStruct(array.shape, array.dtype) for array in through],
        input_output_aliases={**links, **(aliases or {})},
        compiler_params=pltpu.CompilerParams(vmem_limit_bytes=vmem),
        cost_estimate=pl.CostEstimate(flops=1, bytes_accessed=1, transcendentals=0),
        name=name,
    )(*places, *args, *held, *through)


def shaped(shape, dtype):
    return jax.ShapeDtypeStruct(shape, dtype)


def dot(left, right):
    return jnp.dot(left, right, preferred_element_type=F32)


def dot_nt(left, right):
    return lax.dot_general(left, right, (((1,), (1,)), ((), ())), preferred_element_type=F32)


def terms(rows):
    hi = rows.astype(BF16).astype(F32)
    rest = rows - hi
    mid = rest.astype(BF16).astype(F32)
    return hi, mid, rest - mid


def spread(rows):
    hi, mid, low = terms(rows)
    return jnp.concatenate([hi, mid, low, jnp.zeros_like(hi)], axis=0).astype(BF16)


def gather_terms(rows):
    return rows[:R] + rows[R : 2 * R] + rows[2 * R : 3 * R]


def tree(parts):
    while len(parts) > 1:
        odd = parts[len(parts) // 2 * 2 :]
        parts = [left + right for left, right in zip(parts[::2], parts[1::2])] + odd
    return parts[0]


def whole(shape):
    return pl.BlockSpec(shape, lambda *_: (0,) * len(shape), pipeline_mode=ONCE)


def unit_tile(units):
    return 256 if units > 512 and units % 16 == 0 else units


def cast_kernel(mom_ref, *outs):
    half = mom_ref.shape[1] // 2
    low, high = mom_ref[:, :half].astype(BF16), mom_ref[:, half:].astype(BF16)
    for out, part in zip(outs, (low, high, low, high)):
        out[...] = part


def cast_call(mom, **links):
    units, cols = mom.shape
    tile = units // 2 if units % 32 == 0 and units > 512 else units
    part = pl.BlockSpec((tile, cols // 2), lambda f: (f, 0))
    return launch(
        cast_kernel,
        "cast",
        (units // tile,),
        [mom],
        [pl.BlockSpec((tile, cols), lambda f: (f, 0))],
        [part] * 4,
        [shaped((units, cols // 2), BF16)] * 4,
        vmem=MEDIUM,
        **links,
    )


def hidden_kernel(
    replicas,
    x_ref, wg_ref, wu_ref, wd_ref, err_ref, q_ref, dy_any,
    hid_ref, dg_ref, du_ref, left_ref, dyq_ref,
    dy_ref, q_terms, dyq_terms, sem,
):
    fetch = pltpu.make_async_copy(dy_any, dy_ref, sem)

    @pl.when(pl.program_id(0) == 0)
    def _():
        fetch.start()
        q_terms[...] = spread(q_ref[...])

    gate = dot_nt(x_ref[...], wg_ref[...])
    up = dot_nt(x_ref[...], wu_ref[...])
    both = dot_nt(err_ref[0], q_terms[...])

    @pl.when(pl.program_id(0) == 0)
    def _():
        fetch.wait()
        dyq = gather_terms(dot_nt(dy_ref[...], q_terms[...]).T)
        dyq_ref[...] = dyq
        dyq_terms[...] = spread(dyq)

    dh = dot_nt(dy_ref[...], wd_ref[...])
    sig = jax.nn.sigmoid(gate)
    silu = gate * sig
    hid = (silu * up).T.astype(BF16)
    hid_ref[...] = hid
    dg_ref[...] = (dh * up * sig * (1.0 + gate * (1.0 - sig))).astype(BF16)
    du_ref[...] = (dh * silu).astype(BF16)
    both += dot_nt(hid, dyq_terms[...])
    left_ref[...] = gather_terms(both.T) / replicas


def hidden_call(x, dy, wg, wu, wd, err, q_t, replicas, **links):
    tok, depth = x.shape
    units = wg.shape[0]
    tile = unit_tile(units)
    rows = pl.BlockSpec((tile, depth), lambda f: (f, 0))
    part = pl.BlockSpec((tok, tile), lambda f: (0, f))
    return launch(
        functools.partial(hidden_kernel, replicas),
        "hidden",
        (pl.cdiv(units, tile),),
        [x, wg, wu, wd, err, q_t, dy],
        [
            whole((tok, depth)),
            rows,
            rows,
            rows,
            pl.BlockSpec((1, tile, depth), lambda f: (0, f, 0)),
            whole(q_t.shape),
            HELD,
        ],
        [
            pl.BlockSpec((tile, tok), lambda f: (f, 0)),
            part,
            part,
            pl.BlockSpec((R, tile), lambda f: (0, f)),
            whole((R, tok)),
        ],
        [
            shaped((units, tok), BF16),
            shaped((tok, units), BF16),
            shaped((tok, units), BF16),
            shaped((R, units), F32),
            shaped((R, tok), F32),
        ],
        scratch=[
            pltpu.VMEM((tok, depth), BF16),
            pltpu.VMEM((SPLIT, depth), BF16),
            pltpu.VMEM((SPLIT, tok), BF16),
            pltpu.SemaphoreType.DMA(()),
        ],
        **links,
    )


def error_streams(tile, depth):
    shape = (1, tile, depth // STREAMS)
    return [pl.BlockSpec(shape, lambda f, c=c: (0, f, c)) for c in range(STREAMS)]


def columns(ref, step, tile):
    if ref.shape[1] == tile:
        return ref[...]
    return ref[:, pl.ds(pl.multiple_of(step * tile, tile), tile)]


def right_kernel(parts, dy_steps, *refs):
    lefts = refs[:parts]
    errs, (hid_ref, dy_ref, out_ref, left_ref, left_terms, mixed_terms, total) = (
        refs[parts:-7],
        refs[-7:],
    )
    step = pl.program_id(0)
    units = left_ref.shape[1]
    tile, width = errs[0].shape[1:]
    depth = width * len(errs)
    dy_tile = dy_ref.shape[0]
    tail = units % tile
    last = pl.num_programs(0) - 1

    @pl.when(step == 0)
    def _():
        left = tree([ref[...] for ref in lefts])
        left_ref[...] = left
        left_terms[:, :units] = spread(left)
        mixed_terms[...] = spread(gather_terms(dot(left_terms[:, :units], hid_ref[...])))
        gram = lax.dot_general(
            left, left, (((1,), (1,)), ((), ())), precision=HIGH, preferred_element_type=F32
        )
        out_ref[:, depth:] = jnp.concatenate([gram, jnp.zeros((R, 128 - R), F32)], axis=1)
        total[...] = jnp.zeros_like(total)

    @pl.when(step < dy_steps)
    def _():
        total[...] += dot(columns(mixed_terms, step, dy_tile), dy_ref[...])

    if tail:

        @pl.when(step < last)
        def _():
            left = columns(left_terms, step, tile)
            for at, err_ref in enumerate(errs):
                total[:, at * width : (at + 1) * width] += dot(left, err_ref[0])

        @pl.when(step == last)
        def _():
            left = left_terms[:, units - tail : units]
            for at, err_ref in enumerate(errs):
                total[:, at * width : (at + 1) * width] += dot(left, err_ref[0, :tail])

    else:
        left = columns(left_terms, step, tile)
        for at, err_ref in enumerate(errs):
            total[:, at * width : (at + 1) * width] += dot(left, err_ref[0])

    @pl.when(step == last)
    def _():
        out_ref[:, :depth] = gather_terms(total[...])


def right_call(lefts, hid, err, dy, **links):
    units, tok = hid.shape
    depth = dy.shape[1]
    tile = unit_tile(units)
    tiles = pl.cdiv(units, tile)
    dy_steps = 2 if tiles > 1 else 1
    return launch(
        functools.partial(right_kernel, len(lefts), dy_steps),
        "right",
        (tiles,),
        [*lefts] + [err] * STREAMS + [hid, dy],
        [whole((R, units))] * len(lefts)
        + error_streams(tile, depth)
        + [
            whole((units, tok)),
            pl.BlockSpec((tok // dy_steps, depth), lambda f: (jnp.minimum(f, dy_steps - 1), 0)),
        ],
        [whole((R, depth + 128)), whole((R, units))],
        [shaped((R, depth + 128), F32), shaped((R, units), F32)],
        scratch=[
            pltpu.VMEM((SPLIT, tiles * tile), BF16),
            pltpu.VMEM((SPLIT, tok), BF16),
            pltpu.VMEM((SPLIT, depth), F32),
        ],
        vmem=MEDIUM,
        **links,
    )


def sum_kernel(one_ref, two_ref, out_ref):
    out_ref[...] = one_ref[...] + two_ref[...]


def sum_call(one, two, **links):
    return launch(
        sum_kernel,
        "sum",
        (1,),
        [one, two],
        [whole(one.shape)] * 2,
        [whole(one.shape)],
        [shaped(one.shape, one.dtype)],
        vmem=SMALL,
        **links,
    )


def join_kernel(*refs):
    refs[-1][...] = tree([ref[...].astype(F32) for ref in refs[:-1]]).astype(BF16)


def join_call(parts, **links):
    shape = parts[0].shape
    return launch(
        join_kernel,
        "join",
        (1,),
        parts,
        [whole(shape)] * len(parts),
        [whole(shape)],
        [shaped(shape, BF16)],
        vmem=SMALL,
        **links,
    )


def factors_kernel(replicas, sum_ref, left_ref, l_ref, r_ref):
    depth = r_ref.shape[1]
    gram = sum_ref[:, depth : depth + R] / replicas
    row = lax.broadcasted_iota(jnp.int32, (R, R), 0)
    col = lax.broadcasted_iota(jnp.int32, (R, R), 1)
    eye = (row == col).astype(F32)
    basis = jnp.zeros((R, R), F32)
    for k in range(R):
        unit = eye[k : k + 1]
        coeffs = jnp.sum(basis * gram[k : k + 1], axis=1, keepdims=True)
        rest = unit - jnp.sum(coeffs * basis, axis=0, keepdims=True)
        rest_col = jnp.sum(eye * rest, axis=1, keepdims=True)
        image = jnp.sum(rest_col * gram, axis=0, keepdims=True)
        square = jnp.sum(image * rest, axis=1, keepdims=True)
        basis = jnp.where(row == k, rest * lax.rsqrt(jnp.maximum(square, 0.0) + EPS), basis)
    left = jnp.dot(basis, left_ref[...], precision=HIGH, preferred_element_type=F32)
    right = jnp.dot(basis, sum_ref[:, :depth], precision=HIGH, preferred_element_type=F32)
    hi, mid, _ = terms(left)
    zero = jnp.zeros_like(hi)
    l_ref[...] = jnp.concatenate([hi, hi, mid, zero], axis=0).T.astype(BF16)
    hi, mid, _ = terms(right / replicas)
    zero = jnp.zeros_like(hi)
    r_ref[...] = jnp.concatenate([hi, mid, hi, zero], axis=0).astype(BF16)


def factors_call(total, left, replicas, **links):
    units = left.shape[1]
    depth = total.shape[1] - 128
    return launch(
        functools.partial(factors_kernel, replicas),
        "factors",
        (1,),
        [total, left],
        [whole(total.shape), whole(left.shape)],
        [whole((units, SPLIT)), whole((SPLIT, depth))],
        [shaped((units, SPLIT), BF16), shaped((SPLIT, depth), BF16)],
        vmem=LARGE,
        **links,
    )


def other_kernel(where_ref, dg_ref, du_ref, wg_ref, wu_ref, out_ref):
    out_ref[0] = (dot(dg_ref[...], wg_ref[...]) + dot(du_ref[...], wu_ref[...])).astype(BF16)


def mine_kernel(where_ref, dg_ref, du_ref, wg_ref, wu_ref, add_ref, *outs):
    part = dot(dg_ref[...], wg_ref[...]) + dot(du_ref[...], wu_ref[...])
    part = (part + add_ref[0].astype(F32)).astype(BF16)
    for slot, out in enumerate(outs):

        @pl.when(pl.program_id(0) == slot)
        def _(out=out):
            out[...] = part


def blocks_call(pos, parity, slots, count, dg, du, wg, wu, add=None, **links):
    tok, units = dg.shape
    depth = wg.shape[1]
    width = depth // (2 * count)
    where = jnp.stack([pos // 2, parity]).astype(jnp.int32)
    first, steps = slots
    block = pl.BlockSpec((units, width), lambda s, at: (0, 2 * ((s + first) ^ at[0]) + at[1]))
    slot = pl.BlockSpec((1, tok, width), lambda s, at: (s, 0, 0))
    in_specs = [whole((tok, units)), whole((tok, units)), block, block]
    args = [dg, du, wg, wu]
    if add is None:
        kernel = other_kernel
        out_specs = [slot]
        out_shape = [shaped((steps, tok, width), BF16)]
    else:
        kernel = mine_kernel
        in_specs.append(slot)
        args.append(add)
        out_specs = [whole((tok, width))] * steps
        out_shape = [shaped((tok, width), BF16)] * steps
    return launch(
        kernel, "blocks", (steps,), args, in_specs, out_specs, out_shape, places=[where], vmem=MEDIUM, **links
    )


def error_kernel(hid_ref, dy_ref, l_ref, r_ref, *refs):
    errs, out_ref = refs[:-1], refs[-1]
    width = errs[0].shape[2]
    for part, err_ref in enumerate(errs):
        at = slice(part * width, (part + 1) * width)
        grown = dot(hid_ref[...], dy_ref[:, at]) + err_ref[0].astype(F32)
        out_ref[0, :, at] = (grown - dot(l_ref[...], r_ref[:, at])).astype(BF16)


def error_call(hid, dy, err, l, r, **links):
    units, tok = hid.shape
    depth = dy.shape[1]
    tile = 352 if units > 512 else units
    return launch(
        error_kernel,
        "error",
        (pl.cdiv(units, tile),),
        [hid, dy, l, r] + [err] * STREAMS,
        [
            pl.BlockSpec((tile, tok), lambda f: (f, 0)),
            whole(dy.shape),
            pl.BlockSpec((tile, SPLIT), lambda f: (f, 0)),
            whole(r.shape),
            *error_streams(tile, depth),
        ],
        [pl.BlockSpec((1, tile, depth), lambda f: (0, f, 0))],
        [shaped(err.shape, BF16)],
        vmem=LARGE,
        **links,
    )


def updated(w, mom, approx):
    return (w.astype(F32) - 0.1 * (0.9 * mom.astype(F32) + approx)).astype(BF16)


def update_kernel(own, at_ref, mom_ref, l_ref, r_ref, w_ref, *refs):
    pieces, (mom_out, w_out) = refs[:-2], refs[-2:]
    step = pl.program_id(0)

    @pl.when(step < own)
    def _():
        approx = dot(l_ref[...], r_ref[...])
        mom = mom_ref[...]
        mom_out[...] = 0.9 * mom + approx
        w_out[...] = updated(w_ref[...], mom.astype(BF16), approx)

    for slot, piece in enumerate(pieces):

        @pl.when(step == own + slot)
        def _(piece=piece):
            w_out[...] = updated(w_ref[...], piece[...], dot(l_ref[...], r_ref[...]))


def update_call(at, mom, pieces, w, l, r, **links):
    units, cols = mom.shape
    half = pieces[0].shape[1]
    own = cols // half
    tile = units // 2 if units % 32 == 0 and units > 512 else units
    tiles = units // tile

    def during(low, high, column):
        def index(c, f, at):
            row = jnp.where(c < low, 0, jnp.where(c > high, tiles - 1, f))
            return row, column(jnp.clip(c, low, high))

        return pl.BlockSpec((tile, half), index)

    momenta = during(0, own - 1, lambda c: c)
    weights = pl.BlockSpec((tile, half), lambda c, f, at: (f, at[c]))
    return launch(
        functools.partial(update_kernel, own),
        "update",
        (own + len(pieces), tiles),
        [mom, l, r, w, *pieces],
        [
            momenta,
            pl.BlockSpec((tile, SPLIT), lambda c, f, at: (f, 0)),
            pl.BlockSpec((SPLIT, half), lambda c, f, at: (0, at[c])),
            weights,
            *[during(own + s, own + s, lambda c: 0) for s in range(len(pieces))],
        ],
        [momenta, weights],
        [shaped(mom.shape, F32), shaped(w.shape, BF16)],
        places=[at],
        vmem=LARGE,
        **links,
    )


def last_kernel(at_ref, low_ref, high_ref, w_ref, l_ref, r_ref, _, w_out):
    half = low_ref.shape[1]
    approx = dot(l_ref[...], r_ref[...])
    w_out[:, :half] = updated(w_ref[:, :half], low_ref[...], approx[:, :half])
    w_out[:, half:] = updated(w_ref[:, half:], high_ref[...], approx[:, half:])


def last_call(at, low, high, w, l, r, new, **links):
    units, half = low.shape
    tile = 352 if units > 512 else units
    part = pl.BlockSpec((tile, half), lambda f, at: (f, 0))
    place = pl.BlockSpec((tile, 2 * half), lambda f, at: (f, at[0]))
    return launch(
        last_kernel,
        "last",
        (pl.cdiv(units, tile),),
        [low, high, w, l, r, new],
        [
            part,
            part,
            place,
            pl.BlockSpec((tile, SPLIT), lambda f, at: (f, 0)),
            pl.BlockSpec((SPLIT, 2 * half), lambda f, at: (0, at[0])),
            HELD,
        ],
        [place],
        [shaped(w.shape, BF16)],
        places=[at],
        aliases={6: 0},
        vmem=LARGE,
        **links,
    )


def exchange(value, axis, mask):
    size = lax.axis_size(axis)
    return lax.ppermute(value, axis, [(i, i ^ mask) for i in range(size)])


def arrived(one, two):
    return one[:16, :128] + two[:16, :128]


def masks(size):
    return [1 << bit for bit in range(size.bit_length() - 1)]


def body(inputs, out_grads, w_gate, w_up, w_down, err_down, mom_down, q_down):
    replicas = lax.axis_size("dp")
    shards = lax.axis_size("mp")
    rank_dp = lax.axis_index("dp")
    rank_mp = lax.axis_index("mp")
    w_gate, w_up, q_t = w_gate.T, w_up.T, q_down.T
    count = shards // 2
    split = max(1, count // 2)
    turns = [(split, count - split), (0, split)] if count > split else [(0, split)]

    low, high, later_low, later_high = cast_call(mom_down)
    got = {(2, 0): exchange(low, "dp", 2), (1, 1): exchange(high, "dp", 1)}

    hid, d_gate, d_up, left, dyq = hidden_call(
        inputs, out_grads, w_gate, w_up, w_down, err_down, q_t, replicas, held=[low]
    )
    lefts = [left] + [exchange(left, "dp", mask) for mask in range(1, replicas)]

    here, there = rank_mp % 2, 1 - rank_mp % 2
    others, mine = [], [None] * count

    def blocks(turn, order, held=(), through=()):
        side, part = divmod(turn, len(turns))
        parity, slots = (there, here)[side], turns[part]
        add = others[part] if side else None
        size = slots[1] if side else 1
        outs = blocks_call(
            rank_mp,
            parity,
            slots,
            count,
            d_gate,
            d_up,
            w_gate,
            w_up,
            add,
            held=held,
            through=[order, *through],
        )
        if side:
            mine[slots[0] : slots[0] + size] = outs[:size]
        else:
            others.append(outs[0])
        return outs[size:]

    total, left, order, later_low, later_high = right_call(
        lefts,
        hid,
        err_down,
        out_grads,
        held=[arrived(got[2, 0], got[1, 1])],
        through=[dyq, later_low, later_high],
    )
    got[1, 0] = exchange(later_low, "dp", 1)
    got[2, 1] = exchange(later_high, "dp", 2)

    rounds = [("mp", mask) for mask in masks(shards)] + [("dp", mask) for mask in masks(replicas)]
    for index, (axis, mask) in enumerate(rounds):
        more = exchange(total, axis, mask)
        if index < 2 * len(turns):
            (order,) = blocks(index, order, [total])
        relay = index == 2 and count == 4
        through = others[index:] if index < len(turns) else [mine[3]] if relay else []
        held = [arrived(got[1, 0], got[2, 1])] if index == 3 else []
        total, order, *fresh = sum_call(total, more, held=held, through=[order, *through])
        if relay:
            relayed = exchange(fresh[0], "mp", 2)
        elif fresh:
            others[index] = exchange(fresh[0], "mp", 1)
    if count == 4:
        relayed, order = join_call([mine[2], relayed], held=[total], through=[order])
    l, r, got[2, 0], got[1, 1] = factors_call(
        total, left, replicas, held=[order], through=[got[2, 0], got[1, 1]]
    )
    got[3, 0] = exchange(got[2, 0], "dp", 1)
    got[3, 1] = exchange(got[1, 1], "dp", 2)
    if count == 4:
        landed = [exchange(relayed, "mp", 4), exchange(mine[1], "mp", 2)]
    else:
        landed = [exchange(mine[slot], "mp", 2 * slot) for slot in range(1, count)]

    (next_err,) = error_call(hid, out_grads, err_down, l, r)
    keys = [(1, 0), (1, 1), (2, 0), (2, 1)]
    at = jnp.stack([2 * (rank_dp ^ mask) + side for mask, side in [(0, 0), (0, 1)] + keys])
    next_mom, new, order = update_call(
        at.astype(jnp.int32),
        mom_down,
        [got[key] for key in keys],
        w_down,
        l,
        r,
        held=[next_err],
        through=[order],
    )
    far = jnp.reshape(rank_dp ^ 3, (1,)).astype(jnp.int32)
    new, order = last_call(far, got[3, 0], got[3, 1], w_down, l, r, new, through=[order])
    (in_grads,) = join_call([mine[0]] + landed, held=[order])
    return (in_grads, new, next_err, next_mom)


def solution(mesh):
    in_specs = (
        P("dp", None),
        P("dp", None),
        P(None, "mp"),
        P(None, "mp"),
        P("mp", None),
        P("dp", "mp", None),
        P("mp", "dp"),
        P(),
    )
    out_specs = (P("dp", "mp"), P("mp", None), P("dp", "mp", None), P("mp", "dp"))
    return jax.shard_map(body, mesh=mesh, in_specs=in_specs, out_specs=out_specs, check_vma=False)
```

```python
import functools

import jax
import jax.numpy as jnp
from jax import lax
from jax.experimental import pallas as pl
from jax.experimental.pallas import tpu as pltpu
from jax.sharding import PartitionSpec as P

R = 8
SPLIT = 4 * R
EPS = 1e-06
F32 = jnp.float32
BF16 = jnp.bfloat16
HIGH = lax.Precision.HIGHEST
VMEM = 48 * 2**20
SMALL = 12 * 2**20
LARGE = 62 * 2**20
ONCE = pl.Buffered(1)
STREAMS = 4
MEDIUM = 48 * 2**20
HELD = pl.BlockSpec(memory_space=pl.ANY)


def launch(kernel, name, grid, args, in_specs, out_specs, out_shape, *, places=(), held=(),
           through=(), scratch=(), vmem=VMEM, aliases=None):
    n_in, n_out = len(args), len(out_shape)
    n_held, n_through, n_place = len(held), len(through), len(places)
    first = n_place + n_in

    def inner(*refs):
        outs = first + n_held + n_through
        kernel(*refs[:first], *refs[outs : outs + n_out], *refs[outs + n_out + n_through :])

    links = {first + n_held + i: n_out + i for i in range(n_through)}
    return pl.pallas_call(
        inner,
        grid_spec=pltpu.PrefetchScalarGridSpec(
            num_scalar_prefetch=n_place,
            grid=grid,
            in_specs=list(in_specs) + [HELD] * (n_held + n_through),
            out_specs=list(out_specs) + [HELD] * n_through,
            scratch_shapes=list(scratch),
        ),
        out_shape=list(out_shape)
        + [jax.ShapeDtypeStruct(array.shape, array.dtype) for array in through],
        input_output_aliases={**links, **(aliases or {})},
        compiler_params=pltpu.CompilerParams(vmem_limit_bytes=vmem),
        cost_estimate=pl.CostEstimate(flops=1, bytes_accessed=1, transcendentals=0),
        name=name,
    )(*places, *args, *held, *through)


def shaped(shape, dtype):
    return jax.ShapeDtypeStruct(shape, dtype)


def dot(left, right):
    return jnp.dot(left, right, preferred_element_type=F32)


def dot_nt(left, right):
    return lax.dot_general(left, right, (((1,), (1,)), ((), ())), preferred_element_type=F32)


def terms(rows):
    hi = rows.astype(BF16).astype(F32)
    rest = rows - hi
    mid = rest.astype(BF16).astype(F32)
    return hi, mid, rest - mid


def spread(rows):
    hi, mid, low = terms(rows)
    return jnp.concatenate([hi, mid, low, jnp.zeros_like(hi)], axis=0).astype(BF16)


def gather_terms(rows):
    return rows[:R] + rows[R : 2 * R] + rows[2 * R : 3 * R]


def tree(parts):
    while len(parts) > 1:
        odd = parts[len(parts) // 2 * 2 :]
        parts = [left + right for left, right in zip(parts[::2], parts[1::2])] + odd
    return parts[0]


def whole(shape):
    return pl.BlockSpec(shape, lambda *_: (0,) * len(shape), pipeline_mode=ONCE)


def unit_tile(units):
    return 256 if units > 512 and units % 16 == 0 else units


def cast_kernel(mom_ref, *outs):
    half = mom_ref.shape[1] // 2
    low, high = mom_ref[:, :half].astype(BF16), mom_ref[:, half:].astype(BF16)
    for out, part in zip(outs, (low, high, low, high)):
        out[...] = part


def cast_call(mom, **links):
    units, cols = mom.shape
    tile = units // 2 if units % 32 == 0 and units > 512 else units
    part = pl.BlockSpec((tile, cols // 2), lambda f: (f, 0))
    return launch(
        cast_kernel,
        "cast",
        (units // tile,),
        [mom],
        [pl.BlockSpec((tile, cols), lambda f: (f, 0))],
        [part] * 4,
        [shaped((units, cols // 2), BF16)] * 4,
        vmem=MEDIUM,
        **links,
    )


def hidden_kernel(
    replicas,
    x_ref, wg_ref, wu_ref, wd_ref, err_ref, q_ref, dy_any,
    hid_ref, dg_ref, du_ref, left_ref, dyq_ref,
    dy_ref, q_terms, dyq_terms, sem,
):
    fetch = pltpu.make_async_copy(dy_any, dy_ref, sem)

    @pl.when(pl.program_id(0) == 0)
    def _():
        fetch.start()
        q_terms[...] = spread(q_ref[...])

    gate = dot_nt(x_ref[...], wg_ref[...])
    up = dot_nt(x_ref[...], wu_ref[...])
    both = dot_nt(err_ref[0], q_terms[...])

    @pl.when(pl.program_id(0) == 0)
    def _():
        fetch.wait()
        dyq = gather_terms(dot_nt(dy_ref[...], q_terms[...]).T)
        dyq_ref[...] = dyq
        dyq_terms[...] = spread(dyq)

    dh = dot_nt(dy_ref[...], wd_ref[...])
    sig = jax.nn.sigmoid(gate)
    silu = gate * sig
    hid = (silu * up).T.astype(BF16)
    hid_ref[...] = hid
    dg_ref[...] = (dh * up * sig * (1.0 + gate * (1.0 - sig))).astype(BF16)
    du_ref[...] = (dh * silu).astype(BF16)
    both += dot_nt(hid, dyq_terms[...])
    left_ref[...] = gather_terms(both.T) / replicas


def hidden_call(x, dy, wg, wu, wd, err, q_t, replicas, **links):
    tok, depth = x.shape
    units = wg.shape[0]
    tile = unit_tile(units)
    rows = pl.BlockSpec((tile, depth), lambda f: (f, 0))
    part = pl.BlockSpec((tok, tile), lambda f: (0, f))
    return launch(
        functools.partial(hidden_kernel, replicas),
        "hidden",
        (pl.cdiv(units, tile),),
        [x, wg, wu, wd, err, q_t, dy],
        [
            whole((tok, depth)),
            rows,
            rows,
            rows,
            pl.BlockSpec((1, tile, depth), lambda f: (0, f, 0)),
            whole(q_t.shape),
            HELD,
        ],
        [
            pl.BlockSpec((tile, tok), lambda f: (f, 0)),
            part,
            part,
            pl.BlockSpec((R, tile), lambda f: (0, f)),
            whole((R, tok)),
        ],
        [
            shaped((units, tok), BF16),
            shaped((tok, units), BF16),
            shaped((tok, units), BF16),
            shaped((R, units), F32),
            shaped((R, tok), F32),
        ],
        scratch=[
            pltpu.VMEM((tok, depth), BF16),
            pltpu.VMEM((SPLIT, depth), BF16),
            pltpu.VMEM((SPLIT, tok), BF16),
            pltpu.SemaphoreType.DMA(()),
        ],
        **links,
    )


def error_streams(tile, depth):
    shape = (1, tile, depth // STREAMS)
    return [pl.BlockSpec(shape, lambda f, c=c: (0, f, c)) for c in range(STREAMS)]


def columns(ref, step, tile):
    if ref.shape[1] == tile:
        return ref[...]
    return ref[:, pl.ds(pl.multiple_of(step * tile, tile), tile)]


def right_kernel(parts, dy_steps, *refs):
    lefts = refs[:parts]
    errs, (hid_ref, dy_ref, out_ref, left_ref, left_terms, mixed_terms, total) = (
        refs[parts:-7],
        refs[-7:],
    )
    step = pl.program_id(0)
    units = left_ref.shape[1]
    tile, width = errs[0].shape[1:]
    depth = width * len(errs)
    dy_tile = dy_ref.shape[0]
    tail = units % tile
    last = pl.num_programs(0) - 1

    @pl.when(step == 0)
    def _():
        left = tree([ref[...] for ref in lefts])
        left_ref[...] = left
        left_terms[:, :units] = spread(left)
        mixed_terms[...] = spread(gather_terms(dot(left_terms[:, :units], hid_ref[...])))
        gram = lax.dot_general(
            left, left, (((1,), (1,)), ((), ())), precision=HIGH, preferred_element_type=F32
        )
        out_ref[:, depth:] = jnp.concatenate([gram, jnp.zeros((R, 128 - R), F32)], axis=1)
        total[...] = jnp.zeros_like(total)

    @pl.when(step < dy_steps)
    def _():
        total[...] += dot(columns(mixed_terms, step, dy_tile), dy_ref[...])

    if tail:

        @pl.when(step < last)
        def _():
            left = columns(left_terms, step, tile)
            for at, err_ref in enumerate(errs):
                total[:, at * width : (at + 1) * width] += dot(left, err_ref[0])

        @pl.when(step == last)
        def _():
            left = left_terms[:, units - tail : units]
            for at, err_ref in enumerate(errs):
                total[:, at * width : (at + 1) * width] += dot(left, err_ref[0, :tail])

    else:
        left = columns(left_terms, step, tile)
        for at, err_ref in enumerate(errs):
            total[:, at * width : (at + 1) * width] += dot(left, err_ref[0])

    @pl.when(step == last)
    def _():
        out_ref[:, :depth] = gather_terms(total[...])


def right_call(lefts, hid, err, dy, **links):
    units, tok = hid.shape
    depth = dy.shape[1]
    tile = unit_tile(units)
    tiles = pl.cdiv(units, tile)
    dy_steps = 2 if tiles > 1 else 1
    return launch(
        functools.partial(right_kernel, len(lefts), dy_steps),
        "right",
        (tiles,),
        [*lefts] + [err] * STREAMS + [hid, dy],
        [whole((R, units))] * len(lefts)
        + error_streams(tile, depth)
        + [
            whole((units, tok)),
            pl.BlockSpec((tok // dy_steps, depth), lambda f: (jnp.minimum(f, dy_steps - 1), 0)),
        ],
        [whole((R, depth + 128)), whole((R, units))],
        [shaped((R, depth + 128), F32), shaped((R, units), F32)],
        scratch=[
            pltpu.VMEM((SPLIT, tiles * tile), BF16),
            pltpu.VMEM((SPLIT, tok), BF16),
            pltpu.VMEM((SPLIT, depth), F32),
        ],
        vmem=MEDIUM,
        **links,
    )


def sum_kernel(one_ref, two_ref, out_ref):
    out_ref[...] = one_ref[...] + two_ref[...]


def sum_call(one, two, **links):
    return launch(
        sum_kernel,
        "sum",
        (1,),
        [one, two],
        [whole(one.shape)] * 2,
        [whole(one.shape)],
        [shaped(one.shape, one.dtype)],
        vmem=SMALL,
        **links,
    )


def join_kernel(*refs):
    refs[-1][...] = tree([ref[...].astype(F32) for ref in refs[:-1]]).astype(BF16)


def join_call(parts, **links):
    shape = parts[0].shape
    return launch(
        join_kernel,
        "join",
        (1,),
        parts,
        [whole(shape)] * len(parts),
        [whole(shape)],
        [shaped(shape, BF16)],
        **links,
    )


def factors_kernel(replicas, sum_ref, left_ref, l_ref, r_ref):
    depth = r_ref.shape[1]
    gram = sum_ref[:, depth : depth + R] / replicas
    row = lax.broadcasted_iota(jnp.int32, (R, R), 0)
    col = lax.broadcasted_iota(jnp.int32, (R, R), 1)
    eye = (row == col).astype(F32)
    basis = jnp.zeros((R, R), F32)
    for k in range(R):
        unit = eye[k : k + 1]
        coeffs = jnp.sum(basis * gram[k : k + 1], axis=1, keepdims=True)
        rest = unit - jnp.sum(coeffs * basis, axis=0, keepdims=True)
        rest_col = jnp.sum(eye * rest, axis=1, keepdims=True)
        image = jnp.sum(rest_col * gram, axis=0, keepdims=True)
        square = jnp.sum(image * rest, axis=1, keepdims=True)
        basis = jnp.where(row == k, rest * lax.rsqrt(jnp.maximum(square, 0.0) + EPS), basis)
    left = jnp.dot(basis, left_ref[...], precision=HIGH, preferred_element_type=F32)
    right = jnp.dot(basis, sum_ref[:, :depth], precision=HIGH, preferred_element_type=F32)
    hi, mid, _ = terms(left)
    zero = jnp.zeros_like(hi)
    l_ref[...] = jnp.concatenate([hi, hi, mid, zero], axis=0).T.astype(BF16)
    hi, mid, _ = terms(right / replicas)
    zero = jnp.zeros_like(hi)
    r_ref[...] = jnp.concatenate([hi, mid, hi, zero], axis=0).astype(BF16)


def factors_call(total, left, replicas, **links):
    units = left.shape[1]
    depth = total.shape[1] - 128
    return launch(
        functools.partial(factors_kernel, replicas),
        "factors",
        (1,),
        [total, left],
        [whole(total.shape), whole(left.shape)],
        [whole((units, SPLIT)), whole((SPLIT, depth))],
        [shaped((units, SPLIT), BF16), shaped((SPLIT, depth), BF16)],
        vmem=LARGE,
        **links,
    )


def other_kernel(where_ref, dg_ref, du_ref, wg_ref, wu_ref, out_ref):
    out_ref[0] = (dot(dg_ref[...], wg_ref[...]) + dot(du_ref[...], wu_ref[...])).astype(BF16)


def mine_kernel(where_ref, dg_ref, du_ref, wg_ref, wu_ref, add_ref, *outs):
    part = dot(dg_ref[...], wg_ref[...]) + dot(du_ref[...], wu_ref[...])
    part = (part + add_ref[0].astype(F32)).astype(BF16)
    for slot, out in enumerate(outs):

        @pl.when(pl.program_id(0) == slot)
        def _(out=out):
            out[...] = part


def blocks_call(pos, parity, slots, count, dg, du, wg, wu, add=None, **links):
    tok, units = dg.shape
    depth = wg.shape[1]
    width = depth // (2 * count)
    where = jnp.stack([pos // 2, parity]).astype(jnp.int32)
    first, steps = slots
    block = pl.BlockSpec((units, width), lambda s, at: (0, 2 * ((s + first) ^ at[0]) + at[1]))
    slot = pl.BlockSpec((1, tok, width), lambda s, at: (s, 0, 0))
    in_specs = [whole((tok, units)), whole((tok, units)), block, block]
    args = [dg, du, wg, wu]
    if add is None:
        kernel = other_kernel
        out_specs = [slot]
        out_shape = [shaped((steps, tok, width), BF16)]
    else:
        kernel = mine_kernel
        in_specs.append(slot)
        args.append(add)
        out_specs = [whole((tok, width))] * steps
        out_shape = [shaped((tok, width), BF16)] * steps
    return launch(
        kernel, "blocks", (steps,), args, in_specs, out_specs, out_shape, places=[where], vmem=MEDIUM, **links
    )


def error_kernel(hid_ref, l_ref, r_ref, dy_any, *refs):
    errs, (out_ref, dy_ref, sems) = refs[:-3], refs[-3:]
    width = errs[0].shape[2]
    first = pl.program_id(0) == 0
    cuts = [slice(part * width, (part + 1) * width) for part in range(len(errs))]
    fetches = [
        pltpu.make_async_copy(dy_any.at[:, at], dy_ref.at[:, at], sems.at[part])
        for part, at in enumerate(cuts)
    ]

    @pl.when(first)
    def _():
        for fetch in fetches:
            fetch.start()

    for at, err_ref, fetch in zip(cuts, errs, fetches):

        @pl.when(first)
        def _(fetch=fetch):
            fetch.wait()

        grown = dot(hid_ref[...], dy_ref[:, at]) + err_ref[0].astype(F32)
        out_ref[0, :, at] = (grown - dot(l_ref[...], r_ref[:, at])).astype(BF16)


def error_call(hid, dy, err, l, r, **links):
    units, tok = hid.shape
    depth = dy.shape[1]
    tile = 352 if units > 512 else units
    return launch(
        error_kernel,
        "error",
        (pl.cdiv(units, tile),),
        [hid, l, r, dy] + [err] * STREAMS,
        [
            pl.BlockSpec((tile, tok), lambda f: (f, 0)),
            pl.BlockSpec((tile, SPLIT), lambda f: (f, 0)),
            whole(r.shape),
            HELD,
            *error_streams(tile, depth),
        ],
        [pl.BlockSpec((1, tile, depth), lambda f: (0, f, 0))],
        [shaped(err.shape, BF16)],
        scratch=[pltpu.VMEM(dy.shape, BF16), pltpu.SemaphoreType.DMA((STREAMS,))],
        vmem=LARGE,
        **links,
    )


def updated(w, mom, approx):
    return (w.astype(F32) - 0.1 * (0.9 * mom.astype(F32) + approx)).astype(BF16)


def update_kernel(at_ref, mom_ref, l_ref, r_ref, w_ref, *refs):
    pieces, (mom_out, w_out) = refs[:-2], refs[-2:]
    half = pieces[0].shape[1]
    group = pl.program_id(0)
    approx = dot(l_ref[...], r_ref[...])

    @pl.when(group == 0)
    def _():
        mom = mom_ref[...]
        mom_out[...] = 0.9 * mom + approx
        w_out[...] = updated(w_ref[...], mom.astype(BF16), approx)

    for pair in range(len(pieces) // 2):

        @pl.when(group == 1 + pair)
        def _(pair=pair):
            for side, piece in enumerate(pieces[2 * pair : 2 * pair + 2]):
                at = slice(side * half, (side + 1) * half)
                w_out[:, at] = updated(w_ref[:, at], piece[...], approx[:, at])


def update_call(at, mom, pieces, w, l, r, **links):
    units, cols = mom.shape
    half = pieces[0].shape[1]
    tile = 352 if units > 512 else units
    tiles = pl.cdiv(units, tile)

    def during(group, width):
        def index(c, f, at):
            return jnp.where(c < group, 0, jnp.where(c > group, tiles - 1, f)), 0

        return pl.BlockSpec((tile, width), index)

    weights = pl.BlockSpec((tile, cols), lambda c, f, at: (f, at[c]))
    return launch(
        update_kernel,
        "update",
        (1 + len(pieces) // 2, tiles),
        [mom, l, r, w, *pieces],
        [
            during(0, cols),
            pl.BlockSpec((tile, SPLIT), lambda c, f, at: (f, 0)),
            pl.BlockSpec((SPLIT, cols), lambda c, f, at: (0, at[c])),
            weights,
            *[during(1 + slot // 2, half) for slot in range(len(pieces))],
        ],
        [during(0, cols), weights],
        [shaped(mom.shape, F32), shaped(w.shape, BF16)],
        places=[at],
        vmem=LARGE,
        **links,
    )


def last_kernel(at_ref, low_ref, high_ref, w_ref, l_ref, r_ref, _, w_out):
    half = low_ref.shape[1]
    approx = dot(l_ref[...], r_ref[...])
    w_out[:, :half] = updated(w_ref[:, :half], low_ref[...], approx[:, :half])
    w_out[:, half:] = updated(w_ref[:, half:], high_ref[...], approx[:, half:])


def last_call(at, low, high, w, l, r, new, **links):
    units, half = low.shape
    tile = 352 if units > 512 else units
    part = pl.BlockSpec((tile, half), lambda f, at: (f, 0))
    place = pl.BlockSpec((tile, 2 * half), lambda f, at: (f, at[0]))
    return launch(
        last_kernel,
        "last",
        (pl.cdiv(units, tile),),
        [low, high, w, l, r, new],
        [
            part,
            part,
            place,
            pl.BlockSpec((tile, SPLIT), lambda f, at: (f, 0)),
            pl.BlockSpec((SPLIT, 2 * half), lambda f, at: (0, at[0])),
            HELD,
        ],
        [place],
        [shaped(w.shape, BF16)],
        places=[at],
        aliases={6: 0},
        vmem=LARGE,
        **links,
    )


def exchange(value, axis, mask):
    size = lax.axis_size(axis)
    return lax.ppermute(value, axis, [(i, i ^ mask) for i in range(size)])


def arrived(one, two):
    return one[:16, :128] + two[:16, :128]


def masks(size):
    return [1 << bit for bit in range(size.bit_length() - 1)]


def body(inputs, out_grads, w_gate, w_up, w_down, err_down, mom_down, q_down):
    replicas = lax.axis_size("dp")
    shards = lax.axis_size("mp")
    rank_dp = lax.axis_index("dp")
    rank_mp = lax.axis_index("mp")
    w_gate, w_up, q_t = w_gate.T, w_up.T, q_down.T
    count = shards // 2
    split = max(1, count // 2)
    turns = [(split, count - split), (0, split)] if count > split else [(0, split)]

    low, high, later_low, later_high = cast_call(mom_down)
    got = {(2, 0): exchange(low, "dp", 2), (1, 1): exchange(high, "dp", 1)}

    hid, d_gate, d_up, left, dyq = hidden_call(
        inputs, out_grads, w_gate, w_up, w_down, err_down, q_t, replicas, held=[low]
    )
    lefts = [left] + [exchange(left, "dp", mask) for mask in range(1, replicas)]

    here, there = rank_mp % 2, 1 - rank_mp % 2
    others, mine = [], [None] * count

    def blocks(turn, order, held=(), through=()):
        side, part = divmod(turn, len(turns))
        parity, slots = (there, here)[side], turns[part]
        add = others[part] if side else None
        size = slots[1] if side else 1
        outs = blocks_call(
            rank_mp,
            parity,
            slots,
            count,
            d_gate,
            d_up,
            w_gate,
            w_up,
            add,
            held=held,
            through=[order, *through],
        )
        if side:
            mine[slots[0] : slots[0] + size] = outs[:size]
        else:
            others.append(outs[0])
        return outs[size:]

    total, left, order, later_low, later_high = right_call(
        lefts,
        hid,
        err_down,
        out_grads,
        held=[arrived(got[2, 0], got[1, 1])],
        through=[dyq, later_low, later_high],
    )
    got[1, 0] = exchange(later_low, "dp", 1)
    got[2, 1] = exchange(later_high, "dp", 2)

    rounds = [("mp", mask) for mask in masks(shards)] + [("dp", mask) for mask in masks(replicas)]
    for index, (axis, mask) in enumerate(rounds):
        more = exchange(total, axis, mask)
        if index < 2 * len(turns):
            (order,) = blocks(index, order, [total])
        relay = index == 2 and count == 4
        through = others[index:] if index < len(turns) else [mine[3]] if relay else []
        held = [arrived(got[1, 0], got[2, 1])] if index == 3 else []
        total, order, *fresh = sum_call(total, more, held=held, through=[order, *through])
        if relay:
            relayed = exchange(fresh[0], "mp", 2)
        elif fresh:
            others[index] = exchange(fresh[0], "mp", 1)
    if count == 4:
        relayed, order = join_call(
            [mine[2], relayed], held=[total], through=[order], vmem=SMALL
        )
    l, r, got[2, 0], got[1, 1] = factors_call(
        total, left, replicas, held=[order], through=[got[2, 0], got[1, 1]]
    )
    got[3, 0] = exchange(got[2, 0], "dp", 1)
    got[3, 1] = exchange(got[1, 1], "dp", 2)
    if count == 4:
        landed = [exchange(relayed, "mp", 4), exchange(mine[1], "mp", 2)]
    else:
        landed = [exchange(mine[slot], "mp", 2 * slot) for slot in range(1, count)]

    (next_err,) = error_call(hid, out_grads, err_down, l, r)
    keys = [(1, 0), (1, 1), (2, 0), (2, 1)]
    at = jnp.stack([rank_dp, rank_dp ^ 1, rank_dp ^ 2])
    next_mom, new, order = update_call(
        at.astype(jnp.int32),
        mom_down,
        [got[key] for key in keys],
        w_down,
        l,
        r,
        held=[next_err],
        through=[order],
    )
    corner = jnp.reshape(rank_dp ^ 3, (1,)).astype(jnp.int32)
    new, order = last_call(corner, got[3, 0], got[3, 1], w_down, l, r, new, through=[order])
    (in_grads,) = join_call([mine[0]] + landed, held=[order], vmem=SMALL)
    return (in_grads, new, next_err, next_mom)


def solution(mesh):
    in_specs = (
        P("dp", None),
        P("dp", None),
        P(None, "mp"),
        P(None, "mp"),
        P("mp", None),
        P("dp", "mp", None),
        P("mp", "dp"),
        P(),
    )
    out_specs = (P("dp", "mp"), P("mp", None), P("dp", "mp", None), P("mp", "dp"))
    return jax.shard_map(body, mesh=mesh, in_specs=in_specs, out_specs=out_specs, check_vma=False)
```

```python
import functools

import jax
import jax.numpy as jnp
from jax import lax
from jax.experimental import pallas as pl
from jax.experimental.pallas import tpu as pltpu
from jax.sharding import PartitionSpec as P

R = 8
SPLIT = 4 * R
EPS = 1e-06
F32 = jnp.float32
BF16 = jnp.bfloat16
HIGH = lax.Precision.HIGHEST
VMEM = 48 * 2**20
SMALL = 12 * 2**20
LARGE = 62 * 2**20
ONCE = pl.Buffered(1)
STREAMS = 4
MEDIUM = 48 * 2**20
HELD = pl.BlockSpec(memory_space=pl.ANY)


def launch(kernel, name, grid, args, in_specs, out_specs, out_shape, *, places=(), held=(),
           through=(), scratch=(), vmem=VMEM, aliases=None):
    n_in, n_out = len(args), len(out_shape)
    n_held, n_through, n_place = len(held), len(through), len(places)
    first = n_place + n_in

    def inner(*refs):
        outs = first + n_held + n_through
        kernel(*refs[:first], *refs[outs : outs + n_out], *refs[outs + n_out + n_through :])

    links = {first + n_held + i: n_out + i for i in range(n_through)}
    return pl.pallas_call(
        inner,
        grid_spec=pltpu.PrefetchScalarGridSpec(
            num_scalar_prefetch=n_place,
            grid=grid,
            in_specs=list(in_specs) + [HELD] * (n_held + n_through),
            out_specs=list(out_specs) + [HELD] * n_through,
            scratch_shapes=list(scratch),
        ),
        out_shape=list(out_shape)
        + [jax.ShapeDtypeStruct(array.shape, array.dtype) for array in through],
        input_output_aliases={**links, **(aliases or {})},
        compiler_params=pltpu.CompilerParams(vmem_limit_bytes=vmem),
        cost_estimate=pl.CostEstimate(flops=1, bytes_accessed=1, transcendentals=0),
        name=name,
    )(*places, *args, *held, *through)


def shaped(shape, dtype):
    return jax.ShapeDtypeStruct(shape, dtype)


def dot(left, right):
    return jnp.dot(left, right, preferred_element_type=F32)


def dot_nt(left, right):
    return lax.dot_general(left, right, (((1,), (1,)), ((), ())), preferred_element_type=F32)


def terms(rows):
    hi = rows.astype(BF16).astype(F32)
    rest = rows - hi
    mid = rest.astype(BF16).astype(F32)
    return hi, mid, rest - mid


def spread(rows):
    hi, mid, low = terms(rows)
    return jnp.concatenate([hi, mid, low, jnp.zeros_like(hi)], axis=0).astype(BF16)


def gather_terms(rows):
    return rows[:R] + rows[R : 2 * R] + rows[2 * R : 3 * R]


def tree(parts):
    while len(parts) > 1:
        odd = parts[len(parts) // 2 * 2 :]
        parts = [left + right for left, right in zip(parts[::2], parts[1::2])] + odd
    return parts[0]


def whole(shape):
    return pl.BlockSpec(shape, lambda *_: (0,) * len(shape), pipeline_mode=ONCE)


def unit_tile(units):
    return 256 if units > 512 and units % 16 == 0 else units


def cast_kernel(mom_ref, *outs):
    half = mom_ref.shape[1] // 2
    low, high = mom_ref[:, :half].astype(BF16), mom_ref[:, half:].astype(BF16)
    for out, part in zip(outs, (low, high, low, high)):
        out[...] = part


def cast_call(mom, **links):
    units, cols = mom.shape
    tile = units // 2 if units % 32 == 0 and units > 512 else units
    part = pl.BlockSpec((tile, cols // 2), lambda f: (f, 0))
    return launch(
        cast_kernel,
        "cast",
        (units // tile,),
        [mom],
        [pl.BlockSpec((tile, cols), lambda f: (f, 0))],
        [part] * 4,
        [shaped((units, cols // 2), BF16)] * 4,
        vmem=MEDIUM,
        **links,
    )


def hidden_kernel(
    replicas, units,
    q_ref, x_any, dy_any, *refs,
):
    sources, refs = refs[:4], refs[4:]
    (hid_ref, dg_ref, du_ref, left_ref, dyq_ref), refs = refs[:5], refs[5:]
    (x_ref, dy_ref), slots, (q_terms, dyq_terms, once, sems) = refs[:2], refs[2:6], refs[6:]
    step = pl.program_id(0)
    tile = slots[0].shape[1]
    last = pl.cdiv(units, tile) - 1
    tail = units - last * tile
    slot = lax.rem(step, 2)
    fetch_x = pltpu.make_async_copy(x_any, x_ref, once.at[0])
    fetch_dy = pltpu.make_async_copy(dy_any, dy_ref, once.at[1])

    def move(act, at, which):
        def each(rows):
            for k in which:
                source = sources[k].at[0] if len(sources[k].shape) == 3 else sources[k]
                act(
                    pltpu.make_async_copy(
                        source.at[pl.ds(pl.multiple_of(at * tile, tile), rows)],
                        slots[k].at[lax.rem(at, 2), pl.ds(0, rows)],
                        sems.at[k, lax.rem(at, 2)],
                    ),
                    k % 2,
                )

        if tail == tile:
            each(tile)
        else:
            pl.when(at < last)(lambda: each(tile))
            pl.when(at == last)(lambda: each(tail))

    def start(copy, queue):
        copy.start(priority=queue)

    def wait(copy, _):
        copy.wait()

    def finish(gate, up, both, dh):
        sig = jax.nn.sigmoid(gate)
        silu = gate * sig
        hid = (silu * up).T.astype(BF16)
        hid_ref[...] = hid
        dg_ref[...] = (dh * up * sig * (1.0 + gate * (1.0 - sig))).astype(BF16)
        du_ref[...] = (dh * silu).astype(BF16)
        both += dot_nt(hid, dyq_terms[...])
        left_ref[...] = gather_terms(both.T) / replicas

    @pl.when(step == 0)
    def _():
        fetch_x.start()
        move(start, step, (0, 1, 2))
        fetch_dy.start()
        move(start, step, (3,))

    @pl.when(step < last)
    def _():
        move(start, step + 1, (0, 1, 2, 3))

    @pl.when(step == 0)
    def _():
        q_terms[...] = spread(q_ref[...])
        fetch_x.wait()
        move(wait, step, (0,))
        gate = dot_nt(x_ref[...], slots[0][slot])
        move(wait, step, (1,))
        up = dot_nt(x_ref[...], slots[1][slot])
        move(wait, step, (2,))
        both = dot_nt(slots[2][slot], q_terms[...])
        fetch_dy.wait()
        dyq = gather_terms(dot_nt(dy_ref[...], q_terms[...]).T)
        dyq_ref[...] = dyq
        dyq_terms[...] = spread(dyq)
        move(wait, step, (3,))
        finish(gate, up, both, dot_nt(dy_ref[...], slots[3][slot]))

    @pl.when(step > 0)
    def _():
        move(wait, step, (0, 1, 2, 3))
        gate = dot_nt(x_ref[...], slots[0][slot])
        up = dot_nt(x_ref[...], slots[1][slot])
        both = dot_nt(slots[2][slot], q_terms[...])
        finish(gate, up, both, dot_nt(dy_ref[...], slots[3][slot]))


def hidden_call(x, dy, wg, wu, wd, err, q_t, replicas, **links):
    tok, depth = x.shape
    units = wg.shape[0]
    tile = unit_tile(units)
    part = pl.BlockSpec((tok, tile), lambda f: (0, f))
    return launch(
        functools.partial(hidden_kernel, replicas, units),
        "hidden",
        (pl.cdiv(units, tile),),
        [q_t, x, dy, wg, wu, err, wd],
        [whole(q_t.shape)] + [HELD] * 6,
        [
            pl.BlockSpec((tile, tok), lambda f: (f, 0)),
            part,
            part,
            pl.BlockSpec((R, tile), lambda f: (0, f)),
            whole((R, tok)),
        ],
        [
            shaped((units, tok), BF16),
            shaped((tok, units), BF16),
            shaped((tok, units), BF16),
            shaped((R, units), F32),
            shaped((R, tok), F32),
        ],
        scratch=[
            *[pltpu.VMEM((tok, depth), BF16)] * 2,
            *[pltpu.VMEM((2, tile, depth), BF16)] * 4,
            pltpu.VMEM((SPLIT, depth), BF16),
            pltpu.VMEM((SPLIT, tok), BF16),
            pltpu.SemaphoreType.DMA((2,)),
            pltpu.SemaphoreType.DMA((4, 2)),
        ],
        **links,
    )


def error_streams(tile, depth):
    shape = (1, tile, depth // STREAMS)
    return [pl.BlockSpec(shape, lambda f, c=c: (0, f, c)) for c in range(STREAMS)]


def columns(ref, step, tile):
    if ref.shape[1] == tile:
        return ref[...]
    return ref[:, pl.ds(pl.multiple_of(step * tile, tile), tile)]


def right_kernel(parts, dy_steps, *refs):
    lefts = refs[:parts]
    errs, (hid_ref, dy_ref, out_ref, left_ref, left_terms, mixed_terms, total) = (
        refs[parts:-7],
        refs[-7:],
    )
    step = pl.program_id(0)
    units = left_ref.shape[1]
    tile, width = errs[0].shape[1:]
    depth = width * len(errs)
    dy_tile = dy_ref.shape[0]
    tail = units % tile
    last = pl.num_programs(0) - 1

    @pl.when(step == 0)
    def _():
        left = tree([ref[...] for ref in lefts])
        left_ref[...] = left
        left_terms[:, :units] = spread(left)
        mixed_terms[...] = spread(gather_terms(dot(left_terms[:, :units], hid_ref[...])))
        gram = lax.dot_general(
            left, left, (((1,), (1,)), ((), ())), precision=HIGH, preferred_element_type=F32
        )
        out_ref[:, depth:] = jnp.concatenate([gram, jnp.zeros((R, 128 - R), F32)], axis=1)
        total[...] = jnp.zeros_like(total)

    @pl.when(step < dy_steps)
    def _():
        total[...] += dot(columns(mixed_terms, step, dy_tile), dy_ref[...])

    if tail:

        @pl.when(step < last)
        def _():
            left = columns(left_terms, step, tile)
            for at, err_ref in enumerate(errs):
                total[:, at * width : (at + 1) * width] += dot(left, err_ref[0])

        @pl.when(step == last)
        def _():
            left = left_terms[:, units - tail : units]
            for at, err_ref in enumerate(errs):
                total[:, at * width : (at + 1) * width] += dot(left, err_ref[0, :tail])

    else:
        left = columns(left_terms, step, tile)
        for at, err_ref in enumerate(errs):
            total[:, at * width : (at + 1) * width] += dot(left, err_ref[0])

    @pl.when(step == last)
    def _():
        out_ref[:, :depth] = gather_terms(total[...])


def right_call(lefts, hid, err, dy, **links):
    units, tok = hid.shape
    depth = dy.shape[1]
    tile = unit_tile(units)
    tiles = pl.cdiv(units, tile)
    dy_steps = 2 if tiles > 1 else 1
    return launch(
        functools.partial(right_kernel, len(lefts), dy_steps),
        "right",
        (tiles,),
        [*lefts] + [err] * STREAMS + [hid, dy],
        [whole((R, units))] * len(lefts)
        + error_streams(tile, depth)
        + [
            whole((units, tok)),
            pl.BlockSpec((tok // dy_steps, depth), lambda f: (jnp.minimum(f, dy_steps - 1), 0)),
        ],
        [whole((R, depth + 128)), whole((R, units))],
        [shaped((R, depth + 128), F32), shaped((R, units), F32)],
        scratch=[
            pltpu.VMEM((SPLIT, tiles * tile), BF16),
            pltpu.VMEM((SPLIT, tok), BF16),
            pltpu.VMEM((SPLIT, depth), F32),
        ],
        vmem=MEDIUM,
        **links,
    )


def sum_kernel(one_ref, two_ref, out_ref):
    out_ref[...] = one_ref[...] + two_ref[...]


def sum_call(one, two, **links):
    return launch(
        sum_kernel,
        "sum",
        (1,),
        [one, two],
        [whole(one.shape)] * 2,
        [whole(one.shape)],
        [shaped(one.shape, one.dtype)],
        vmem=SMALL,
        **links,
    )


def join_kernel(*refs):
    refs[-1][...] = tree([ref[...].astype(F32) for ref in refs[:-1]]).astype(BF16)


def join_call(parts, **links):
    shape = parts[0].shape
    return launch(
        join_kernel,
        "join",
        (1,),
        parts,
        [whole(shape)] * len(parts),
        [whole(shape)],
        [shaped(shape, BF16)],
        vmem=SMALL,
        **links,
    )


def factors_kernel(replicas, sum_ref, left_ref, l_ref, r_ref):
    depth = r_ref.shape[1]
    gram = sum_ref[:, depth : depth + R] / replicas
    row = lax.broadcasted_iota(jnp.int32, (R, R), 0)
    col = lax.broadcasted_iota(jnp.int32, (R, R), 1)
    eye = (row == col).astype(F32)
    basis = jnp.zeros((R, R), F32)
    for k in range(R):
        unit = eye[k : k + 1]
        coeffs = jnp.sum(basis * gram[k : k + 1], axis=1, keepdims=True)
        rest = unit - jnp.sum(coeffs * basis, axis=0, keepdims=True)
        rest_col = jnp.sum(eye * rest, axis=1, keepdims=True)
        image = jnp.sum(rest_col * gram, axis=0, keepdims=True)
        square = jnp.sum(image * rest, axis=1, keepdims=True)
        basis = jnp.where(row == k, rest * lax.rsqrt(jnp.maximum(square, 0.0) + EPS), basis)
    left = jnp.dot(basis, left_ref[...], precision=HIGH, preferred_element_type=F32)
    right = jnp.dot(basis, sum_ref[:, :depth], precision=HIGH, preferred_element_type=F32)
    hi, mid, _ = terms(left)
    zero = jnp.zeros_like(hi)
    l_ref[...] = jnp.concatenate([hi, hi, mid, zero], axis=0).T.astype(BF16)
    hi, mid, _ = terms(right / replicas)
    zero = jnp.zeros_like(hi)
    r_ref[...] = jnp.concatenate([hi, mid, hi, zero], axis=0).astype(BF16)


def factors_call(total, left, replicas, **links):
    units = left.shape[1]
    depth = total.shape[1] - 128
    return launch(
        functools.partial(factors_kernel, replicas),
        "factors",
        (1,),
        [total, left],
        [whole(total.shape), whole(left.shape)],
        [whole((units, SPLIT)), whole((SPLIT, depth))],
        [shaped((units, SPLIT), BF16), shaped((SPLIT, depth), BF16)],
        vmem=LARGE,
        **links,
    )


def other_kernel(where_ref, dg_ref, du_ref, wg_ref, wu_ref, out_ref):
    out_ref[0] = (dot(dg_ref[...], wg_ref[...]) + dot(du_ref[...], wu_ref[...])).astype(BF16)


def mine_kernel(where_ref, dg_ref, du_ref, wg_ref, wu_ref, add_ref, *outs):
    part = dot(dg_ref[...], wg_ref[...]) + dot(du_ref[...], wu_ref[...])
    part = (part + add_ref[0].astype(F32)).astype(BF16)
    for slot, out in enumerate(outs):

        @pl.when(pl.program_id(0) == slot)
        def _(out=out):
            out[...] = part


def blocks_call(pos, parity, slots, count, dg, du, wg, wu, add=None, **links):
    tok, units = dg.shape
    depth = wg.shape[1]
    width = depth // (2 * count)
    where = jnp.stack([pos // 2, parity]).astype(jnp.int32)
    first, steps = slots
    block = pl.BlockSpec((units, width), lambda s, at: (0, 2 * ((s + first) ^ at[0]) + at[1]))
    slot = pl.BlockSpec((1, tok, width), lambda s, at: (s, 0, 0))
    in_specs = [whole((tok, units)), whole((tok, units)), block, block]
    args = [dg, du, wg, wu]
    if add is None:
        kernel = other_kernel
        out_specs = [slot]
        out_shape = [shaped((steps, tok, width), BF16)]
    else:
        kernel = mine_kernel
        in_specs.append(slot)
        args.append(add)
        out_specs = [whole((tok, width))] * steps
        out_shape = [shaped((tok, width), BF16)] * steps
    return launch(
        kernel, "blocks", (steps,), args, in_specs, out_specs, out_shape, places=[where], vmem=MEDIUM, **links
    )


def error_kernel(hid_ref, dy_ref, l_ref, r_ref, *refs):
    errs, out_ref = refs[:-1], refs[-1]
    width = errs[0].shape[2]
    for part, err_ref in enumerate(errs):
        at = slice(part * width, (part + 1) * width)
        grown = dot(hid_ref[...], dy_ref[:, at]) + err_ref[0].astype(F32)
        out_ref[0, :, at] = (grown - dot(l_ref[...], r_ref[:, at])).astype(BF16)


def error_call(hid, dy, err, l, r, **links):
    units, tok = hid.shape
    depth = dy.shape[1]
    tile = 352 if units > 512 else units
    return launch(
        error_kernel,
        "error",
        (pl.cdiv(units, tile),),
        [hid, dy, l, r] + [err] * STREAMS,
        [
            pl.BlockSpec((tile, tok), lambda f: (f, 0)),
            whole(dy.shape),
            pl.BlockSpec((tile, SPLIT), lambda f: (f, 0)),
            whole(r.shape),
            *error_streams(tile, depth),
        ],
        [pl.BlockSpec((1, tile, depth), lambda f: (0, f, 0))],
        [shaped(err.shape, BF16)],
        vmem=LARGE,
        **links,
    )


def updated(w, mom, approx):
    return (w.astype(F32) - 0.1 * (0.9 * mom.astype(F32) + approx)).astype(BF16)


def update_kernel(own, at_ref, mom_ref, l_ref, r_ref, w_ref, *refs):
    pieces, (mom_out, w_out) = refs[:-2], refs[-2:]
    step = pl.program_id(0)

    @pl.when(step < own)
    def _():
        approx = dot(l_ref[...], r_ref[...])
        mom = mom_ref[...]
        mom_out[...] = 0.9 * mom + approx
        w_out[...] = updated(w_ref[...], mom.astype(BF16), approx)

    for slot, piece in enumerate(pieces):

        @pl.when(step == own + slot)
        def _(piece=piece):
            w_out[...] = updated(w_ref[...], piece[...], dot(l_ref[...], r_ref[...]))


def update_call(at, mom, pieces, w, l, r, **links):
    units, cols = mom.shape
    half = pieces[0].shape[1]
    own = cols // half
    tile = units // 2 if units % 32 == 0 and units > 512 else units
    tiles = units // tile

    def during(low, high, column):
        def index(c, f, at):
            row = jnp.where(c < low, 0, jnp.where(c > high, tiles - 1, f))
            return row, column(jnp.clip(c, low, high))

        return pl.BlockSpec((tile, half), index)

    momenta = during(0, own - 1, lambda c: c)
    weights = pl.BlockSpec((tile, half), lambda c, f, at: (f, at[c]))
    return launch(
        functools.partial(update_kernel, own),
        "update",
        (own + len(pieces), tiles),
        [mom, l, r, w, *pieces],
        [
            momenta,
            pl.BlockSpec((tile, SPLIT), lambda c, f, at: (f, 0)),
            pl.BlockSpec((SPLIT, half), lambda c, f, at: (0, at[c])),
            weights,
            *[during(own + s, own + s, lambda c: 0) for s in range(len(pieces))],
        ],
        [momenta, weights],
        [shaped(mom.shape, F32), shaped(w.shape, BF16)],
        places=[at],
        vmem=LARGE,
        **links,
    )


def last_kernel(at_ref, low_ref, high_ref, w_ref, l_ref, r_ref, _, w_out):
    half = low_ref.shape[1]
    approx = dot(l_ref[...], r_ref[...])
    w_out[:, :half] = updated(w_ref[:, :half], low_ref[...], approx[:, :half])
    w_out[:, half:] = updated(w_ref[:, half:], high_ref[...], approx[:, half:])


def last_call(at, low, high, w, l, r, new, **links):
    units, half = low.shape
    tile = 352 if units > 512 else units
    part = pl.BlockSpec((tile, half), lambda f, at: (f, 0))
    place = pl.BlockSpec((tile, 2 * half), lambda f, at: (f, at[0]))
    return launch(
        last_kernel,
        "last",
        (pl.cdiv(units, tile),),
        [low, high, w, l, r, new],
        [
            part,
            part,
            place,
            pl.BlockSpec((tile, SPLIT), lambda f, at: (f, 0)),
            pl.BlockSpec((SPLIT, 2 * half), lambda f, at: (0, at[0])),
            HELD,
        ],
        [place],
        [shaped(w.shape, BF16)],
        places=[at],
        aliases={6: 0},
        vmem=LARGE,
        **links,
    )


def exchange(value, axis, mask):
    size = lax.axis_size(axis)
    return lax.ppermute(value, axis, [(i, i ^ mask) for i in range(size)])


def arrived(one, two):
    return one[:16, :128] + two[:16, :128]


def masks(size):
    return [1 << bit for bit in range(size.bit_length() - 1)]


def body(inputs, out_grads, w_gate, w_up, w_down, err_down, mom_down, q_down):
    replicas = lax.axis_size("dp")
    shards = lax.axis_size("mp")
    rank_dp = lax.axis_index("dp")
    rank_mp = lax.axis_index("mp")
    w_gate, w_up, q_t = w_gate.T, w_up.T, q_down.T
    count = shards // 2
    split = max(1, count // 2)
    turns = [(split, count - split), (0, split)] if count > split else [(0, split)]

    low, high, later_low, later_high = cast_call(mom_down)
    got = {(2, 0): exchange(low, "dp", 2), (1, 1): exchange(high, "dp", 1)}

    hid, d_gate, d_up, left, dyq = hidden_call(
        inputs, out_grads, w_gate, w_up, w_down, err_down, q_t, replicas, held=[low]
    )
    lefts = [left] + [exchange(left, "dp", mask) for mask in range(1, replicas)]

    here, there = rank_mp % 2, 1 - rank_mp % 2
    others, mine = [], [None] * count

    def blocks(turn, order, held=(), through=()):
        side, part = divmod(turn, len(turns))
        parity, slots = (there, here)[side], turns[part]
        add = others[part] if side else None
        size = slots[1] if side else 1
        outs = blocks_call(
            rank_mp,
            parity,
            slots,
            count,
            d_gate,
            d_up,
            w_gate,
            w_up,
            add,
            held=held,
            through=[order, *through],
        )
        if side:
            mine[slots[0] : slots[0] + size] = outs[:size]
        else:
            others.append(outs[0])
        return outs[size:]

    total, left, order, later_low, later_high = right_call(
        lefts,
        hid,
        err_down,
        out_grads,
        held=[arrived(got[2, 0], got[1, 1])],
        through=[dyq, later_low, later_high],
    )
    got[1, 0] = exchange(later_low, "dp", 1)
    got[2, 1] = exchange(later_high, "dp", 2)

    rounds = [("mp", mask) for mask in masks(shards)] + [("dp", mask) for mask in masks(replicas)]
    for index, (axis, mask) in enumerate(rounds):
        more = exchange(total, axis, mask)
        if index < 2 * len(turns):
            (order,) = blocks(index, order, [total])
        relay = index == 2 and count == 4
        through = others[index:] if index < len(turns) else [mine[3]] if relay else []
        held = [arrived(got[1, 0], got[2, 1])] if index == 3 else []
        total, order, *fresh = sum_call(total, more, held=held, through=[order, *through])
        if relay:
            relayed = exchange(fresh[0], "mp", 2)
        elif fresh:
            others[index] = exchange(fresh[0], "mp", 1)
    if count == 4:
        relayed, order = join_call([mine[2], relayed], held=[total], through=[order])
    l, r, got[2, 0], got[1, 1] = factors_call(
        total, left, replicas, held=[order], through=[got[2, 0], got[1, 1]]
    )
    got[3, 0] = exchange(got[2, 0], "dp", 1)
    got[3, 1] = exchange(got[1, 1], "dp", 2)
    if count == 4:
        landed = [exchange(relayed, "mp", 4), exchange(mine[1], "mp", 2)]
    else:
        landed = [exchange(mine[slot], "mp", 2 * slot) for slot in range(1, count)]

    (next_err,) = error_call(hid, out_grads, err_down, l, r)
    keys = [(1, 0), (1, 1), (2, 0), (2, 1)]
    at = jnp.stack([2 * (rank_dp ^ mask) + side for mask, side in [(0, 0), (0, 1)] + keys])
    next_mom, new, order = update_call(
        at.astype(jnp.int32),
        mom_down,
        [got[key] for key in keys],
        w_down,
        l,
        r,
        held=[next_err],
        through=[order],
    )
    far = jnp.reshape(rank_dp ^ 3, (1,)).astype(jnp.int32)
    new, order = last_call(far, got[3, 0], got[3, 1], w_down, l, r, new, through=[order])
    (in_grads,) = join_call([mine[0]] + landed, held=[order])
    return (in_grads, new, next_err, next_mom)


def solution(mesh):
    in_specs = (
        P("dp", None),
        P("dp", None),
        P(None, "mp"),
        P(None, "mp"),
        P("mp", None),
        P("dp", "mp", None),
        P("mp", "dp"),
        P(),
    )
    out_specs = (P("dp", "mp"), P("mp", None), P("dp", "mp", None), P("mp", "dp"))
    return jax.shard_map(body, mesh=mesh, in_specs=in_specs, out_specs=out_specs, check_vma=False)
```

```python
import functools

import jax
import jax.numpy as jnp
from jax import lax
from jax.experimental import pallas as pl
from jax.experimental.pallas import tpu as pltpu
from jax.sharding import PartitionSpec as P

R = 8
SPLIT = 4 * R
EPS = 1e-06
F32 = jnp.float32
BF16 = jnp.bfloat16
HIGH = lax.Precision.HIGHEST
VMEM = 48 * 2**20
SMALL = 12 * 2**20
LARGE = 62 * 2**20
ONCE = pl.Buffered(1)
STREAMS = 4
MEDIUM = 48 * 2**20
HELD = pl.BlockSpec(memory_space=pl.ANY)


def launch(kernel, name, grid, args, in_specs, out_specs, out_shape, *, places=(), held=(),
           through=(), scratch=(), vmem=VMEM, aliases=None):
    n_in, n_out = len(args), len(out_shape)
    n_held, n_through, n_place = len(held), len(through), len(places)
    first = n_place + n_in

    def inner(*refs):
        outs = first + n_held + n_through
        kernel(*refs[:first], *refs[outs : outs + n_out], *refs[outs + n_out + n_through :])

    links = {first + n_held + i: n_out + i for i in range(n_through)}
    return pl.pallas_call(
        inner,
        grid_spec=pltpu.PrefetchScalarGridSpec(
            num_scalar_prefetch=n_place,
            grid=grid,
            in_specs=list(in_specs) + [HELD] * (n_held + n_through),
            out_specs=list(out_specs) + [HELD] * n_through,
            scratch_shapes=list(scratch),
        ),
        out_shape=list(out_shape)
        + [jax.ShapeDtypeStruct(array.shape, array.dtype) for array in through],
        input_output_aliases={**links, **(aliases or {})},
        compiler_params=pltpu.CompilerParams(vmem_limit_bytes=vmem),
        cost_estimate=pl.CostEstimate(flops=1, bytes_accessed=1, transcendentals=0),
        name=name,
    )(*places, *args, *held, *through)


def shaped(shape, dtype):
    return jax.ShapeDtypeStruct(shape, dtype)


def dot(left, right):
    return jnp.dot(left, right, preferred_element_type=F32)


def dot_nt(left, right):
    return lax.dot_general(left, right, (((1,), (1,)), ((), ())), preferred_element_type=F32)


def terms(rows):
    hi = rows.astype(BF16).astype(F32)
    rest = rows - hi
    mid = rest.astype(BF16).astype(F32)
    return hi, mid, rest - mid


def spread(rows):
    hi, mid, low = terms(rows)
    return jnp.concatenate([hi, mid, low, jnp.zeros_like(hi)], axis=0).astype(BF16)


def gather_terms(rows):
    return rows[:R] + rows[R : 2 * R] + rows[2 * R : 3 * R]


def tree(parts):
    while len(parts) > 1:
        odd = parts[len(parts) // 2 * 2 :]
        parts = [left + right for left, right in zip(parts[::2], parts[1::2])] + odd
    return parts[0]


def whole(shape):
    return pl.BlockSpec(shape, lambda *_: (0,) * len(shape), pipeline_mode=ONCE)


def unit_tile(units):
    return 256 if units > 512 and units % 16 == 0 else units


def cast_kernel(mom_ref, *outs):
    half = mom_ref.shape[1] // 2
    low, high = mom_ref[:, :half].astype(BF16), mom_ref[:, half:].astype(BF16)
    for out, part in zip(outs, (low, high, low, high)):
        out[...] = part


def cast_call(mom, **links):
    units, cols = mom.shape
    tile = units // 2 if units % 32 == 0 and units > 512 else units
    part = pl.BlockSpec((tile, cols // 2), lambda f: (f, 0))
    return launch(
        cast_kernel,
        "cast",
        (units // tile,),
        [mom],
        [pl.BlockSpec((tile, cols), lambda f: (f, 0))],
        [part] * 4,
        [shaped((units, cols // 2), BF16)] * 4,
        vmem=MEDIUM,
        **links,
    )


def hidden_kernel(
    replicas,
    x_ref, wg_ref, wu_ref, wd_ref, err_ref, q_ref, dy_any,
    hid_ref, dg_ref, du_ref, left_ref, dyq_ref,
    dy_ref, q_terms, dyq_terms, sem,
):
    fetch = pltpu.make_async_copy(dy_any, dy_ref, sem)

    @pl.when(pl.program_id(0) == 0)
    def _():
        fetch.start()
        q_terms[...] = spread(q_ref[...])

    gate = dot_nt(x_ref[...], wg_ref[...])
    up = dot_nt(x_ref[...], wu_ref[...])
    both = dot_nt(err_ref[0], q_terms[...])

    @pl.when(pl.program_id(0) == 0)
    def _():
        fetch.wait()
        dyq = gather_terms(dot_nt(dy_ref[...], q_terms[...]).T)
        dyq_ref[...] = dyq
        dyq_terms[...] = spread(dyq)

    dh = dot_nt(dy_ref[...], wd_ref[...])
    sig = jax.nn.sigmoid(gate)
    silu = gate * sig
    hid = (silu * up).T.astype(BF16)
    hid_ref[...] = hid
    dg_ref[...] = (dh * up * sig * (1.0 + gate * (1.0 - sig))).astype(BF16)
    du_ref[...] = (dh * silu).astype(BF16)
    both += dot_nt(hid, dyq_terms[...])
    left_ref[...] = gather_terms(both.T) / replicas


def hidden_call(x, dy, wg, wu, wd, err, q_t, replicas, **links):
    tok, depth = x.shape
    units = wg.shape[0]
    tile = unit_tile(units)
    rows = pl.BlockSpec((tile, depth), lambda f: (f, 0))
    part = pl.BlockSpec((tok, tile), lambda f: (0, f))
    return launch(
        functools.partial(hidden_kernel, replicas),
        "hidden",
        (pl.cdiv(units, tile),),
        [x, wg, wu, wd, err, q_t, dy],
        [
            whole((tok, depth)),
            rows,
            rows,
            rows,
            pl.BlockSpec((1, tile, depth), lambda f: (0, f, 0)),
            whole(q_t.shape),
            HELD,
        ],
        [
            pl.BlockSpec((tile, tok), lambda f: (f, 0)),
            part,
            part,
            pl.BlockSpec((R, tile), lambda f: (0, f)),
            whole((R, tok)),
        ],
        [
            shaped((units, tok), BF16),
            shaped((tok, units), BF16),
            shaped((tok, units), BF16),
            shaped((R, units), F32),
            shaped((R, tok), F32),
        ],
        scratch=[
            pltpu.VMEM((tok, depth), BF16),
            pltpu.VMEM((SPLIT, depth), BF16),
            pltpu.VMEM((SPLIT, tok), BF16),
            pltpu.SemaphoreType.DMA(()),
        ],
        **links,
    )


def error_streams(tile, depth):
    shape = (1, tile, depth // STREAMS)
    return [pl.BlockSpec(shape, lambda f, c=c: (0, f, c)) for c in range(STREAMS)]


def columns(ref, step, tile):
    if ref.shape[1] == tile:
        return ref[...]
    return ref[:, pl.ds(pl.multiple_of(step * tile, tile), tile)]


def right_kernel(parts, dy_steps, *refs):
    lefts = refs[:parts]
    errs, (hid_ref, dy_ref, out_ref, left_ref, left_terms, mixed_terms, total) = (
        refs[parts:-7],
        refs[-7:],
    )
    step = pl.program_id(0)
    units = left_ref.shape[1]
    tile, width = errs[0].shape[1:]
    depth = width * len(errs)
    dy_tile = dy_ref.shape[0]
    tail = units % tile
    last = pl.num_programs(0) - 1

    @pl.when(step == 0)
    def _():
        left = tree([ref[...] for ref in lefts])
        left_ref[...] = left
        left_terms[:, :units] = spread(left)
        mixed_terms[...] = spread(gather_terms(dot(left_terms[:, :units], hid_ref[...])))
        gram = lax.dot_general(
            left, left, (((1,), (1,)), ((), ())), precision=HIGH, preferred_element_type=F32
        )
        out_ref[:, depth:] = jnp.concatenate([gram, jnp.zeros((R, 128 - R), F32)], axis=1)
        total[...] = jnp.zeros_like(total)

    @pl.when(step < dy_steps)
    def _():
        total[...] += dot(columns(mixed_terms, step, dy_tile), dy_ref[...])

    if tail:

        @pl.when(step < last)
        def _():
            left = columns(left_terms, step, tile)
            for at, err_ref in enumerate(errs):
                total[:, at * width : (at + 1) * width] += dot(left, err_ref[0])

        @pl.when(step == last)
        def _():
            left = left_terms[:, units - tail : units]
            for at, err_ref in enumerate(errs):
                total[:, at * width : (at + 1) * width] += dot(left, err_ref[0, :tail])

    else:
        left = columns(left_terms, step, tile)
        for at, err_ref in enumerate(errs):
            total[:, at * width : (at + 1) * width] += dot(left, err_ref[0])

    @pl.when(step == last)
    def _():
        out_ref[:, :depth] = gather_terms(total[...])


def right_call(lefts, hid, err, dy, **links):
    units, tok = hid.shape
    depth = dy.shape[1]
    tile = unit_tile(units)
    tiles = pl.cdiv(units, tile)
    dy_steps = 2 if tiles > 1 else 1
    return launch(
        functools.partial(right_kernel, len(lefts), dy_steps),
        "right",
        (tiles,),
        [*lefts] + [err] * STREAMS + [hid, dy],
        [whole((R, units))] * len(lefts)
        + error_streams(tile, depth)
        + [
            whole((units, tok)),
            pl.BlockSpec((tok // dy_steps, depth), lambda f: (jnp.minimum(f, dy_steps - 1), 0)),
        ],
        [whole((R, depth + 128)), whole((R, units))],
        [shaped((R, depth + 128), F32), shaped((R, units), F32)],
        scratch=[
            pltpu.VMEM((SPLIT, tiles * tile), BF16),
            pltpu.VMEM((SPLIT, tok), BF16),
            pltpu.VMEM((SPLIT, depth), F32),
        ],
        vmem=MEDIUM,
        **links,
    )


def sum_kernel(one_ref, two_ref, out_ref):
    out_ref[...] = one_ref[...] + two_ref[...]


def sum_call(one, two, **links):
    return launch(
        sum_kernel,
        "sum",
        (1,),
        [one, two],
        [whole(one.shape)] * 2,
        [whole(one.shape)],
        [shaped(one.shape, one.dtype)],
        vmem=SMALL,
        **links,
    )


def join_kernel(*refs):
    refs[-1][...] = tree([ref[...].astype(F32) for ref in refs[:-1]]).astype(BF16)


def join_call(parts, **links):
    shape = parts[0].shape
    return launch(
        join_kernel,
        "join",
        (1,),
        parts,
        [whole(shape)] * len(parts),
        [whole(shape)],
        [shaped(shape, BF16)],
        vmem=SMALL,
        **links,
    )


def factors_kernel(replicas, sum_ref, left_ref, l_ref, r_ref):
    depth = r_ref.shape[1]
    gram = sum_ref[:, depth : depth + R] / replicas
    row = lax.broadcasted_iota(jnp.int32, (R, R), 0)
    col = lax.broadcasted_iota(jnp.int32, (R, R), 1)
    eye = (row == col).astype(F32)
    basis = jnp.zeros((R, R), F32)
    for k in range(R):
        unit = eye[k : k + 1]
        coeffs = jnp.sum(basis * gram[k : k + 1], axis=1, keepdims=True)
        rest = unit - jnp.sum(coeffs * basis, axis=0, keepdims=True)
        rest_col = jnp.sum(eye * rest, axis=1, keepdims=True)
        image = jnp.sum(rest_col * gram, axis=0, keepdims=True)
        square = jnp.sum(image * rest, axis=1, keepdims=True)
        basis = jnp.where(row == k, rest * lax.rsqrt(jnp.maximum(square, 0.0) + EPS), basis)
    left = jnp.dot(basis, left_ref[...], precision=HIGH, preferred_element_type=F32)
    right = jnp.dot(basis, sum_ref[:, :depth], precision=HIGH, preferred_element_type=F32)
    hi, mid, _ = terms(left)
    zero = jnp.zeros_like(hi)
    l_ref[...] = jnp.concatenate([hi, hi, mid, zero], axis=0).T.astype(BF16)
    hi, mid, _ = terms(right / replicas)
    zero = jnp.zeros_like(hi)
    r_ref[...] = jnp.concatenate([hi, mid, hi, zero], axis=0).astype(BF16)


def factors_call(total, left, replicas, **links):
    units = left.shape[1]
    depth = total.shape[1] - 128
    return launch(
        functools.partial(factors_kernel, replicas),
        "factors",
        (1,),
        [total, left],
        [whole(total.shape), whole(left.shape)],
        [whole((units, SPLIT)), whole((SPLIT, depth))],
        [shaped((units, SPLIT), BF16), shaped((SPLIT, depth), BF16)],
        vmem=LARGE,
        **links,
    )


def other_kernel(where_ref, dg_ref, du_ref, wg_ref, wu_ref, out_ref):
    out_ref[0] = (dot(dg_ref[...], wg_ref[...]) + dot(du_ref[...], wu_ref[...])).astype(BF16)


def mine_kernel(where_ref, dg_ref, du_ref, wg_ref, wu_ref, add_ref, *outs):
    part = dot(dg_ref[...], wg_ref[...]) + dot(du_ref[...], wu_ref[...])
    part = (part + add_ref[0].astype(F32)).astype(BF16)
    for slot, out in enumerate(outs):

        @pl.when(pl.program_id(0) == slot)
        def _(out=out):
            out[...] = part


def blocks_call(pos, parity, slots, count, dg, du, wg, wu, add=None, **links):
    tok, units = dg.shape
    depth = wg.shape[1]
    width = depth // (2 * count)
    where = jnp.stack([pos // 2, parity]).astype(jnp.int32)
    first, steps = slots
    block = pl.BlockSpec((units, width), lambda s, at: (0, 2 * ((s + first) ^ at[0]) + at[1]))
    slot = pl.BlockSpec((1, tok, width), lambda s, at: (s, 0, 0))
    in_specs = [whole((tok, units)), whole((tok, units)), block, block]
    args = [dg, du, wg, wu]
    if add is None:
        kernel = other_kernel
        out_specs = [slot]
        out_shape = [shaped((steps, tok, width), BF16)]
    else:
        kernel = mine_kernel
        in_specs.append(slot)
        args.append(add)
        out_specs = [whole((tok, width))] * steps
        out_shape = [shaped((tok, width), BF16)] * steps
    return launch(
        kernel, "blocks", (steps,), args, in_specs, out_specs, out_shape, places=[where], vmem=MEDIUM, **links
    )


def updated(w, mom, approx):
    return (w.astype(F32) - 0.1 * (0.9 * mom.astype(F32) + approx)).astype(BF16)


def final_kernel(early, own, at_ref, hid_ref, dy_ref, err_ref, l_ref, r_ref, w_ref, mom_ref, *refs):
    pieces, (err_out, w_out, mom_out) = refs[:-3], refs[-3:]
    step = pl.program_id(0)
    approx = dot(l_ref[...], r_ref[...])
    grown = dot(hid_ref[...], dy_ref[...]) + err_ref[0].astype(F32)
    err_out[0] = (grown - approx).astype(BF16)

    @pl.when((step >= early) & (step < early + own))
    def _():
        mom = mom_ref[...]
        mom_out[...] = 0.9 * mom + approx
        w_out[...] = updated(w_ref[...], mom.astype(BF16), approx)

    for slot, piece in enumerate(pieces):

        @pl.when(step == early + own + slot)
        def _(piece=piece):
            w_out[...] = updated(w_ref[...], piece[...], approx)


def final_call(at, early, hid, dy, err, l, r, w, mom, pieces, **links):
    units, tok = hid.shape
    cols = mom.shape[1]
    half = pieces[0].shape[1]
    own = cols // half
    tile = units // 2 if units % 32 == 0 and units > 512 else units
    tiles = units // tile
    count = dy.shape[1] // half

    def place(c, at):
        return 2 * (at[0] ^ ((c // own + 3) % 4)) + c % own

    def held_to(low, high, column):
        def index(c, f, at):
            row = jnp.where(c < low, 0, jnp.where(c > high, tiles - 1, f))
            return row, column(jnp.clip(c, low, high), at)

        return pl.BlockSpec((tile, half), index)

    weights = held_to(early, count - 1, place)
    momenta = held_to(early, early + own - 1, lambda c, at: c - early)
    arrived = [held_to(early + own + s, early + own + s, lambda c, at: 0) for s in range(len(pieces))]
    error = pl.BlockSpec((1, tile, half), lambda c, f, at: (0, f, place(c, at)))
    return launch(
        functools.partial(final_kernel, early, own),
        "final",
        (count, tiles),
        [hid, dy, err, l, r, w, mom, *pieces],
        [
            pl.BlockSpec((tile, tok), lambda c, f, at: (f, 0)),
            pl.BlockSpec((tok, half), lambda c, f, at: (0, place(c, at))),
            error,
            pl.BlockSpec((tile, SPLIT), lambda c, f, at: (f, 0)),
            pl.BlockSpec((SPLIT, half), lambda c, f, at: (0, place(c, at))),
            weights,
            momenta,
            *arrived,
        ],
        [error, weights, momenta],
        [shaped(err.shape, BF16), shaped(w.shape, BF16), shaped(mom.shape, F32)],
        places=[at],
        vmem=LARGE,
        **links,
    )


def last_kernel(at_ref, low_ref, high_ref, w_ref, l_ref, r_ref, _, w_out):
    half = low_ref.shape[1]
    approx = dot(l_ref[...], r_ref[...])
    w_out[:, :half] = updated(w_ref[:, :half], low_ref[...], approx[:, :half])
    w_out[:, half:] = updated(w_ref[:, half:], high_ref[...], approx[:, half:])


def last_call(at, low, high, w, l, r, new, **links):
    units, half = low.shape
    tile = 352 if units > 512 else units
    part = pl.BlockSpec((tile, half), lambda f, at: (f, 0))
    place = pl.BlockSpec((tile, 2 * half), lambda f, at: (f, at[0]))
    return launch(
        last_kernel,
        "last",
        (pl.cdiv(units, tile),),
        [low, high, w, l, r, new],
        [
            part,
            part,
            place,
            pl.BlockSpec((tile, SPLIT), lambda f, at: (f, 0)),
            pl.BlockSpec((SPLIT, 2 * half), lambda f, at: (0, at[0])),
            HELD,
        ],
        [place],
        [shaped(w.shape, BF16)],
        places=[at],
        aliases={6: 0},
        vmem=LARGE,
        **links,
    )


def exchange(value, axis, mask):
    size = lax.axis_size(axis)
    return lax.ppermute(value, axis, [(i, i ^ mask) for i in range(size)])


def arrived(one, two):
    return one[:16, :128] + two[:16, :128]


def masks(size):
    return [1 << bit for bit in range(size.bit_length() - 1)]


def body(inputs, out_grads, w_gate, w_up, w_down, err_down, mom_down, q_down):
    replicas = lax.axis_size("dp")
    shards = lax.axis_size("mp")
    rank_dp = lax.axis_index("dp")
    rank_mp = lax.axis_index("mp")
    w_gate, w_up, q_t = w_gate.T, w_up.T, q_down.T
    count = shards // 2
    split = max(1, count // 2)
    turns = [(split, count - split), (0, split)] if count > split else [(0, split)]

    low, high, later_low, later_high = cast_call(mom_down)
    got = {(2, 0): exchange(low, "dp", 2), (1, 1): exchange(high, "dp", 1)}

    hid, d_gate, d_up, left, dyq = hidden_call(
        inputs, out_grads, w_gate, w_up, w_down, err_down, q_t, replicas, held=[low]
    )
    lefts = [left] + [exchange(left, "dp", mask) for mask in range(1, replicas)]

    here, there = rank_mp % 2, 1 - rank_mp % 2
    others, mine = [], [None] * count

    def blocks(turn, order, held=(), through=()):
        side, part = divmod(turn, len(turns))
        parity, slots = (there, here)[side], turns[part]
        add = others[part] if side else None
        size = slots[1] if side else 1
        outs = blocks_call(
            rank_mp,
            parity,
            slots,
            count,
            d_gate,
            d_up,
            w_gate,
            w_up,
            add,
            held=held,
            through=[order, *through],
        )
        if side:
            mine[slots[0] : slots[0] + size] = outs[:size]
        else:
            others.append(outs[0])
        return outs[size:]

    total, left, order, later_low, later_high = right_call(
        lefts,
        hid,
        err_down,
        out_grads,
        held=[arrived(got[2, 0], got[1, 1])],
        through=[dyq, later_low, later_high],
    )
    got[1, 0] = exchange(later_low, "dp", 1)
    got[2, 1] = exchange(later_high, "dp", 2)

    rounds = [("mp", mask) for mask in masks(shards)] + [("dp", mask) for mask in masks(replicas)]
    for index, (axis, mask) in enumerate(rounds):
        more = exchange(total, axis, mask)
        if index < 2 * len(turns):
            (order,) = blocks(index, order, [total])
        relay = index == 2 and count == 4
        through = others[index:] if index < len(turns) else [mine[3]] if relay else []
        held = [arrived(got[1, 0], got[2, 1])] if index == 3 else []
        total, order, *fresh = sum_call(total, more, held=held, through=[order, *through])
        if relay:
            relayed = exchange(fresh[0], "mp", 2)
        elif fresh:
            others[index] = exchange(fresh[0], "mp", 1)
    if count == 4:
        relayed, order = join_call([mine[2], relayed], held=[total], through=[order])
    l, r, got[2, 0], got[1, 1] = factors_call(
        total, left, replicas, held=[order], through=[got[2, 0], got[1, 1]]
    )
    got[3, 0] = exchange(got[2, 0], "dp", 1)
    got[3, 1] = exchange(got[1, 1], "dp", 2)
    if count == 4:
        landed = [exchange(relayed, "mp", 4), exchange(mine[1], "mp", 2)]
    else:
        landed = [exchange(mine[slot], "mp", 2 * slot) for slot in range(1, count)]

    next_err, new, next_mom, order = final_call(
        jnp.reshape(rank_dp, (1,)).astype(jnp.int32),
        2,
        hid,
        out_grads,
        err_down,
        l,
        r,
        w_down,
        mom_down,
        [got[key] for key in [(1, 0), (1, 1), (2, 0), (2, 1)]],
        through=[order],
    )
    far = jnp.reshape(rank_dp ^ 3, (1,)).astype(jnp.int32)
    new, order = last_call(far, got[3, 0], got[3, 1], w_down, l, r, new, through=[order])
    (in_grads,) = join_call([mine[0]] + landed, held=[order])
    return (in_grads, new, next_err, next_mom)


def solution(mesh):
    in_specs = (
        P("dp", None),
        P("dp", None),
        P(None, "mp"),
        P(None, "mp"),
        P("mp", None),
        P("dp", "mp", None),
        P("mp", "dp"),
        P(),
    )
    out_specs = (P("dp", "mp"), P("mp", None), P("dp", "mp", None), P("mp", "dp"))
    return jax.shard_map(body, mesh=mesh, in_specs=in_specs, out_specs=out_specs, check_vma=False)
```
